32 devices in a mesh: section: 2 (over x), dp: 16 (over z, y, core).
Axes of the slice: x: 2, y: 2, z: 4, core: 2. Of those that a mesh axis runs over, the one named last changes fastest.
Arguments:
- cells_in: bfloat16 [32, 1024, 256], P('dp'), may hold values from -6 to 6
- out_grad: bfloat16 [32, 1024, 256], P('dp'), may hold values from -6 to 6
- segment_ids: int32 [32, 1024], P('dp'), may hold values from 0 to 11, never falling along the last dimension, each value on 1 to 512 neighbouring positions
- real_lengths: int32 [32], P('dp'), may hold values from 512 to 1024, as said below
- w_qkv: bfloat16 [2, 256, 768], P('section'), may hold values from -0.375 to 0.375
- w_attn_out: bfloat16 [2, 256, 256], P('section'), may hold values from -2 to 2
- w_up: bfloat16 [2, 256, 512], P('section'), may hold values from -0.375 to 0.375
- w_down: bfloat16 [2, 512, 256], P('section'), may hold values from -0.25 to 0.25
- norm_gains: float32 [2, 2, 256], P('section'), may hold values from 0.5 to 1.5
- biases: float32 [2, 6, 256], P('section'), may hold values from -3 to 3
- up_bias: float32 [2, 512], P('section'), may hold values from -3 to 3
Outputs:
- layer_out: bfloat16 [2, 32, 1024, 256], P('section', 'dp')
- input_grad: float32 [2, 32, 1024, 256], P('section', 'dp')
- grad_qkv: float32 [2, 256, 768], P('section')
- grad_attn_out: float32 [2, 256, 256], P('section')
- grad_up: float32 [2, 256, 512], P('section')
- grad_down: float32 [2, 512, 256], P('section')
- grad_gains: float32 [2, 2, 256], P('section')
- grad_biases: float32 [2, 6, 256], P('section')
- grad_up_bias: float32 [2, 512], P('section')
The draws below stay inside these ranges and needn't reach their ends.
Inputs may be any that keep to these rules, and one draw needn't show every extreme that they name: segment_ids never fall along a row; the tokens of one cell share one number. The first real_lengths[r] tokens of row r are real, the rest padding.
All inputs are finite; a program needn't handle non-finite values.
Results may differ from the reference program's by a relative error of at most 0.013.
Values may be sent and summed in bfloat16 or wider, within the bound.
A program may use at most 192 MiB of HBM per device.

```python
import math
import jax
import jax.numpy as jnp
import numpy as np
from jax import lax

D = 256
HEADS = 4
FF = 512
SEQ = 1024
LAYERS = 2
ROWS = 32


def draw_real_lengths(key, part):
    key = jax.random.fold_in(key, 7)
    first_key, second_key, third_key = jax.random.split(key, 3)
    lengths = SEQ - jax.random.randint(first_key, (ROWS,), 0, SEQ // 2 + 1)
    longest_row = jax.random.randint(second_key, (), 0, ROWS)
    shortest_row = (longest_row + 1 + jax.random.randint(third_key, (), 0, ROWS - 1)) % ROWS
    row_numbers = jnp.arange(ROWS, dtype=jnp.int32)
    lengths = jnp.where(row_numbers == longest_row, SEQ, lengths)
    lengths = jnp.where(row_numbers == shortest_row, SEQ - SEQ // 2, lengths)
    return lengths.astype(jnp.int32)


def levels(stream_key, dims, cuts, least, largest):
    def one(position, shards_of):
        draws = jax.random.uniform(jax.random.fold_in(jax.random.fold_in(stream_key, 6), position), (shards_of,), jnp.float32, least / len(cuts), largest / len(cuts))
        return jnp.repeat(jnp.exp(draws), dims[position] // shards_of).reshape((-1,) + (1,) * (len(dims) - position - 1))

    loudness = one(*cuts[0])
    for cut in cuts[1:]:
        loudness = loudness * one(*cut)
    return loudness


def length_profile(count, total, reach, slope):
    portions = [(1 << 20) // math.isqrt(standing ** slope) + 1 for standing in range(2, count + 1)]
    spare, given = total - reach - (count - 1), [1] * (count - 1)
    while spare > 0:
        candidates = [i for i in range(count - 1) if given[i] < reach]
        whole, left = sum([portions[i] for i in candidates]), spare
        for i in candidates:
            more = min(reach - given[i], max(1, left * portions[i] // whole), spare)
            given[i] = given[i] + more
            spare = spare - more
    return np.array([reach] + given)


def ragged(stream_key, amount, total, reach, skew):
    if amount == 2:
        one = jax.random.randint(stream_key, (), max(1, total - reach), min(reach, total - 1) + 1)
        return jnp.stack([one, total - one])
    sizes = jnp.asarray(length_profile(amount, total, reach, skew), jnp.int32)
    pairs = (amount - 1) // 2
    giver, receiver = sizes[1:1 + 2 * pairs:2], sizes[2:2 + 2 * pairs:2]
    room = jnp.minimum(giver - 1, reach - receiver)
    shifted = jax.random.randint(jax.random.fold_in(stream_key, 1), (pairs,), 0, 1 << 20) % (room + 1)
    sizes = sizes.at[1:1 + 2 * pairs:2].set(giver - shifted).at[2:2 + 2 * pairs:2].set(receiver + shifted)
    return sizes[jax.random.permutation(jax.random.fold_in(stream_key, 2), amount)]


def bell_draw(key, dims, scale, most, shards=(), kind=jnp.bfloat16):
    values = scale * jax.random.normal(key, dims, jnp.float32)
    if shards:
        values = values * levels(key, dims, shards, -0.22, 0.18)
    return jnp.clip(values, -most, most).astype(kind)


def setup_inputs(seed: int = 0) -> dict:
    keys = jax.random.split(jax.random.key(seed), 12)
    return {
        "cells_in": bell_draw(keys[0], (ROWS, SEQ, D), 1.0, 6.0, ((0, 16),)),
        "out_grad": bell_draw(keys[1], (ROWS, SEQ, D), 1.0, 6.0, ((0, 16),)),
        "segment_ids": jax.vmap(lambda own: jnp.searchsorted(jnp.cumsum(ragged(own, SEQ // 128 + 4, SEQ, SEQ // 2, 2)), jnp.arange(SEQ), side="right"))(jax.random.split(keys[2], ROWS)).reshape((ROWS, SEQ)).astype(jnp.int32),
        "real_lengths": draw_real_lengths(jax.random.fold_in(keys[11], 71), 0),
        "w_qkv": bell_draw(keys[4], (LAYERS, D, 3 * D), D ** -0.5, 0.375, ((0, 2),)),
        "w_attn_out": bell_draw(keys[5], (LAYERS, D, D), (D // 32) ** -0.5, 2.0, ((0, 2),)),
        "w_up": bell_draw(keys[6], (LAYERS, D, FF), D ** -0.5, 0.375, ((0, 2),)),
        "w_down": bell_draw(keys[7], (LAYERS, FF, D), FF ** -0.5, 0.25, ((0, 2),)),
        "norm_gains": jnp.clip(1.0 + 0.1 * jax.random.normal(keys[8], (LAYERS, 2, D), jnp.float32), 0.5, 1.5),
        "biases": bell_draw(keys[9], (LAYERS, 6, D), 0.5, 3.0, ((0, 2),), jnp.float32),
        "up_bias": bell_draw(keys[10], (LAYERS, FF), 0.5, 3.0, ((0, 2),), jnp.float32),
    }


HIGHEST_MODE = lax.Precision.HIGHEST

@jax.custom_vjp
def low(v):
    return lax.optimization_barrier(v.astype(jnp.bfloat16)).astype(jnp.float32)

@jax.custom_vjp
def low_back(v):
    return v

def low_keep(v):
    return (low(v), None)

def low_pass(kept, grad):
    return (grad,)

def back_keep(v):
    return (v, None)

def back_low(kept, grad):
    return (low(grad),)
low.defvjp(low_keep, low_pass)
low_back.defvjp(back_keep, back_low)

def layer_norm(residual, gain, shift):
    centred = residual - lax.optimization_barrier(jnp.mean(residual, axis=-1, keepdims=True))
    spread = lax.optimization_barrier(jnp.mean(centred * centred, axis=-1, keepdims=True))
    return centred * lax.rsqrt(spread + 1e-05) * gain + shift

def allowed_pairs(seg_query, positions, seg_rows, len_rows):
    key_positions = jnp.arange(seg_rows.shape[-1], dtype=jnp.int32)
    same_cell = seg_query[:, :, None] == seg_rows[:, None, :]
    real_query = positions[None, :, None] < len_rows[:, None, None]
    real_key = key_positions[None, None, :] < len_rows[:, None, None]
    itself = positions[:, None] == key_positions[None, :]
    return same_cell & real_query & real_key | itself[None]

def one_layer(layer_in, params, seg_rows, len_rows):
    w_packed, w_output, w_upper, w_lower, gains, shifts, up_shift = params
    row_count, seq_len, width = layer_in.shape
    head_dim = width // HEADS
    score_scale = 1.0 / math.sqrt(head_dim)
    flat_in = layer_in.reshape(row_count * seq_len, width)
    packed_shift = jnp.concatenate([shifts[0], jnp.zeros_like(shifts[0]), shifts[1]])
    packed = jnp.dot(flat_in, w_packed, precision=HIGHEST_MODE) + packed_shift
    packed = low_back(low(packed)).reshape(row_count, seq_len, 3, HEADS, head_dim)
    queries = packed[:, :, 0]
    keys_all = packed[:, :, 1]
    values_all = packed[:, :, 2]
    query_block = min(512, seq_len)
    block_count = seq_len // query_block
    query_blocks = queries.reshape(row_count, block_count, query_block, HEADS, head_dim).transpose(1, 0, 2, 3, 4)
    seg_blocks = seg_rows.reshape(row_count, block_count, query_block).transpose(1, 0, 2)
    block_starts = jnp.arange(block_count, dtype=jnp.int32) * query_block

    def attend_block(block_args):
        query_part, seg_part, block_start = block_args
        scores = jnp.einsum('rqhd,rkhd->rhqk', query_part, keys_all, precision=HIGHEST_MODE)
        scores = low_back(scores * score_scale)
        positions = block_start + jnp.arange(query_block, dtype=jnp.int32)
        usable = allowed_pairs(seg_part, positions, seg_rows, len_rows)[:, None]
        weights = low(jax.nn.softmax(jnp.where(usable, scores, -1e+30), axis=-1))
        return jnp.einsum('rhqk,rkhd->rqhd', weights, values_all, precision=HIGHEST_MODE)
    context = lax.map(jax.checkpoint(attend_block), (query_blocks, seg_blocks, block_starts))
    context = context.transpose(1, 0, 2, 3, 4).reshape(row_count * seq_len, width)
    context = low_back(low(context))
    attended = low_back(jnp.dot(context, w_output, precision=HIGHEST_MODE) + shifts[2])
    hidden = layer_norm(flat_in + attended, gains[0], shifts[3])
    upper = low_back(jnp.dot(low(hidden), w_upper, precision=HIGHEST_MODE) + up_shift)
    active = low(jax.nn.gelu(upper))
    lowered = low_back(jnp.dot(active, w_lower, precision=HIGHEST_MODE) + shifts[4])
    result = layer_norm(hidden + lowered, gains[1], shifts[5])
    return result.reshape(row_count, seq_len, width)

def reference(cells_in, out_grad, segment_ids, real_lengths, w_qkv, w_attn_out, w_up, w_down, norm_gains, biases, up_bias):
    params = tuple((array.astype(jnp.float32) for array in (w_qkv, w_attn_out, w_up, w_down, norm_gains, biases, up_bias)))
    first_params = tuple((array[0] for array in params))
    second_params = tuple((array[1] for array in params))
    group_rows = math.gcd(ROWS, max(1, 4096 // SEQ))
    group_count = ROWS // group_rows

    def grouped(array):
        return array.reshape((group_count, group_rows) + array.shape[1:])

    def per_group(totals, pieces):
        cells, cotangent, seg_rows, len_rows = pieces

        def forward(cells_value, probe, first_value, second_value):
            first_out = low(one_layer(cells_value, first_value, seg_rows, len_rows))
            second_out = one_layer(low_back(first_out) + probe, second_value, seg_rows, len_rows)
            return (first_out, second_out)
        cells_float = cells.astype(jnp.float32)
        outputs, pullback = jax.vjp(forward, cells_float, jnp.zeros_like(cells_float), first_params, second_params)
        first_out, second_out = outputs
        d_cells, d_probe, d_first, d_second = pullback((jnp.zeros_like(first_out), cotangent.astype(jnp.float32)))
        totals = jax.tree.map(jnp.add, totals, (d_first, d_second))
        return (totals, (first_out.astype(jnp.bfloat16), second_out.astype(jnp.bfloat16), d_cells, d_probe))
    initial = jax.tree.map(jnp.zeros_like, (first_params, second_params))
    totals, stacked = lax.scan(per_group, initial, (grouped(cells_in), grouped(out_grad), grouped(segment_ids), grouped(real_lengths)))
    whole_shape = (ROWS, SEQ, D)
    layer_out = jnp.stack([stacked[0].reshape(whole_shape), stacked[1].reshape(whole_shape)])
    input_grad = jnp.stack([stacked[2].reshape(whole_shape), stacked[3].reshape(whole_shape)])
    grad_list = [jnp.stack([first_grad, second_grad]) for first_grad, second_grad in zip(totals[0], totals[1])]
    return (layer_out, input_grad, grad_list[0], grad_list[1], grad_list[2], grad_list[3], grad_list[4], grad_list[5], grad_list[6])
```

```python
import functools, types
import jax, jax.numpy as jnp
from jax import lax
from jax.experimental import pallas as pl
from jax.experimental.pallas import tpu as pltpu
bf16=jnp.bfloat16; f32=jnp.float32
H=4; HD=64; T=128; RB=256
C0=0.7978845608028654; C1=0.044715
BIG=2.0**50

def dot(a,b): return lax.dot_general(a,b,(((1,),(0,)),((),())),preferred_element_type=f32)
def dot_tn(a,b): return lax.dot_general(a,b,(((0,),(0,)),((),())),preferred_element_type=f32)

def setup(R):
    n=R.n
    tok=lax.broadcasted_iota(jnp.int32,(128,n),1)
    c=lax.broadcasted_iota(jnp.int32,(128,n),0)
    seg=jnp.where(tok<R.length, R.seg_v[...], 12)
    used=c<13
    kc=jnp.where(used&(c==seg),BIG,0.0).astype(bf16)
    qc=jnp.where(used&(c!=seg),-BIG,0.0).astype(bf16).T
    for p in range(2):
        R.qaug[p,:,128:256]=qc
    ones=jnp.where((c<12)&(c%4==0),1.0,0.0)
    for h in range(H):
        R.kaugT[h,128:256,:]=kc
        o=64*(1-h%2)
        R.kaugT[h,o:o+64,:]=jnp.zeros((64,n),bf16)

def ranges(R):
    nt=R.n//T
    real=(R.length+T-1)//T
    for i in range(nt):
        a=R.seg_s[0,i*T]; b=R.seg_s[0,i*T+T-1]
        lo=0; hi=0
        for j in range(nt):
            lo=lo+(R.seg_s[0,j*T+T-1]<a).astype(jnp.int32)
            hi=hi+(R.seg_s[0,j*T]<=b).astype(jnp.int32)
        hi=jnp.minimum(hi,real)
        R.rng[0,i]=lo
        R.rng[1,i]=jnp.where(i<real, hi-lo, 0)

VARIANTS=((0,2),(2,3),(3,4),(4,5),(5,6),(6,8))
def over_tiles(R, full, padded):
    nt=R.n//T
    for i in range(nt):
        lo=max(0,i-4); hi=min(nt,i+5)
        full(i,lo*T,(hi-lo)*T)
def over_tiles_dyn(R, full, padded):
    nt=R.n//T
    def step(i,_):
        lo=R.rng[0,i]; n=R.rng[1,i]
        pl.when(n==0)(lambda: padded(i))
        for a,b in VARIANTS:
            @pl.when((n>a)&(n<=b))
            def _(b=b):
                start=pl.multiple_of(jnp.minimum(lo,nt-b)*T,T)
                full(i,start,b*T)
        return 0
    lax.fori_loop(0,nt,step,0)

def lane_half(rows,h):
    return (lax.broadcasted_iota(jnp.int32,(rows,128),1)//64)==(h%2)

def project(R,l):
    n=R.n
    def step(b,_):
        rows=pl.ds(pl.multiple_of(b*RB,RB),RB)
        sh=jnp.concatenate([R.biases[l,0:1],jnp.zeros((1,256),f32),R.biases[l,1:2]],axis=1)
        pk=(dot(R.x[l,rows,:],R.wqkv[l])+sh).astype(bf16)
        q=pk[:,0:256]*jnp.asarray(0.125,bf16)
        k=pk[:,256:512]; v=pk[:,512:768]
        R.qkv[l,rows,0:256]=q
        R.qkv[l,rows,256:768]=pk[:,256:768]
        R.qaug[0,rows,0:128]=q[:,0:128]
        R.qaug[1,rows,0:128]=q[:,128:256]
        kT=k.T
        for h in range(H):
            R.kaugT[h,64*(h%2):64*(h%2)+64,rows]=kT[64*h:64*h+64]
            m=lane_half(RB,h)
            R.vm[h,rows,:]=jnp.where(m,v[:,128*(h//2):128*(h//2)+128],jnp.zeros((),bf16))
        return 0
    lax.fori_loop(0,n//RB,step,0)

def valid_rows(R,start,rows):
    return (start+lax.broadcasted_iota(jnp.int32,(rows,1),0))<R.length

def attend_tile(R,l,i,lo,W):
    rows=pl.ds(pl.multiple_of(i*T,T),T); cols=pl.ds(lo,W)
    valid=valid_rows(R,i*T,T)
    for p in range(2):
        o=None
        for h in (2*p,2*p+1):
            s=dot(R.qaug[p,rows,:],R.kaugT[h,:,cols])
            m=jnp.max(s,axis=1,keepdims=True)
            e=jnp.exp(s-m)
            r=jnp.where(valid,1.0/jnp.sum(e,axis=1,keepdims=True),0.0)
            pr=(e*r).astype(bf16)
            R.P[l,h,rows,cols]=pr
            t=dot(pr,R.vm[h,cols,:])
            o=t if o is None else o+t
        vv=R.qkv[l,rows,512+128*p:640+128*p].astype(f32)
        oo=jnp.where(valid,o,vv); R.ctx[l,rows,128*p:128*p+128]=oo.astype(bf16); R.octx[l,rows,128*p:128*p+128]=oo

def attend_pad(R,l,i):
    rows=pl.ds(pl.multiple_of(i*T,T),T)
    R.ctx[l,rows,:]=R.qkv[l,rows,512:768]; R.octx[l,rows,:]=R.qkv[l,rows,512:768].astype(f32)

def norm(v):
    c=v-jnp.mean(v,axis=-1,keepdims=True)
    s=lax.rsqrt(jnp.mean(c*c,axis=-1,keepdims=True)+1e-5)
    return c*s,s

def feed(R,l):
    def step(b,_):
        rows=pl.ds(pl.multiple_of(b*RB,RB),RB)
        att=dot(R.ctx[l,rows,:],R.wout[l])+R.biases[l,2:3]
        n1,s1=norm(R.x[l,rows,:].astype(f32)+att)
        hid=n1*R.gains[l,0:1]+R.biases[l,3:4]
        hl=hid.astype(bf16)
        u=dot(hl,R.wup[l])+R.upb[l]
        u2=u*u
        t=jnp.tanh(u*(C0+(C0*C1)*u2))
        hu=0.5*u
        act=(hu+hu*t).astype(bf16)
        gp=0.5+0.5*t+hu*(1.0-t*t)*(C0+(3*C0*C1)*u2)
        low=dot(act,R.wdown[l])+R.biases[l,4:5]
        n2,s2=norm(hid+low)
        out=(n2*R.gains[l,1:2]+R.biases[l,5:6]).astype(bf16)
        R.n1[l,rows,:]=n1; R.s1[l,rows,:]=s1; R.hl[l,rows,:]=hl
        R.gp[l,rows,:]=gp; R.act[l,rows,:]=act
        R.n2[l,rows,:]=n2; R.s2[l,rows,:]=s2
        R.outs[l][rows,:]=out
        if l==0: R.x[1,rows,:]=out
        return 0
    lax.fori_loop(0,R.n//RB,step,0)

def norm_back(g,n,s,gain):
    gg=g*gain
    return s*(gg-jnp.mean(gg,axis=-1,keepdims=True)-n*jnp.mean(gg*n,axis=-1,keepdims=True))

def colsum(v): return jnp.sum(v,axis=0,keepdims=True)

def feed_back(R,l,grad):
    n=R.n
    R.woutT[...]=R.wout[l].T
    R.wupT[...]=R.wup[l].T
    R.wdownT[...]=R.wdown[l].T
    R.wqkvT[...]=R.wqkv[l].T
    R.ggains[l]=jnp.zeros((2,256),f32)
    R.gbias[l]=jnp.zeros((6,256),f32)
    R.gupb[l]=jnp.zeros((1,512),f32)
    c=lax.broadcasted_iota(jnp.int32,(256,128),1); d=lax.broadcasted_iota(jnp.int32,(256,128),0)
    R.sel[...]=jnp.where((c<12)&(d//64==c%4),1.0,0.0).astype(bf16)
    def step(b,_):
        rows=pl.ds(pl.multiple_of(b*RB,RB),RB)
        g=grad(rows)
        n2=R.n2[l,rows,:]
        d2=norm_back(g,n2,R.s2[l,rows,:],R.gains[l,1:2])
        R.ggains[l,1:2]+=colsum(g*n2)
        R.gbias[l,5:6]+=colsum(g)
        dl=d2.astype(bf16)
        R.dlow[rows,:]=dl
        R.gbias[l,4:5]+=colsum(d2)
        du=dot(dl,R.wdownT[...])*R.gp[l,rows,:]
        R.gupb[l]+=colsum(du)
        du=du.astype(bf16)
        R.dup[rows,:]=du
        dh=d2+dot(du,R.wupT[...])
        n1=R.n1[l,rows,:]
        d1=norm_back(dh,n1,R.s1[l,rows,:],R.gains[l,0:1])
        R.ggains[l,0:1]+=colsum(dh*n1)
        R.gbias[l,3:4]+=colsum(dh)
        R.gbias[l,2:3]+=colsum(d1)
        R.d1[rows,:]=d1
        da=d1.astype(bf16)
        R.datt[rows,:]=da
        dc=dot(da,R.woutT[...]).astype(bf16)
        e=dc.astype(f32)*R.octx[l,rows,:]
        eh=e.astype(bf16)
        el=(e-eh.astype(f32)).astype(bf16)
        dt=-(dot(eh,R.sel[...])+dot(el,R.sel[...]))
        h1=dt.astype(bf16).astype(f32)
        r1=dt-h1
        h2=r1.astype(bf16).astype(f32)
        lane=lax.broadcasted_iota(jnp.int32,(RB,128),1)
        cc=jnp.where(lane<4,h1,jnp.where(lane<8,h2,r1-h2)).astype(bf16)
        for p in range(2):
            R.doaug[p,rows,0:128]=dc[:,128*p:128*p+128]
            R.doaug[p,rows,128:256]=cc
        R.doT[:,rows]=dc.T
        k=R.qkv[l,rows,256:512]
        v=R.qkv[l,rows,512:768]
        R.qT[:,rows]=R.qkv[l,rows,0:256].T
        vT=v.T
        for h in range(H):
            m=lane_half(RB,h)
            R.vm[h,rows,:]=jnp.where(m,k[:,128*(h//2):128*(h//2)+128],jnp.zeros((),bf16))
            R.kaugT[h,64*(h%2):64*(h%2)+64,rows]=vT[64*h:64*h+64]
        return 0
    lax.fori_loop(0,n//RB,step,0)
    R.gdown[l]=dot_tn(R.act[l],R.dlow[...])
    R.gup[l]=dot_tn(R.hl[l],R.dup[...])
    R.gout[l]=dot_tn(R.ctx[l],R.datt[...])

def attend_back_tile(R,l,i,lo,W):
    rows=pl.ds(pl.multiple_of(i*T,T),T); cols=pl.ds(lo,W)
    for p in range(2):
        dq=None
        for h in (2*p,2*p+1):
            hs=slice(64*h,64*h+64)
            pr=R.P[l,h,rows,cols]
            dp=dot(R.doaug[p,rows,:],R.kaugT[h,:,cols])
            ds=(pr.astype(f32)*dp).astype(bf16)
            t=dot(ds,R.vm[h,cols,:])
            dq=t if dq is None else dq+t
            R.dvT[hs,cols]+=dot(R.doT[hs,rows],pr)
            R.dkT[hs,cols]+=dot(R.qT[hs,rows],ds)
        R.dqkv[rows,128*p:128*p+128]=(dq*0.125).astype(bf16)

def attend_back_pad(R,l,i):
    rows=pl.ds(pl.multiple_of(i*T,T),T)
    R.dqkv[rows,0:256]=jnp.zeros((T,256),bf16)

def project_back(R,l,put):
    def step(b,_):
        rows=pl.ds(pl.multiple_of(b*RB,RB),RB)
        valid=valid_rows(R,b*RB,RB)
        dk=R.dkT[:,rows].T
        dv=R.dvT[:,rows].T
        dc=jnp.concatenate([R.doaug[0,rows,0:128],R.doaug[1,rows,0:128]],axis=1)
        dv=dv+jnp.where(valid,0.0,dc.astype(f32))
        R.dqkv[rows,256:512]=dk.astype(bf16)
        R.dqkv[rows,512:768]=dv.astype(bf16)
        R.gbias[l,1:2]+=colsum(dv)
        R.gbias[l,0:1]+=colsum(R.dqkv[rows,0:256].astype(f32))
        put(rows,R.d1[rows,:]+dot(R.dqkv[rows,:],R.wqkvT[...]))
        return 0
    lax.fori_loop(0,R.n//RB,step,0)
    R.gqkv[l]=dot_tn(R.x[l],R.dqkv[...])

def forward(R,l):
    project(R,l)
    over_tiles(R,functools.partial(attend_tile,R,l),functools.partial(attend_pad,R,l))
    feed(R,l)

def backward(R,l,grad,put):
    feed_back(R,l,grad)
    R.dkT[...]=jnp.zeros_like(R.dkT)
    R.dvT[...]=jnp.zeros_like(R.dvT)
    over_tiles(R,functools.partial(attend_back_tile,R,l),functools.partial(attend_back_pad,R,l))
    project_back(R,l,put)

def scratch(n):
    V=lambda *s: pltpu.VMEM(s[:-1],s[-1])
    return dict(
        x=V(2,n,256,bf16), qkv=V(2,n,768,bf16), ctx=V(2,n,256,bf16),octx=V(2,n,256,f32), P=V(2,H,n,n,bf16),
        n1=V(2,n,256,f32), s1=V(2,n,1,f32), n2=V(2,n,256,f32), s2=V(2,n,1,f32),
        hl=V(2,n,256,bf16), gp=V(2,n,512,f32), act=V(2,n,512,bf16),
        qaug=V(2,n,256,bf16), kaugT=V(H,256,n,bf16), vm=V(H,n,128,bf16),
        doaug=V(2,n,256,bf16), doT=V(256,n,bf16), qT=V(256,n,bf16),
        dkT=V(256,n,f32), dvT=V(256,n,f32), dqkv=V(n,768,bf16),
        dlow=V(n,256,bf16), dup=V(n,512,bf16), datt=V(n,256,bf16), d1=V(n,256,f32),
        woutT=V(256,256,bf16), wupT=V(512,256,bf16), wdownT=V(256,512,bf16), wqkvT=V(768,256,bf16),
        sel=V(256,128,bf16), rng=pltpu.SMEM((2,n//T),jnp.int32))


MESHID=pl.DeviceIdType.MESH
INS=["len_s","seg_v","cells","ograd","wqkv","wout","wup","wdown","gains","biases","upb"]
OUTS=["out0","out1","din0","din1","rout","rdin","gqkv","gout","gup","gdown","ggains","gbias","gupb"]
def kernel_call(seg,length,cells,ograd,wqkv,wout,wup,wdown,gains,biases,upb):
    n=cells.shape[0]
    sc=scratch(n); sc["ss"]=pltpu.SemaphoreType.DMA((2,)); sc["rs"]=pltpu.SemaphoreType.DMA((2,)); names=list(sc)
    def kern(*refs):
        R=types.SimpleNamespace(**dict(zip(INS+OUTS+names,refs)))
        R.n=n; R.length=R.len_s[0]; R.outs=[R.out0,R.out1]
        sec=lax.axis_index("section")
        other=(1-sec,lax.axis_index("dp"))
        bar=pltpu.get_barrier_semaphore()
        pl.semaphore_signal(bar,1,device_id=other,device_id_type=MESHID)
        pl.semaphore_wait(bar,1)
        setup(R)
        R.x[0]=R.cells[...]
        forward(R,0); forward(R,1)
        R.so[...]=jnp.where(sec==0,R.out1[...],R.out0[...])
        c0=pltpu.make_async_remote_copy(R.so,R.rout,R.ss.at[0],R.rs.at[0],device_id=other,device_id_type=MESHID)
        c0.start()
        cc=lax.broadcasted_iota(jnp.int32,(128,n),0)
        for h in range(H): R.kaugT[h,128:256,:]=jnp.where((cc<12)&(cc%4==h),1.0,0.0).astype(bf16)
        def put1(rows,v): R.din1[rows,:]=v
        def put0(rows,v): R.din0[rows,:]=v
        backward(R,1,lambda rows: R.ograd[rows,:].astype(f32),put1)
        backward(R,0,lambda rows: R.din1[rows,:].astype(bf16).astype(f32),put0)
        R.sd[...]=jnp.where(sec==0,R.din1[...],R.din0[...]).astype(bf16)
        c1=pltpu.make_async_remote_copy(R.sd,R.rdin,R.ss.at[1],R.rs.at[1],device_id=other,device_id_type=MESHID)
        c1.start(); c0.wait(); c1.wait()
    sc["so"]=pltpu.VMEM((n,256),bf16); sc["sd"]=pltpu.VMEM((n,256),bf16); names.extend(["so","sd"])
    vm=pl.BlockSpec(memory_space=pltpu.VMEM); sm=pl.BlockSpec(memory_space=pltpu.SMEM)
    outs=[jax.ShapeDtypeStruct((n,256),bf16)]*2+[jax.ShapeDtypeStruct((n,256),f32)]*2+[jax.ShapeDtypeStruct((n,256),bf16)]*2+[jax.ShapeDtypeStruct(s,f32) for s in ((2,256,768),(2,256,256),(2,256,512),(2,512,256),(2,2,256),(2,6,256),(2,1,512))]
    return pl.pallas_call(kern,out_shape=outs,in_specs=[sm]+[vm]*10,out_specs=[vm]*13,scratch_shapes=list(sc.values()),
        compiler_params=pltpu.CompilerParams(vmem_limit_bytes=64*2**20,collective_id=0,has_side_effects=True))(length,seg,cells,ograd,wqkv,wout,wup,wdown,gains,biases,upb.reshape(2,1,512))

def on_device(cells_in,out_grad,segment_ids,real_lengths,*weights):
    sec=lax.axis_index("section")
    def both(w):
        o=lax.ppermute(w,"section",[(0,1),(1,0)])
        return jnp.where(sec==0,jnp.concatenate([w,o]),jnp.concatenate([o,w]))
    ws=[both(w) for w in weights]
    mine=lambda a: lax.dynamic_index_in_dim(a,sec,0,keepdims=False)
    out0,out1,din0,din1,rout,rdin,*grads=kernel_call(mine(segment_ids)[None],mine(real_lengths)[None],mine(cells_in),mine(out_grad),*ws)
    first=sec==0
    layer_out=jnp.where(first,jnp.stack([out0,rout]),jnp.stack([rout,out1]))[None]
    rd=rdin.astype(f32)
    input_grad=jnp.where(first,jnp.stack([din0,rd]),jnp.stack([rd,din1]))[None]
    grads=lax.psum(grads,("section","dp"))
    grads=[lax.dynamic_index_in_dim(g,sec,0,keepdims=True) for g in grads]
    grads[-1]=grads[-1].reshape(1,512)
    return (layer_out,input_grad,*grads)

def solution(mesh):
    from jax.sharding import PartitionSpec as P
    w3=P("section",None,None); w2=P("section",None)
    return jax.shard_map(on_device,mesh=mesh,
        in_specs=(P("dp",None,None),P("dp",None,None),P("dp",None),P("dp"),w3,w3,w3,w3,w3,w3,w2),
        out_specs=(P("section","dp",None,None),P("section","dp",None,None),w3,w3,w3,w3,w3,w3,w2),check_vma=False)
```

```python
import types

import jax
import jax.numpy as jnp
from jax import lax
from jax.experimental import pallas as pl
from jax.experimental.pallas import tpu as pltpu
from jax.sharding import PartitionSpec as P

MESH = pl.DeviceIdType.MESH
bf16 = jnp.bfloat16
f32 = jnp.float32
HEADS = 4
TILE = 256
REACH = 511
SEGMENTS = 12
CODE = 2.0**50
GELU_A = 0.7978845608028654
GELU_B = 0.044715


def dot(a, b):
    return lax.dot_general(a, b, (((1,), (0,)), ((), ())), preferred_element_type=f32)


def dot_tn(a, b):
    return lax.dot_general(a, b, (((0,), (0,)), ((), ())), preferred_element_type=f32)


def lanes(rows, width=128):
    return lax.broadcasted_iota(jnp.int32, (rows, width), 1)


def column_sum(v):
    return jnp.sum(v, axis=0, keepdims=True)


def setup(R):
    n = R.n
    token = lax.broadcasted_iota(jnp.int32, (64, n), 1)
    code = lax.broadcasted_iota(jnp.int32, (64, n), 0)
    segment = jnp.where(token < R.length, R.seg_row, SEGMENTS)
    used = code <= SEGMENTS
    key_code = jnp.where(used & (code == segment), CODE, 0.0).astype(bf16)
    query_code = jnp.where(used & (code != segment), -CODE, 0.0).astype(bf16)
    R.qcode[...] = jnp.concatenate([jnp.zeros((64, n), bf16), query_code], axis=0).T
    for h in range(HEADS):
        R.kc[128 * h + 64 : 128 * h + 128, :] = key_code
    R.vT[256:320, :] = jnp.zeros((64, n), bf16)


def spans(n):
    out = []
    for i in range(n // TILE):
        lo = max(0, (i * TILE - REACH) // 128 * 128)
        hi = min(n, -(-(i * TILE + TILE + REACH) // 128) * 128)
        out.append((lo, hi - lo))
    return out


def head_tile(pair, h):
    return pair if h % 2 == 0 else pltpu.roll(pair, 64, 1)


def real_rows(R, start, rows):
    return (start + lax.broadcasted_iota(jnp.int32, (rows, 1), 0)) < R.length


def pick_heads(t):
    lane = lanes(TILE, 256) // 64
    o = t[0:TILE]
    for h in range(1, HEADS):
        o = jnp.where(lane == h, t[h * TILE : h * TILE + TILE], o)
    return o


def project(R, l):
    n = R.n
    shift = jnp.concatenate([R.biases[l, 0:1], jnp.zeros((1, 256), f32), R.biases[l, 1:2]], axis=1)
    packed = dot(R.x[l], R.wqkv[l]) + shift
    lane = lanes(n)
    q = packed[:, 0:256] * 0.125
    R.qn[l] = q.astype(bf16)
    for h in range(HEADS):
        t = head_tile(q[:, 128 * (h // 2) : 128 * (h // 2) + 128], h)
        R.qh[h] = jnp.where(lane < 64, t, 0.0).astype(bf16) + R.qcode[...]
    k = packed[:, 256:512].astype(bf16)
    R.kn[l] = k
    R.vn[l] = packed[:, 512:768].astype(bf16)
    kT = k.T
    for h in range(HEADS):
        R.kc[128 * h : 128 * h + 64, :] = kT[64 * h : 64 * h + 64]


def attend_tile(R, l, i):
    lo, width = spans(R.n)[i]
    rows, cols = pl.ds(i * TILE, TILE), pl.ds(lo, width)
    real = real_rows(R, i * TILE, TILE)
    for h in range(HEADS):
        s = dot(R.qh[h, rows, :], R.kc[128 * h : 128 * h + 128, cols])
        e = jnp.exp(s - jnp.max(s, axis=1, keepdims=True))
        r = jnp.where(real, 1.0 / jnp.sum(e, axis=1, keepdims=True), 0.0)
        R.P[i][h * TILE : h * TILE + TILE, :] = (e * r).astype(bf16)
    o = pick_heads(dot(R.P[i][...], R.vn[l, cols, :]))
    o = jnp.where(real, o, R.vn[l, rows, :].astype(f32))
    R.octx[l, rows, :] = o


def norm(v):
    c = v - jnp.mean(v, axis=-1, keepdims=True)
    s = lax.rsqrt(jnp.mean(c * c, axis=-1, keepdims=True) + 1e-5)
    return c * s, s


def feed(R, l):
    att = dot(R.octx[l].astype(bf16), R.wout[l]) + R.biases[l, 2:3]
    n1, s1 = norm(R.x[l].astype(f32) + att)
    hidden = n1 * R.gains[l, 0:1] + R.biases[l, 3:4]
    low = hidden.astype(bf16)
    u = dot(low, R.wup[l]) + R.upb[l]
    q = (GELU_A * GELU_B) * (u * u)
    w = 0.5 * jnp.tanh(u * (q + GELU_A)) + 0.5
    a = u * w
    act = a.astype(bf16)
    slope = w + a * ((1.0 - w) * (6.0 * q + 2.0 * GELU_A))
    n2, s2 = norm(hidden + (dot(act, R.wdown[l]) + R.biases[l, 4:5]))
    R.n1[l] = n1
    R.stat[l, :, 4:5] = s1
    R.gp[l] = slope
    R.act[l] = act
    R.n2[l] = n2
    R.stat[l, :, 5:6] = s2
    R.x[l + 1] = (n2 * R.gains[l, 1:2] + R.biases[l, 5:6]).astype(bf16)


def norm_back(g, n, s, gain):
    gg = g * gain
    return s * (gg - jnp.mean(gg, axis=-1, keepdims=True) - n * jnp.mean(gg * n, axis=-1, keepdims=True))


def put_small(ref, row, v):
    ref[0, row : row + 1, :] = v[:, 0:128]
    ref[1, row : row + 1, :] = v[:, 128:256]


def feed_back(R, l, g):
    n = R.n
    R.woutT[...] = R.wout[l].T
    R.wupT[...] = R.wup[l].T
    R.wdownT[...] = R.wdown[l].T
    R.wqkvT[...] = R.wqkv[l].T
    small = R.small_a.at[l]
    n2 = R.n2[l]
    d2 = norm_back(g, n2, R.stat[l, :, 5:6], R.gains[l, 1:2])
    put_small(small, 1, column_sum(g * n2))
    put_small(small, 5, column_sum(g))
    dl = d2.astype(bf16)
    R.dlow[...] = dl
    put_small(small, 4, column_sum(d2))
    du = dot(dl, R.wdownT[...]) * R.gp[l]
    up = column_sum(du)
    put_small(small, 6, up[:, 0:256])
    put_small(small, 7, up[:, 256:512])
    du = du.astype(bf16)
    R.dup[...] = du
    dh = d2 + dot(du, R.wupT[...])
    n1 = R.n1[l]
    low = (n1 * R.gains[l, 0:1] + R.biases[l, 3:4]).astype(bf16)
    d1 = norm_back(dh, n1, R.stat[l, :, 4:5], R.gains[l, 0:1])
    put_small(small, 0, column_sum(dh * n1))
    put_small(small, 3, column_sum(dh))
    put_small(small, 2, column_sum(d1))
    R.d1[...] = d1
    da = d1.astype(bf16)
    R.datt[...] = da
    dcb = dot(da, R.woutT[...]).astype(bf16)
    R.dctx[...] = dcb
    dc = dcb.astype(f32)
    e = dc * R.octx[l]
    lane = lanes(n)
    for h in range(HEADS):
        pair = slice(128 * (h // 2), 128 * (h // 2) + 128)
        R.delta[:, h : h + 1] = jnp.sum(
            jnp.where((lane // 64) == (h % 2), e[:, pair], 0.0), axis=1, keepdims=True
        )
        R.doh[h] = jnp.where(lane < 64, head_tile(dc[:, pair], h), 0.0).astype(bf16)
    R.doT[...] = dcb.T
    R.qT[...] = R.qn[l].T
    R.vT[0:256, :] = R.vn[l].T
    R.grad_a[l, :, 0:256] = dot_tn(R.octx[l].astype(bf16), R.datt[...])
    R.grad_a[l, :, 256:768] = dot_tn(low, R.dup[...])
    R.grad_a[l, :, 768:1280] = dot_tn(R.dlow[...], R.act[l])
    R.dkT[...] = jnp.zeros_like(R.dkT)
    R.dvT[...] = jnp.zeros_like(R.dvT)


def attend_back_tile(R, l, i):
    lo, width = spans(R.n)[i]
    rows, cols = pl.ds(i * TILE, TILE), pl.ds(lo, width)
    for h in range(HEADS):
        head, part = slice(64 * h, 64 * h + 64), slice(h * TILE, h * TILE + TILE)
        p = R.P[i][part, :]
        dp = dot(R.doh[h, rows, :], R.vT[64 * h : 64 * h + 128, cols])
        R.DS[part, 0:width] = (p.astype(f32) * (dp - R.delta[rows, h : h + 1])).astype(bf16)
        R.dvT[head, cols] += dot(R.doT[head, rows], p)
    for h in range(HEADS):
        head, part = slice(64 * h, 64 * h + 64), slice(h * TILE, h * TILE + TILE)
        R.dkT[head, cols] += dot(R.qT[head, rows], R.DS[part, 0:width])
    R.dqkv[rows, 0:256] = (pick_heads(dot(R.DS[:, 0:width], R.kn[l, cols, :])) * 0.125).astype(bf16)


def project_back(R, l):
    real = real_rows(R, 0, R.n)
    dv = R.dvT[...].T + jnp.where(real, 0.0, R.dctx[...].astype(f32))
    R.dqkv[:, 256:512] = R.dkT[...].T.astype(bf16)
    R.dqkv[:, 512:768] = dv.astype(bf16)
    put_small(R.small_b.at[l], 0, column_sum(R.dqkv[:, 0:256].astype(f32)))
    put_small(R.small_b.at[l], 1, column_sum(dv))
    d = R.d1[...] + dot(R.dqkv[...], R.wqkvT[...])
    R.d1[...] = d
    R.dinb[l] = d.astype(bf16)


def weight_back(R, l):
    R.grad_b[l] = dot_tn(R.x[l], R.dqkv[...])


class Links:
    def __init__(self, dp, send, recv, local):
        self.sec = lax.axis_index("section")
        self.dp = lax.axis_index("dp")
        self.send, self.recv, self.local_sem = send, recv, local
        self.used = 0
        self.used_local = 0
        self.core = self.dp % 2
        self.chips = min(8, dp // 2)
        self.groups = dp // (2 * self.chips)
        self.chip = (self.dp // 2) % self.chips
        self.pending = []

    def flip(self, index, bit):
        return index + bit - 2 * bit * ((index // bit) % 2)

    def xor(self, index, mask):
        bit = 1
        while bit <= mask:
            if mask & bit:
                index = self.flip(index, bit)
            bit *= 2
        return index

    def section_peer(self):
        return (1 - self.sec, self.dp)

    def core_peer(self):
        return (self.sec, self.flip(self.dp, 1))

    def chip_peer(self, k):
        return (self.sec, self.xor(self.dp, 2 * k))

    def group_peer(self, k):
        return (self.sec, self.xor(self.dp, 2 * self.chips * k))

    def peers(self):
        out = [self.section_peer(), self.core_peer()]
        out += [self.chip_peer(k) for k in range(1, self.chips)]
        out += [self.group_peer(k) for k in range(1, self.groups)]
        return out

    def remote(self, src, dst, peer):
        i = self.used
        self.used += 1
        return pltpu.make_async_remote_copy(
            src, dst, self.send.at[i], self.recv.at[i], device_id=peer, device_id_type=MESH
        )

    def local(self, src, dst):
        i = self.used_local
        self.used_local += 1
        return pltpu.make_async_copy(src, dst, self.local_sem.at[i])


def reduction(K, l, grad, small, R, name):
    get = lambda part: getattr(R, name + "_" + part).at[l]
    r1, s2, r2, acc, r3, res = [get(p) for p in ("r1", "s2", "r2", "acc", "r3", "res")]
    q1, q2, t2, qacc, q3, qres = [get(p) for p in ("q1", "q2", "t2", "qacc", "q3", "qres")]
    c, chip, chips, groups = K.core, K.chip, K.chips, K.groups
    half = grad.shape[0] // 2
    piece = half // chips
    mine = pl.ds(c * half, half)
    other = pl.ds((1 - c) * half, half)
    part = pl.ds(c * half + chip * piece, piece)
    owner = K.sec == l
    core_out = [
        K.remote(grad.at[other], r1, K.core_peer()),
        K.remote(small.at[1 - c], q1, K.core_peer()),
    ]
    scatter = []
    for k in range(1, chips):
        there = K.xor(chip, k)
        scatter.append(K.remote(s2.at[pl.ds(there * piece, piece)], r2.at[k], K.chip_peer(k)))
        scatter.append(K.remote(q2, t2.at[k], K.chip_peer(k)))
    across = [K.remote(acc, r3, K.section_peer()), K.remote(qacc, q3, K.section_peer())]
    spread = []
    if groups > 1:
        r4, q4 = get("r4"), get("q4")
        for k in range(1, groups):
            spread.append(K.remote(acc, r4.at[k], K.group_peer(k)))
            spread.append(K.remote(qacc, q4.at[k], K.group_peer(k)))
    gather = [K.remote(res.at[part], res.at[part], K.chip_peer(k)) for k in range(1, chips)]
    core_back = K.remote(res.at[mine], res.at[mine], K.core_peer())
    small_back = K.remote(qres.at[c], qres.at[c], K.core_peer())

    def begin():
        for x in core_out:
            x.start()

    def scatter_pieces():
        for x in core_out:
            x.wait()
        total = grad[mine, :] + r1[...]
        grad[mine, :] = total
        s2[...] = total.astype(bf16)
        q2[...] = small[c] + q1[...]
        for x in scatter:
            x.start()

    def sum_pieces():
        for x in scatter:
            x.wait()
        total = grad[part, :]
        little = q2[...]
        for k in range(1, chips):
            total = total + r2[k].astype(f32)
            little = little + t2[k]
        acc[...] = total
        qacc[...] = little

        @pl.when(jnp.logical_not(owner))
        def _():
            for x in across:
                x.start()
                x.wait_send()

    def gather_pieces():
        @pl.when(owner)
        def _():
            for x in across:
                x.wait_recv()
            acc[...] += r3[...]
            qacc[...] += q3[...]
            for x in spread:
                x.start()
            for x in spread:
                x.wait()
            total, little = acc[...], qacc[...]
            for k in range(1, groups):
                total = total + r4[k]
                little = little + q4[k]
            res[part, :] = total.astype(bf16)
            qres[c] = little
            for x in gather:
                x.start()
            small_back.start()

    def share():
        @pl.when(owner)
        def _():
            for x in gather:
                x.wait()
            core_back.start()

    def finish(write):
        @pl.when(owner)
        def _():
            core_back.wait()
            small_back.wait()
            write(res, qres)

    return begin, scatter_pieces, sum_pieces, gather_pieces, share, finish


def scratch(n, chips, groups):
    def V(*s):
        return pltpu.VMEM(s[:-1], s[-1])

    out = dict(
        wqkv=V(2, 256, 768, bf16), wout=V(2, 256, 256, bf16), wup=V(2, 256, 512, bf16), wdown=V(2, 512, 256, bf16),
        gains=V(2, 2, 256, f32), biases=V(2, 6, 256, f32), upb=V(2, 1, 512, f32),
        x=V(3, n, 256, bf16), qn=V(2, n, 256, bf16), kn=V(2, n, 256, bf16), vn=V(2, n, 256, bf16),
        octx=V(2, n, 256, f32), DS=V(HEADS * TILE, n, bf16),
        n1=V(2, n, 256, f32), n2=V(2, n, 256, f32), stat=V(2, n, 128, f32),
        gp=V(2, n, 512, f32), act=V(2, n, 512, bf16),
        qcode=V(n, 128, bf16), qh=V(HEADS, n, 128, bf16), kc=V(512, n, bf16), vT=V(320, n, bf16),
        doh=V(HEADS, n, 128, bf16), doT=V(256, n, bf16), qT=V(256, n, bf16), delta=V(n, 128, f32), dctx=V(n, 256, bf16),
        dkT=V(256, n, f32), dvT=V(256, n, f32), dqkv=V(n, 768, bf16),
        d1=V(n, 256, f32),
        woutT=V(256, 256, bf16), wupT=V(512, 256, bf16), wdownT=V(256, 512, bf16), wqkvT=V(768, 256, bf16),
        dinb=V(2, n, 256, bf16), rdin=V(n, 256, bf16),
        small_a=V(2, 2, 8, 128, f32), small_b=V(2, 2, 8, 128, f32),
    )
    for name, width in (("a", 1280), ("b", 768)):
        piece = 128 // chips
        out["grad_" + name] = V(2, 256, width, f32)
        out[name + "_r1"] = V(2, 128, width, f32)
        out[name + "_s2"] = V(2, 128, width, bf16)
        out[name + "_r2"] = V(2, chips, piece, width, bf16)
        out[name + "_acc"] = V(2, piece, width, f32)
        out[name + "_r3"] = V(2, piece, width, f32)
        out[name + "_res"] = V(2, 256, width, bf16)
        out[name + "_q1"] = V(2, 8, 128, f32)
        out[name + "_q2"] = V(2, 8, 128, f32)
        out[name + "_t2"] = V(2, chips, 8, 128, f32)
        out[name + "_qacc"] = V(2, 8, 128, f32)
        out[name + "_q3"] = V(2, 8, 128, f32)
        out[name + "_qres"] = V(2, 2, 8, 128, f32)
        if groups > 1:
            out[name + "_r4"] = V(2, groups, piece, width, f32)
            out[name + "_q4"] = V(2, groups, 8, 128, f32)
    for i, (_, width) in enumerate(spans(n)):
        out["P%d" % i] = V(HEADS * TILE, width, bf16)
    copies = 32 + 4 * (8 + 3 * chips + 2 * groups)
    out["send"] = pltpu.SemaphoreType.DMA((copies,))
    out["recv"] = pltpu.SemaphoreType.DMA((copies,))
    out["local"] = pltpu.SemaphoreType.DMA((64,))
    return out


INS = ["len_s", "seg_v", "cells", "ograd", "i_wqkv", "i_wout", "i_wup", "i_wdown", "i_gains", "i_biases", "i_upb"]
OUTS = ["layer_out", "input_grad", "gqkv", "gout", "gup", "gdown", "ggains", "gbias", "gupb"]
WEIGHTS = ["wqkv", "wout", "wup", "wdown", "gains", "biases", "upb"]


def body(R, n, dp):
    K = Links(dp, R.send, R.recv, R.local)
    sec, c = K.sec, K.core
    R.n = n
    R.P = [getattr(R, "P%d" % i) for i in range(n // TILE)]
    R.dup = R.DS.at[:, pl.ds(0, 512)]
    R.dlow = R.DS.at[:, pl.ds(512, 256)]
    R.datt = R.DS.at[:, pl.ds(768, 256)]
    R.length = R.len_s[sec]
    R.seg_row = R.seg_v[pl.ds(sec, 1), :]

    barrier = pltpu.get_barrier_semaphore()
    peers = K.peers()
    for peer in peers:
        pl.semaphore_signal(barrier, 1, device_id=peer, device_id_type=MESH)

    take_x = K.local(R.cells.at[sec], R.x.at[0])
    take_g = K.local(R.ograd.at[sec], R.dinb.at[0])
    own = [K.local(getattr(R, "i_" + w).at[0], getattr(R, w).at[sec]) for w in WEIGHTS]
    take_x.start()
    for x in own:
        x.start()
    take_g.start()

    away, forward_on = {}, {}
    for w in WEIGHTS:
        src, slots = getattr(R, "i_" + w).at[0], getattr(R, w)
        if w in ("gains", "biases", "upb"):
            away[w] = K.remote(src, slots.at[sec], K.section_peer())
        else:
            half = src.shape[0] // 2
            rows = pl.ds(c * half, half)
            away[w] = K.remote(src.at[rows], slots.at[sec, rows], K.section_peer())
            theirs = slots.at[1 - sec, rows]
            forward_on[w] = K.remote(theirs, theirs, K.core_peer())

    setup(R)
    pl.semaphore_wait(barrier, len(peers))
    first = ("biases", "wqkv")
    second = ("gains", "upb", "wout", "wup", "wdown")
    for w in first + second:
        away[w].start()
    take_x.wait()
    for x in own:
        x.wait()
    for w in first:
        away[w].wait()
    forward_on["wqkv"].start()
    forward_on["wqkv"].wait()

    n_tiles = n // TILE
    x_out = [
        (K.local(R.x.at[l + 1], R.layer_out.at[0, sec]), K.remote(R.x.at[l + 1], R.layer_out.at[0, sec], K.section_peer()))
        for l in range(2)
    ]

    def start_out(l, pair):
        pl.when(sec == l)(pair[0].start)
        pl.when(sec != l)(pair[1].start)

    stash = [getattr(R, "stash%d" % i) for i in range(n_tiles)]
    put_away = [K.local(R.P[i], stash[i]) for i in range(n_tiles)]
    bring_back = [K.local(stash[i], R.P[i]) for i in range(n_tiles)]
    for l in range(2):
        project(R, l)
        for i in range(n_tiles):
            if l == 1:
                put_away[i].wait()
            attend_tile(R, l, i)
            if l == 0:
                put_away[i].start()
                if i == n_tiles - 2:
                    for w in second:
                        away[w].wait()
                    for w in ("wout", "wup", "wdown"):
                        forward_on[w].start()
        if l == 0:
            for w in ("wout", "wup", "wdown"):
                forward_on[w].wait()
        feed(R, l)
        start_out(l, x_out[l])

    R.small_b[...] = jnp.zeros_like(R.small_b)
    A = [reduction(K, l, R.grad_a.at[l], R.small_a.at[l], R, "a") for l in range(2)]
    B = [reduction(K, l, R.grad_b.at[l], R.small_b.at[l], R, "b") for l in range(2)]
    BEGIN, SCATTER, SUM, GATHER, SHARE, FINISH = range(6)

    din_local = [K.local(R.d1, R.input_grad.at[0, sec]) for l in range(2)]
    quarter = n // 4
    din_away = [
        K.remote(R.dinb.at[1], R.rdin, K.section_peer()),
        [K.remote(R.dinb.at[0, pl.ds(i * quarter, quarter)], R.rdin.at[pl.ds(i * quarter, quarter)], K.section_peer()) for i in range(4)],
    ]
    take_g.wait()

    def start_din(l):
        @pl.when(sec == l)
        def _():
            din_local[l].start()

        @pl.when(sec != l)
        def _():
            for x in [din_away[0]] if l == 1 else din_away[1]:
                x.start()

    for j in range(2):
        l = 1 - j
        if j == 1:
            pl.when(sec == 1)(din_local[1].wait)
        feed_back(R, l, R.dinb[j].astype(f32))
        A[l][BEGIN]()
        if j == 1:
            B[1][SCATTER]()
        for i in range(n_tiles):
            if j == 1:
                bring_back[i].wait()
            attend_back_tile(R, l, i)
            if j == 0:
                bring_back[i].start()
            if i == 1:
                A[l][SCATTER]()
            if i == 2 and j == 1:
                A[1][SUM]()
            if i == 3 and j == 1:
                B[1][SUM]()
        project_back(R, l)
        start_din(l)
        weight_back(R, l)
        B[l][BEGIN]()

    downT = R.octx.at[1, pl.ds(0, 512)]

    def rows_of_small(qres, row):
        return jnp.concatenate([qres[0, row : row + 1, :], qres[1, row : row + 1, :]], axis=1)

    outs = []

    def write_a(l):
        copies = [
            K.local(R.grad_a.at[l, :, pl.ds(0, 256)], R.gout.at[0]),
            K.local(R.grad_a.at[l, :, pl.ds(256, 512)], R.gup.at[0]),
            K.local(downT, R.gdown.at[0]),
        ]

        def write(res, qres):
            R.grad_a[l, :, 0:768] = res[:, 0:768].astype(f32)
            downT[...] = res[:, 768:1280].astype(f32).T
            for i in range(2):
                R.ggains[0, i : i + 1, :] = rows_of_small(qres, i)
                R.gupb[0, :, 256 * i : 256 * i + 256] = rows_of_small(qres, 6 + i)
            for i in range(2, 6):
                R.gbias[0, i : i + 1, :] = rows_of_small(qres, i)
            for x in copies:
                x.start()

        outs.append((l, copies))
        return write

    def write_b(l):
        copies = [K.local(R.grad_b.at[l], R.gqkv.at[0])]

        def write(res, qres):
            R.grad_b[l] = res[...].astype(f32)
            for i in range(2):
                R.gbias[0, i : i + 1, :] = rows_of_small(qres, i)
            for x in copies:
                x.start()

        outs.append((l, copies))
        return write

    A[1][GATHER]()
    B[1][GATHER]()
    B[0][SCATTER]()
    A[0][SUM]()
    A[1][SHARE]()
    B[1][SHARE]()
    A[0][GATHER]()
    B[0][SUM]()
    A[1][FINISH](write_a(1))
    B[1][FINISH](write_b(1))
    B[0][GATHER]()

    widen = [K.local(R.octx.at[0, pl.ds(i * quarter, quarter)], R.input_grad.at[0, 1 - sec, pl.ds(i * quarter, quarter)]) for i in range(4)]

    def take(i):
        rows = pl.ds(i * quarter, quarter)
        R.octx[0, rows, :] = R.rdin[rows, :].astype(f32)
        widen[i].start()

    @pl.when(sec == 1)
    def _():
        din_away[0].wait_recv()
        for i in range(4):
            take(i)

    A[0][SHARE]()

    @pl.when(sec == 0)
    def _():
        for i in range(4):
            din_away[1][i].wait_recv()
            take(i)

    B[0][SHARE]()
    A[0][FINISH](write_a(0))
    B[0][FINISH](write_b(0))

    for i in range(4):
        widen[i].wait()
    for l in range(2):

        @pl.when(sec == l)
        def _():
            x_out[l][0].wait()
            x_out[1 - l][1].wait_send()
            x_out[l][1].wait_recv()
            if l == 0:
                din_local[0].wait()
                din_away[0].wait_send()
            else:
                for x in din_away[1]:
                    x.wait_send()
            for owner, copies in outs:
                if owner == l:
                    for x in copies:
                        x.wait()


def kernel_call(dp, n, lengths, segments, cells, ograd, *weights):
    chips = min(8, dp // 2)
    groups = dp // (2 * chips)
    sc = scratch(n, chips, groups)

    def kern(*refs):
        body(types.SimpleNamespace(**dict(zip(names, refs))), n, dp)

    stash = [(HEADS * TILE, width) for _, width in spans(n)]
    names = INS + OUTS + ["stash%d" % i for i in range(len(stash))] + list(sc)
    vmem, smem, anywhere = [pl.BlockSpec(memory_space=m) for m in (pltpu.VMEM, pltpu.SMEM, pl.ANY)]
    shapes = [((1, 2, n, 256), bf16), ((1, 2, n, 256), f32), ((1, 256, 768), f32), ((1, 256, 256), f32),
              ((1, 256, 512), f32), ((1, 512, 256), f32), ((1, 2, 256), f32), ((1, 6, 256), f32), ((1, 1, 512), f32)] + [(s, bf16) for s in stash]
    return pl.pallas_call(
        kern,
        out_shape=[jax.ShapeDtypeStruct(*s) for s in shapes],
        in_specs=[smem, vmem] + [anywhere] * 9,
        out_specs=[anywhere] * 6 + [vmem] * 3 + [anywhere] * len(stash),
        scratch_shapes=list(sc.values()),
        compiler_params=pltpu.CompilerParams(
            vmem_limit_bytes=64 * 2**20, collective_id=0, has_side_effects=True
        ),
    )(lengths, segments, cells, ograd, *weights)


def solution(mesh):
    dp = mesh.shape["dp"]

    def on_device(cells, ograd, segments, lengths, *weights):
        weights = weights[:-1] + (weights[-1][:, None, :],)
        out = kernel_call(dp, cells.shape[1], lengths, segments, cells, ograd, *weights)
        return (*out[:8], out[8][:, 0, :])

    w3, w2 = P("section", None, None), P("section", None)
    rows = P("section", "dp", None, None)
    return jax.shard_map(
        on_device,
        mesh=mesh,
        in_specs=(P("dp", None, None), P("dp", None, None), P("dp", None), P("dp"), w3, w3, w3, w3, w3, w3, w2),
        out_specs=(rows, rows, w3, w3, w3, w3, w3, w3, w2),
        check_vma=False,
    )
```

```python
import types

import jax
import jax.numpy as jnp
from jax import lax
from jax.experimental import pallas as pl
from jax.experimental.pallas import tpu as pltpu
from jax.sharding import PartitionSpec as P

MESH = pl.DeviceIdType.MESH
bf16 = jnp.bfloat16
f32 = jnp.float32
HEADS = 4
TILE = 256
REACH = 511
SEGMENTS = 12
CODE = 2.0**50
GELU_A = 0.7978845608028654
GELU_B = 0.044715


def dot(a, b):
    return lax.dot_general(a, b, (((1,), (0,)), ((), ())), preferred_element_type=f32)


def dot_tn(a, b):
    return lax.dot_general(a, b, (((0,), (0,)), ((), ())), preferred_element_type=f32)


def lanes(rows, width=128):
    return lax.broadcasted_iota(jnp.int32, (rows, width), 1)


def column_sum(v):
    return jnp.sum(v, axis=0, keepdims=True)


def setup(R):
    n = R.n
    token = lax.broadcasted_iota(jnp.int32, (64, n), 1)
    code = lax.broadcasted_iota(jnp.int32, (64, n), 0)
    segment = jnp.where(token < R.length, R.seg_row, SEGMENTS)
    used = code <= SEGMENTS
    key_code = jnp.where(used & (code == segment), CODE, 0.0).astype(bf16)
    query_code = jnp.where(used & (code != segment), -CODE, 0.0).astype(bf16)
    R.qcode[...] = jnp.concatenate([jnp.zeros((64, n), bf16), query_code], axis=0).T
    for h in range(HEADS):
        R.kc[128 * h + 64 : 128 * h + 128, :] = key_code
    R.vT[256:320, :] = jnp.zeros((64, n), bf16)


def spans(n):
    out = []
    for i in range(n // TILE):
        lo = max(0, (i * TILE - REACH) // 128 * 128)
        hi = min(n, -(-(i * TILE + TILE + REACH) // 128) * 128)
        out.append((lo, hi - lo))
    return out


def head_tile(pair, h):
    return pair if h % 2 == 0 else pltpu.roll(pair, 64, 1)


def real_rows(R, start, rows):
    return (start + lax.broadcasted_iota(jnp.int32, (rows, 1), 0)) < R.length


def pick_heads(t):
    lane = lanes(TILE, 256) // 64
    o = t[0:TILE]
    for h in range(1, HEADS):
        o = jnp.where(lane == h, t[h * TILE : h * TILE + TILE], o)
    return o


def project(R, l):
    n = R.n
    shift = jnp.concatenate([R.biases[l, 0], jnp.zeros((1, 256), f32), R.biases[l, 1]], axis=1)
    packed = dot(R.x[l], R.wqkv[l]) + shift
    lane = lanes(n)
    q = packed[:, 0:256] * 0.125
    R.qn[l] = q.astype(bf16)
    for h in range(HEADS):
        t = head_tile(q[:, 128 * (h // 2) : 128 * (h // 2) + 128], h)
        R.qh[h] = jnp.where(lane < 64, t, 0.0).astype(bf16) + R.qcode[...]
    k = packed[:, 256:512].astype(bf16)
    R.kn[l] = k
    R.vn[l] = packed[:, 512:768].astype(bf16)
    kT = k.T
    for h in range(HEADS):
        R.kc[128 * h : 128 * h + 64, :] = kT[64 * h : 64 * h + 64]


def attend_tile(R, l, i):
    lo, width = spans(R.n)[i]
    rows, cols = pl.ds(i * TILE, TILE), pl.ds(lo, width)
    real = real_rows(R, i * TILE, TILE)
    for h in range(HEADS):
        s = dot(R.qh[h, rows, :], R.kc[128 * h : 128 * h + 128, cols])
        e = jnp.exp(s - jnp.max(s, axis=1, keepdims=True))
        r = jnp.where(real, 1.0 / jnp.sum(e, axis=1, keepdims=True), 0.0)
        R.P[i][h * TILE : h * TILE + TILE, :] = (e * r).astype(bf16)
    o = pick_heads(dot(R.P[i][...], R.vn[l, cols, :]))
    o = jnp.where(real, o, R.vn[l, rows, :].astype(f32))
    R.octx[l, rows, :] = o


def norm(v):
    c = v - jnp.mean(v, axis=-1, keepdims=True)
    s = lax.rsqrt(jnp.mean(c * c, axis=-1, keepdims=True) + 1e-5)
    return c * s, s


def feed(R, l):
    att = dot(R.octx[l].astype(bf16), R.wout[l]) + R.biases[l, 2]
    n1, s1 = norm(R.x[l].astype(f32) + att)
    hidden = n1 * R.gains[l, 0:1] + R.biases[l, 3]
    low = hidden.astype(bf16)
    u = dot(low, R.wup[l]) + R.upb[l]
    q = (GELU_A * GELU_B) * (u * u)
    w = 0.5 * jnp.tanh(u * (q + GELU_A)) + 0.5
    a = u * w
    act = a.astype(bf16)
    slope = w + a * ((1.0 - w) * (6.0 * q + 2.0 * GELU_A))
    n2, s2 = norm(hidden + (dot(act, R.wdown[l]) + R.biases[l, 4]))
    R.n1[l] = n1
    R.stat[l, :, 4:5] = s1
    R.gp[l] = slope
    R.act[l] = act
    R.n2[l] = n2
    R.stat[l, :, 5:6] = s2
    R.x[l + 1] = (n2 * R.gains[l, 1:2] + R.biases[l, 5]).astype(bf16)


def norm_back(g, n, s, gain):
    gg = g * gain
    return s * (gg - jnp.mean(gg, axis=-1, keepdims=True) - n * jnp.mean(gg * n, axis=-1, keepdims=True))


def put_small(ref, row, v):
    ref[0, row : row + 1, :] = v[:, 0:128]
    ref[1, row : row + 1, :] = v[:, 128:256]


def feed_back(R, l, g):
    n = R.n
    R.woutT[...] = R.wout[l].T
    R.wupT[...] = R.wup[l].T
    R.wdownT[...] = R.wdown[l].T
    R.wqkvT[...] = R.wqkv[l].T
    small = R.small.at[l]
    n2 = R.n2[l]
    d2 = norm_back(g, n2, R.stat[l, :, 5:6], R.gains[l, 1:2])
    put_small(small, 1, column_sum(g * n2))
    put_small(small, 5, column_sum(g))
    dl = d2.astype(bf16)
    R.dlow[...] = dl
    put_small(small, 4, column_sum(d2))
    du = dot(dl, R.wdownT[...]) * R.gp[l]
    up = column_sum(du)
    put_small(small, 6, up[:, 0:256])
    put_small(small, 7, up[:, 256:512])
    du = du.astype(bf16)
    R.dup[...] = du
    dh = d2 + dot(du, R.wupT[...])
    n1 = R.n1[l]
    low = (n1 * R.gains[l, 0:1] + R.biases[l, 3]).astype(bf16)
    d1 = norm_back(dh, n1, R.stat[l, :, 4:5], R.gains[l, 0:1])
    put_small(small, 0, column_sum(dh * n1))
    put_small(small, 3, column_sum(dh))
    put_small(small, 2, column_sum(d1))
    R.d1[...] = d1
    da = d1.astype(bf16)
    R.datt[...] = da
    dcb = dot(da, R.woutT[...]).astype(bf16)
    R.dctx[...] = dcb
    dc = dcb.astype(f32)
    e = dc * R.octx[l]
    lane = lanes(n)
    for h in range(HEADS):
        pair = slice(128 * (h // 2), 128 * (h // 2) + 128)
        R.delta[:, h : h + 1] = jnp.sum(
            jnp.where((lane // 64) == (h % 2), e[:, pair], 0.0), axis=1, keepdims=True
        )
        R.doh[h] = jnp.where(lane < 64, head_tile(dc[:, pair], h), 0.0).astype(bf16)
    R.doT[...] = dcb.T
    R.qT[...] = R.qn[l].T
    R.vT[0:256, :] = R.vn[l].T
    R.grad_a[l, :, 0:256] = dot_tn(R.octx[l].astype(bf16), R.datt[...])
    R.grad_a[l, :, 256:768] = dot_tn(low, R.dup[...])
    R.grad_a[l, :, 768:1280] = dot_tn(R.dlow[...], R.act[l])
    R.dkT[...] = jnp.zeros_like(R.dkT)
    R.dvT[...] = jnp.zeros_like(R.dvT)


def attend_back_tile(R, l, i):
    lo, width = spans(R.n)[i]
    rows, cols = pl.ds(i * TILE, TILE), pl.ds(lo, width)
    for h in range(HEADS):
        head, part = slice(64 * h, 64 * h + 64), slice(h * TILE, h * TILE + TILE)
        p = R.P[i][part, :]
        dp = dot(R.doh[h, rows, :], R.vT[64 * h : 64 * h + 128, cols])
        R.DS[part, 0:width] = (p.astype(f32) * (dp - R.delta[rows, h : h + 1])).astype(bf16)
        R.dvT[head, cols] += dot(R.doT[head, rows], p)
    for h in range(HEADS):
        head, part = slice(64 * h, 64 * h + 64), slice(h * TILE, h * TILE + TILE)
        R.dkT[head, cols] += dot(R.qT[head, rows], R.DS[part, 0:width])
    R.dqkv[rows, 0:256] = (pick_heads(dot(R.DS[:, 0:width], R.kn[l, cols, :])) * 0.125).astype(bf16)


def project_back(R, l):
    real = real_rows(R, 0, R.n)
    dv = R.dvT[...].T + jnp.where(real, 0.0, R.dctx[...].astype(f32))
    R.dqkv[:, 256:512] = R.dkT[...].T.astype(bf16)
    R.dqkv[:, 512:768] = dv.astype(bf16)
    put_small(R.small.at[l], 8, column_sum(R.dqkv[:, 0:256].astype(f32)))
    put_small(R.small.at[l], 9, column_sum(dv))
    d = R.d1[...] + dot(R.dqkv[...], R.wqkvT[...])
    R.d1[...] = d
    R.dinb[l] = d.astype(bf16)


def weight_back(R, l):
    R.grad_b[l] = dot_tn(R.x[l], R.dqkv[...])


class Links:
    def __init__(self, dp, send, recv, local):
        self.sec = lax.axis_index("section")
        self.dp = lax.axis_index("dp")
        self.send, self.recv, self.local_sem = send, recv, local
        self.used = 0
        self.used_local = 0
        self.core = self.dp % 2
        self.chips = min(8, dp // 2)
        self.groups = dp // (2 * self.chips)
        self.chip = (self.dp // 2) % self.chips
        self.pending = []

    def flip(self, index, bit):
        return index + bit - 2 * bit * ((index // bit) % 2)

    def xor(self, index, mask):
        bit = 1
        while bit <= mask:
            if mask & bit:
                index = self.flip(index, bit)
            bit *= 2
        return index

    def section_peer(self):
        return (1 - self.sec, self.dp)

    def core_peer(self):
        return (self.sec, self.flip(self.dp, 1))

    def chip_peer(self, k):
        return (self.sec, self.xor(self.dp, 2 * k))

    def group_peer(self, k):
        return (self.sec, self.xor(self.dp, 2 * self.chips * k))

    def peers(self):
        out = [self.section_peer(), self.core_peer()]
        out += [self.chip_peer(k) for k in range(1, self.chips)]
        out += [self.group_peer(k) for k in range(1, self.groups)]
        return out

    def remote(self, src, dst, peer):
        i = self.used
        self.used += 1
        return pltpu.make_async_remote_copy(
            src, dst, self.send.at[i], self.recv.at[i], device_id=peer, device_id_type=MESH
        )

    def local(self, src, dst):
        i = self.used_local
        self.used_local += 1
        return pltpu.make_async_copy(src, dst, self.local_sem.at[i])


def reduction(K, l, grad, small, R, name):
    get = lambda part: getattr(R, name + "_" + part).at[l]
    r1, s2, r2, acc, r3, done = [get(p) for p in ("r1", "s2", "r2", "acc", "r3", "done")]
    res = getattr(R, "res_" + name)
    c, chip, chips, groups = K.core, K.chip, K.chips, K.groups
    half = grad.shape[0] // 2
    piece = half // chips
    mine = pl.ds(c * half, half)
    other = pl.ds((1 - c) * half, half)
    part = pl.ds(c * half + chip * piece, piece)
    owner = K.sec == l
    core_out = [K.remote(grad.at[other], r1, K.core_peer())]
    scatter = []
    for k in range(1, chips):
        there = K.xor(chip, k)
        scatter.append(K.remote(s2.at[pl.ds(there * piece, piece)], r2.at[k], K.chip_peer(k)))
    across = [K.remote(acc, r3, K.section_peer())]
    gather = [K.remote(done, res.at[part], K.chip_peer(k)) for k in range(1, chips)]
    keep = K.local(done, res.at[part])
    core_back = [K.remote(res.at[mine], res.at[mine], K.core_peer())]
    spread = []
    if groups > 1:
        r4 = get("r4")
        spread = [K.remote(acc, r4.at[k], K.group_peer(k)) for k in range(1, groups)]
    if small is not None:
        q1, q2, t2, qacc, q3, qres = [get(p) for p in ("q1", "q2", "t2", "qacc", "q3", "qres")]
        core_out.append(K.remote(small.at[1 - c], q1, K.core_peer()))
        scatter += [K.remote(q2, t2.at[k], K.chip_peer(k)) for k in range(1, chips)]
        across.append(K.remote(qacc, q3, K.section_peer()))
        core_back.append(K.remote(qres.at[c], qres.at[c], K.core_peer()))
        small_out = K.local(qres, R.small_out)
        if groups > 1:
            q4 = get("q4")
            spread += [K.remote(qacc, q4.at[k], K.group_peer(k)) for k in range(1, groups)]

    def begin():
        for x in core_out:
            x.start()

    def scatter_pieces():
        for x in core_out:
            x.wait()
        total = grad[mine, :] + r1[...]
        grad[mine, :] = total
        s2[...] = total.astype(bf16)
        if small is not None:
            q2[...] = small[c] + q1[...]
        for x in scatter:
            x.start()

    def sum_pieces():
        for x in scatter:
            x.wait()
        total = grad[part, :]
        for k in range(1, chips):
            total = total + r2[k].astype(f32)
        acc[...] = total
        if small is not None:
            little = q2[...]
            for k in range(1, chips):
                little = little + t2[k]
            qacc[...] = little

        @pl.when(jnp.logical_not(owner))
        def _():
            for x in across:
                x.start()
            for x in across:
                x.wait_send()

    def gather_pieces():
        @pl.when(owner)
        def _():
            for x in across:
                x.wait_recv()
            acc[...] += r3[...]
            if small is not None:
                qacc[...] += q3[...]
            for x in spread:
                x.start()
            for x in spread:
                x.wait()
            total = acc[...]
            for k in range(1, groups):
                total = total + r4[k]
            done[...] = total.astype(bf16)
            for x in gather:
                x.start()
            keep.start()
            if small is not None:
                little = qacc[...]
                for k in range(1, groups):
                    little = little + q4[k]
                qres[c] = little
                core_back[1].start()

    def share():
        @pl.when(owner)
        def _():
            for x in gather:
                x.wait()
            keep.wait()
            core_back[0].start()

    def finish():
        @pl.when(owner)
        def _():
            for x in core_back:
                x.wait()
            if small is not None:
                small_out.start()
                small_out.wait()

    return begin, scatter_pieces, sum_pieces, gather_pieces, share, finish


def scratch(n, chips, groups):
    def V(*s):
        return pltpu.VMEM(s[:-1], s[-1])

    out = dict(
        wqkv=V(2, 256, 768, bf16), wout=V(2, 256, 256, bf16), wup=V(2, 256, 512, bf16), wdown=V(2, 512, 256, bf16),
        gains=V(2, 2, 256, f32), biases=V(2, 6, 1, 256, f32), upb=V(2, 1, 512, f32),
        x=V(3, n, 256, bf16), qn=V(2, n, 256, bf16), kn=V(2, n, 256, bf16), vn=V(2, n, 256, bf16),
        octx=V(2, n, 256, f32), DS=V(HEADS * TILE, n, bf16),
        n1=V(2, n, 256, f32), n2=V(2, n, 256, f32), stat=V(2, n, 128, f32),
        gp=V(2, n, 512, f32), act=V(2, n, 512, bf16),
        qcode=V(n, 128, bf16), qh=V(HEADS, n, 128, bf16), kc=V(512, n, bf16), vT=V(320, n, bf16),
        doh=V(HEADS, n, 128, bf16), doT=V(256, n, bf16), qT=V(256, n, bf16), delta=V(n, 128, f32), dctx=V(n, 256, bf16),
        dkT=V(256, n, f32), dvT=V(256, n, f32), dqkv=V(n, 768, bf16),
        d1=V(n, 256, f32),
        woutT=V(256, 256, bf16), wupT=V(512, 256, bf16), wdownT=V(256, 512, bf16), wqkvT=V(768, 256, bf16),
        dinb=V(2, n, 256, bf16),
        small=V(2, 2, 16, 128, f32),
    )
    for name, width in (("a", 1280), ("b", 768)):
        piece = 128 // chips
        out["grad_" + name] = V(2, 256, width, f32)
        out[name + "_r1"] = V(2, 128, width, f32)
        out[name + "_s2"] = V(2, 128, width, bf16)
        out[name + "_r2"] = V(2, chips, piece, width, bf16)
        out[name + "_acc"] = V(2, piece, width, f32)
        out[name + "_r3"] = V(2, piece, width, f32)
        out[name + "_done"] = V(2, piece, width, bf16)
        if groups > 1:
            out[name + "_r4"] = V(2, groups, piece, width, f32)
    for part, lead in (("q1", ()), ("q2", ()), ("t2", (chips,)), ("qacc", ()), ("q3", ()), ("qres", (2,)), ("q4", (groups,))):
        out["b_" + part] = V(2, *lead, 16, 128, f32)
    for i, (_, width) in enumerate(spans(n)):
        out["P%d" % i] = V(HEADS * TILE, width, bf16)
    copies = 32 + 4 * (8 + 3 * chips + 2 * groups)
    out["send"] = pltpu.SemaphoreType.DMA((copies,))
    out["recv"] = pltpu.SemaphoreType.DMA((copies,))
    out["local"] = pltpu.SemaphoreType.DMA((64,))
    return out


INS = ["len_s", "seg_v", "cells", "ograd", "i_wqkv", "i_wout", "i_wup", "i_wdown", "i_gains", "i_biases", "i_upb"]
OUTS = ["layer_out", "din_own", "rdin", "res_a", "res_b", "small_out"]
WEIGHTS = ["wqkv", "wout", "wup", "wdown", "gains", "biases", "upb"]


def body(R, n, dp):
    K = Links(dp, R.send, R.recv, R.local)
    sec, c = K.sec, K.core
    R.n = n
    R.P = [getattr(R, "P%d" % i) for i in range(n // TILE)]
    R.dup = R.DS.at[:, pl.ds(0, 512)]
    R.dlow = R.DS.at[:, pl.ds(512, 256)]
    R.datt = R.DS.at[:, pl.ds(768, 256)]
    R.length = R.len_s[sec]
    R.seg_row = R.seg_v[pl.ds(sec, 1), :]

    barrier = pltpu.get_barrier_semaphore()
    peers = K.peers()
    for peer in peers:
        pl.semaphore_signal(barrier, 1, device_id=peer, device_id_type=MESH)

    take_x = K.local(R.cells.at[sec], R.x.at[0])
    take_g = K.local(R.ograd.at[sec], R.dinb.at[0])
    given = {w: getattr(R, "i_" + w) if w == "biases" else getattr(R, "i_" + w).at[0] for w in WEIGHTS}
    own = [K.local(given[w], getattr(R, w).at[sec]) for w in WEIGHTS]
    take_x.start()
    for x in own:
        x.start()
    take_g.start()

    away, forward_on = {}, {}
    for w in WEIGHTS:
        src, slots = given[w], getattr(R, w)
        if w in ("gains", "biases", "upb"):
            away[w] = K.remote(src, slots.at[sec], K.section_peer())
        else:
            half = src.shape[0] // 2
            rows = pl.ds(c * half, half)
            away[w] = K.remote(src.at[rows], slots.at[sec, rows], K.section_peer())
            theirs = slots.at[1 - sec, rows]
            forward_on[w] = K.remote(theirs, theirs, K.core_peer())

    setup(R)
    pl.semaphore_wait(barrier, len(peers))
    first = ("biases", "wqkv")
    second = ("gains", "upb", "wout", "wup", "wdown")
    for w in first + second:
        away[w].start()
    take_x.wait()
    for x in own:
        x.wait()

    def take_first():
        for w in first:
            away[w].wait()
        forward_on["wqkv"].start()

    @pl.when(sec == 1)
    def _():
        take_first()
        forward_on["wqkv"].wait()

    n_tiles = n // TILE
    x_out = [
        (K.local(R.x.at[l + 1], R.layer_out.at[sec]), K.remote(R.x.at[l + 1], R.layer_out.at[sec], K.section_peer()))
        for l in range(2)
    ]

    def start_out(l, pair):
        pl.when(sec == l)(pair[0].start)
        pl.when(sec != l)(pair[1].start)

    stash = [getattr(R, "stash%d" % i) for i in range(n_tiles)]
    put_away = [K.local(R.P[i], stash[i]) for i in range(n_tiles)]
    bring_back = [K.local(stash[i], R.P[i]) for i in range(n_tiles)]

    def starts(copies):
        for x in copies:
            x.start()

    def waits(copies):
        for x in copies:
            x.wait()

    def forward(l, _):
        def at(layer, *steps):
            @pl.when(l == layer)
            def _():
                for step in steps:
                    step()

        project(R, l)
        at(1, lambda: waits(put_away))
        for i in range(n_tiles):
            attend_tile(R, l, i)
            if i == n_tiles - 2:
                at(
                    0,
                    lambda: starts(put_away[: n_tiles - 1]),
                    lambda: pl.when(sec == 0)(take_first),
                    lambda: waits([away[w] for w in second]),
                    lambda: starts([forward_on[w] for w in ("wout", "wup", "wdown")]),
                )
        at(0, lambda: starts(put_away[n_tiles - 1 :]), lambda: waits([forward_on[w] for w in ("wout", "wup", "wdown")]),
            lambda: pl.when(sec == 0)(forward_on["wqkv"].wait))
        feed(R, l)
        at(0, lambda: start_out(0, x_out[0]))
        at(1, lambda: start_out(1, x_out[1]))
        return 0

    lax.fori_loop(0, 2, forward, 0)

    R.small[...] = jnp.zeros_like(R.small)
    A = [reduction(K, l, R.grad_a.at[l], None, R, "a") for l in range(2)]
    B = [reduction(K, l, R.grad_b.at[l], R.small.at[l], R, "b") for l in range(2)]
    BEGIN, SCATTER, SUM, GATHER, SHARE, FINISH = range(6)

    din_local = [K.local(R.d1, R.din_own) for l in range(2)]
    quarter = n // 4
    din_away = [
        K.remote(R.dinb.at[1], R.rdin, K.section_peer()),
        [K.remote(R.dinb.at[0, pl.ds(i * quarter, quarter)], R.rdin.at[pl.ds(i * quarter, quarter)], K.section_peer()) for i in range(4)],
    ]
    take_g.wait()

    def start_din(l, part=slice(None)):
        @pl.when(sec == l)
        def _():
            din_local[l].start()

        @pl.when(sec != l)
        def _():
            starts([din_away[0]] if l == 1 else din_away[1][:2])

    def backward(j, _):
        l = 1 - j

        def at(turn, *steps):
            @pl.when(j == turn)
            def _():
                for step in steps:
                    step()

        at(1, lambda: pl.when(sec == 1)(din_local[1].wait))
        feed_back(R, l, R.dinb[j].astype(f32))
        at(0, A[1][BEGIN])
        at(1, A[0][BEGIN], B[1][SCATTER], lambda: waits(bring_back))
        for i in range(n_tiles):
            attend_back_tile(R, l, i)
            if i == 1:
                at(0, A[1][SCATTER], lambda: starts(bring_back[:2]))
                at(1, A[0][SCATTER])
            if i == 2:
                at(1, A[1][SUM])
        at(0, lambda: starts(bring_back[2:]))
        at(1, B[1][SUM])
        project_back(R, l)
        at(0, lambda: start_din(1))
        at(1, lambda: start_din(0))
        weight_back(R, l)
        at(0, B[1][BEGIN])
        at(1, B[0][BEGIN])
        return 0

    lax.fori_loop(0, 2, backward, 0)

    B[0][SCATTER]()
    A[0][SUM]()
    A[1][GATHER]()
    B[1][GATHER]()
    A[0][GATHER]()
    B[0][SUM]()
    pl.when(sec == 1)(lambda: starts(din_away[1][2:]))
    A[1][SHARE]()
    B[1][SHARE]()
    B[0][GATHER]()
    A[0][SHARE]()
    A[1][FINISH]()
    B[1][FINISH]()
    B[0][SHARE]()
    A[0][FINISH]()
    B[0][FINISH]()

    for l in range(2):

        @pl.when(sec == l)
        def _():
            x_out[l][0].wait()
            x_out[1 - l][1].wait_send()
            x_out[l][1].wait_recv()
            if l == 0:
                din_local[0].wait()
                din_away[0].wait_send()
                for x in din_away[1]:
                    x.wait_recv()
            else:
                for x in din_away[1]:
                    x.wait_send()
                din_away[0].wait_recv()


def place(n, *refs):
    names = OUTS + ["layer", "grad", "gqkv", "gout", "gup", "gdown", "ggains", "gbias", "gupb", "d", "a", "b", "df", "af", "bf", "tf", "small", "lay", "sem"]
    R = types.SimpleNamespace(**dict(zip(names, refs)))
    sec = lax.axis_index("section")
    used = iter(range(16))
    copy = lambda src, dst: pltpu.make_async_copy(src, dst, R.sem.at[next(used)])
    loads = [copy(R.res_a, R.a), copy(R.res_b, R.b), copy(R.rdin, R.d), copy(R.small_out, R.small)]
    loads += [copy(R.din_own, R.df.at[sec]), copy(R.layer_out, R.lay)]
    for x in loads:
        x.start()

    def row(small, i):
        return jnp.concatenate([small[0, i : i + 1, :], small[1, i : i + 1, :]], axis=1)

    loads[3].wait()
    for i in range(2):
        R.ggains[0, i : i + 1, :] = row(R.small, i)
        R.gupb[0, :, 256 * i : 256 * i + 256] = row(R.small, 6 + i)
        R.gbias[i] = row(R.small, 8 + i)
    for i in range(2, 6):
        R.gbias[i] = row(R.small, i)
    loads[0].wait()
    R.af[...] = R.a[:, 0:768].astype(f32)
    out = [copy(R.af.at[:, pl.ds(0, 256)], R.gout.at[0]), copy(R.af.at[:, pl.ds(256, 512)], R.gup.at[0])]
    R.tf[...] = R.a[:, 768:1280].astype(f32).T
    out += [copy(R.tf, R.gdown.at[0])]
    for x in out:
        x.start()
    loads[1].wait()
    R.bf[...] = R.b[...].astype(f32)
    out += [copy(R.bf, R.gqkv.at[0])]
    out[-1].start()
    loads[2].wait()
    R.df[1 - sec] = R.d[...].astype(f32)
    loads[4].wait()
    out += [copy(R.df, R.grad.at[0])]
    out[-1].start()
    loads[5].wait()
    out += [copy(R.lay, R.layer.at[0])]
    out[-1].start()
    for x in out:
        x.wait()


def kernel_call(dp, n, lengths, segments, cells, ograd, *weights):
    chips = min(8, dp // 2)
    groups = dp // (2 * chips)
    sc = scratch(n, chips, groups)

    def kern(*refs):
        body(types.SimpleNamespace(**dict(zip(names, refs))), n, dp)

    stash = [(HEADS * TILE, width) for _, width in spans(n)]
    names = INS + OUTS + ["stash%d" % i for i in range(len(stash))] + list(sc)
    vmem, smem, anywhere = [pl.BlockSpec(memory_space=m) for m in (pltpu.VMEM, pltpu.SMEM, pl.ANY)]
    shapes = [((2, n, 256), bf16), ((n, 256), f32), ((n, 256), bf16), ((256, 1280), bf16), ((256, 768), bf16)]
    shapes += [((2, 16, 128), f32)] + [(s, bf16) for s in stash]
    parts = pl.pallas_call(
        kern,
        out_shape=[jax.ShapeDtypeStruct(*s) for s in shapes],
        in_specs=[smem, vmem] + [anywhere] * 9,
        out_specs=[anywhere] * (len(OUTS) + len(stash)),
        scratch_shapes=list(sc.values()),
        compiler_params=pltpu.CompilerParams(
            vmem_limit_bytes=62 * 2**20, collective_id=0, has_side_effects=True
        ),
    )(lengths, segments, cells, ograd, *weights)[: len(OUTS)]
    shapes = [((1, 2, n, 256), bf16), ((1, 2, n, 256), f32), ((1, 256, 768), f32), ((1, 256, 256), f32),
              ((1, 256, 512), f32), ((1, 512, 256), f32), ((1, 2, 256), f32), ((6, 1, 256), f32), ((1, 1, 512), f32)]
    return pl.pallas_call(
        lambda *refs: place(n, *refs),
        out_shape=[jax.ShapeDtypeStruct(*s) for s in shapes],
        in_specs=[anywhere] * len(OUTS),
        out_specs=[anywhere] * 6 + [vmem] * 3,
        scratch_shapes=[
            pltpu.VMEM((n, 256), bf16), pltpu.VMEM((256, 1280), bf16), pltpu.VMEM((256, 768), bf16),
            pltpu.VMEM((2, n, 256), f32), pltpu.VMEM((256, 768), f32), pltpu.VMEM((256, 768), f32), pltpu.VMEM((512, 256), f32),
            pltpu.VMEM((2, 16, 128), f32), pltpu.VMEM((2, n, 256), bf16),
            pltpu.SemaphoreType.DMA((16,)),
        ],
        compiler_params=pltpu.CompilerParams(vmem_limit_bytes=62 * 2**20),
    )(*parts)


def solution(mesh):
    dp = mesh.shape["dp"]

    def on_device(cells, ograd, segments, lengths, *weights):
        *matrices, biases, up = weights
        weights = (*matrices, biases.transpose(1, 0, 2), up[:, None, :])
        out = kernel_call(dp, cells.shape[1], lengths, segments, cells, ograd, *weights)
        return (*out[:7], out[7].transpose(1, 0, 2), out[8][:, 0, :])

    w3, w2 = P("section", None, None), P("section", None)
    rows = P("section", "dp", None, None)
    return jax.shard_map(
        on_device,
        mesh=mesh,
        in_specs=(P("dp", None, None), P("dp", None, None), P("dp", None), P("dp"), w3, w3, w3, w3, w3, w3, w2),
        out_specs=(rows, rows, w3, w3, w3, w3, w3, w3, w2),
        check_vma=False,
    )
```

```python
import types

import jax
import jax.numpy as jnp
from jax import lax
from jax.experimental import pallas as pl
from jax.experimental.pallas import tpu as pltpu
from jax.sharding import PartitionSpec as P

MESH = pl.DeviceIdType.MESH
bf16 = jnp.bfloat16
f32 = jnp.float32
HEADS = 4
TILE = 256
REACH = 511
SEGMENTS = 12
CODE = 2.0**50
GELU_A = 0.7978845608028654
GELU_B = 0.044715


def dot(a, b):
    return lax.dot_general(a, b, (((1,), (0,)), ((), ())), preferred_element_type=f32)


def dot_tn(a, b):
    return lax.dot_general(a, b, (((0,), (0,)), ((), ())), preferred_element_type=f32)


def lanes(rows, width=128):
    return lax.broadcasted_iota(jnp.int32, (rows, width), 1)


def column_sum(v):
    return jnp.sum(v, axis=0, keepdims=True)


def setup(R):
    n = R.n
    token = lax.broadcasted_iota(jnp.int32, (64, n), 1)
    code = lax.broadcasted_iota(jnp.int32, (64, n), 0)
    segment = jnp.where(token < R.length, R.seg_row, SEGMENTS)
    used = code <= SEGMENTS
    key_code = jnp.where(used & (code == segment), CODE, 0.0).astype(bf16)
    query_code = jnp.where(used & (code != segment), -CODE, 0.0).astype(bf16)
    R.qcode[...] = jnp.concatenate([jnp.zeros((64, n), bf16), query_code], axis=0).T
    for h in range(HEADS):
        R.kc[128 * h + 64 : 128 * h + 128, :] = key_code
    R.vT[256:320, :] = jnp.zeros((64, n), bf16)


def spans(n):
    out = []
    for i in range(n // TILE):
        lo = max(0, (i * TILE - REACH) // 128 * 128)
        hi = min(n, -(-(i * TILE + TILE + REACH) // 128) * 128)
        out.append((lo, hi - lo))
    return out


def head_tile(pair, h):
    return pair if h % 2 == 0 else pltpu.roll(pair, 64, 1)


def real_rows(R, start, rows):
    return (start + lax.broadcasted_iota(jnp.int32, (rows, 1), 0)) < R.length


def pick_heads(t):
    lane = lanes(TILE, 256) // 64
    o = t[0:TILE]
    for h in range(1, HEADS):
        o = jnp.where(lane == h, t[h * TILE : h * TILE + TILE], o)
    return o


def project(R, l):
    n = R.n
    shift = jnp.concatenate([R.biases[l, 0], jnp.zeros((1, 256), f32), R.biases[l, 1]], axis=1)
    packed = dot(R.x[l], R.wqkv[l]) + shift
    lane = lanes(n)
    q = packed[:, 0:256] * 0.125
    R.qn[l] = q.astype(bf16)
    for h in range(HEADS):
        t = head_tile(q[:, 128 * (h // 2) : 128 * (h // 2) + 128], h)
        R.qh[h] = jnp.where(lane < 64, t, 0.0).astype(bf16) + R.qcode[...]
    k = packed[:, 256:512].astype(bf16)
    R.kn[l] = k
    R.vn[l] = packed[:, 512:768].astype(bf16)
    kT = k.T
    for h in range(HEADS):
        R.kc[128 * h : 128 * h + 64, :] = kT[64 * h : 64 * h + 64]


def attend_tile(R, l, i):
    lo, width = spans(R.n)[i]
    rows, cols = pl.ds(i * TILE, TILE), pl.ds(lo, width)
    real = real_rows(R, i * TILE, TILE)
    for h in range(HEADS):
        s = dot(R.qh[h, rows, :], R.kc[128 * h : 128 * h + 128, cols])
        e = jnp.exp(s - jnp.max(s, axis=1, keepdims=True))
        r = jnp.where(real, 1.0 / jnp.sum(e, axis=1, keepdims=True), 0.0)
        R.P[i][h * TILE : h * TILE + TILE, :] = (e * r).astype(bf16)
    o = pick_heads(dot(R.P[i][...], R.vn[l, cols, :]))
    o = jnp.where(real, o, R.vn[l, rows, :].astype(f32))
    R.octx[l, rows, :] = o


def norm(v):
    c = v - jnp.mean(v, axis=-1, keepdims=True)
    s = lax.rsqrt(jnp.mean(c * c, axis=-1, keepdims=True) + 1e-5)
    return c * s, s


def feed(R, l):
    att = dot(R.octx[l].astype(bf16), R.wout[l]) + R.biases[l, 2]
    n1, s1 = norm(R.x[l].astype(f32) + att)
    hidden = n1 * R.gains[l, 0:1] + R.biases[l, 3]
    low = hidden.astype(bf16)
    u = dot(low, R.wup[l]) + R.upb[l]
    q = (GELU_A * GELU_B) * (u * u)
    w = 0.5 * jnp.tanh(u * (q + GELU_A)) + 0.5
    a = u * w
    act = a.astype(bf16)
    slope = w + a * ((1.0 - w) * (6.0 * q + 2.0 * GELU_A))
    n2, s2 = norm(hidden + (dot(act, R.wdown[l]) + R.biases[l, 4]))
    R.n1[l] = n1
    R.stat[l, :, 4:5] = s1
    R.gp[l] = slope
    R.act[l] = act
    R.n2[l] = n2
    R.stat[l, :, 5:6] = s2
    R.x[l + 1] = (n2 * R.gains[l, 1:2] + R.biases[l, 5]).astype(bf16)


def norm_back(g, n, s, gain):
    gg = g * gain
    return s * (gg - jnp.mean(gg, axis=-1, keepdims=True) - n * jnp.mean(gg * n, axis=-1, keepdims=True))


def put_small(ref, row, v):
    ref[0, row : row + 1, :] = v[:, 0:128]
    ref[1, row : row + 1, :] = v[:, 128:256]


def feed_back(R, l, g):
    n = R.n
    R.woutT[...] = R.wout[l].T
    R.wupT[...] = R.wup[l].T
    R.wdownT[...] = R.wdown[l].T
    R.wqkvT[...] = R.wqkv[l].T
    small = R.small.at[l]
    n2 = R.n2[l]
    d2 = norm_back(g, n2, R.stat[l, :, 5:6], R.gains[l, 1:2])
    put_small(small, 1, column_sum(g * n2))
    put_small(small, 5, column_sum(g))
    dl = d2.astype(bf16)
    R.dlow[...] = dl
    put_small(small, 4, column_sum(d2))
    du = dot(dl, R.wdownT[...]) * R.gp[l]
    up = column_sum(du)
    put_small(small, 6, up[:, 0:256])
    put_small(small, 7, up[:, 256:512])
    du = du.astype(bf16)
    R.dup[...] = du
    dh = d2 + dot(du, R.wupT[...])
    n1 = R.n1[l]
    low = (n1 * R.gains[l, 0:1] + R.biases[l, 3]).astype(bf16)
    d1 = norm_back(dh, n1, R.stat[l, :, 4:5], R.gains[l, 0:1])
    put_small(small, 0, column_sum(dh * n1))
    put_small(small, 3, column_sum(dh))
    put_small(small, 2, column_sum(d1))
    R.d1[...] = d1
    da = d1.astype(bf16)
    R.datt[...] = da
    dcb = dot(da, R.woutT[...]).astype(bf16)
    R.dctx[...] = dcb
    dc = dcb.astype(f32)
    e = dc * R.octx[l]
    lane = lanes(n)
    for h in range(HEADS):
        pair = slice(128 * (h // 2), 128 * (h // 2) + 128)
        R.delta[:, h : h + 1] = jnp.sum(
            jnp.where((lane // 64) == (h % 2), e[:, pair], 0.0), axis=1, keepdims=True
        )
        R.doh[h] = jnp.where(lane < 64, head_tile(dc[:, pair], h), 0.0).astype(bf16)
    R.doT[...] = dcb.T
    R.qT[...] = R.qn[l].T
    R.vT[0:256, :] = R.vn[l].T
    R.grad_a[l, :, 0:256] = dot_tn(R.octx[l].astype(bf16), R.datt[...])
    R.grad_a[l, :, 256:768] = dot_tn(low, R.dup[...])
    R.grad_a[l, :, 768:1280] = dot_tn(R.dlow[...], R.act[l])


def add_columns(ref, head, lo, begun, v):
    old = max(0, min(begun - lo, v.shape[1]))
    if old:
        ref[head, pl.ds(lo, old)] += v[:, 0:old]
    if old < v.shape[1]:
        ref[head, pl.ds(lo + old, v.shape[1] - old)] = v[:, old:]


def attend_back_tile(R, l, i):
    lo, width = spans(R.n)[i]
    begun = max([a + b for a, b in spans(R.n)[:i]], default=0)
    rows, cols = pl.ds(i * TILE, TILE), pl.ds(lo, width)
    for h in range(HEADS):
        head, part = slice(64 * h, 64 * h + 64), slice(h * TILE, h * TILE + TILE)
        p = R.P[i][part, :]
        dp = dot(R.doh[h, rows, :], R.vT[64 * h : 64 * h + 128, cols])
        R.DS[part, 0:width] = (p.astype(f32) * (dp - R.delta[rows, h : h + 1])).astype(bf16)
        add_columns(R.dvT, head, lo, begun, dot(R.doT[head, rows], p))
    for h in range(HEADS):
        head, part = slice(64 * h, 64 * h + 64), slice(h * TILE, h * TILE + TILE)
        add_columns(R.dkT, head, lo, begun, dot(R.qT[head, rows], R.DS[part, 0:width]))
    R.dqkv[rows, 0:256] = (pick_heads(dot(R.DS[:, 0:width], R.kn[l, cols, :])) * 0.125).astype(bf16)


def project_back(R, l):
    real = real_rows(R, 0, R.n)
    dv = R.dvT[...].T + jnp.where(real, 0.0, R.dctx[...].astype(f32))
    R.dqkv[:, 256:512] = R.dkT[...].T.astype(bf16)
    R.dqkv[:, 512:768] = dv.astype(bf16)
    put_small(R.small.at[l], 8, column_sum(R.dqkv[:, 0:256].astype(f32)))
    put_small(R.small.at[l], 9, column_sum(dv))
    d = R.d1[...] + dot(R.dqkv[...], R.wqkvT[...])
    R.d1[...] = d
    R.dinb[l] = d.astype(bf16)


def weight_back(R, l):
    R.grad_b[l] = dot_tn(R.x[l], R.dqkv[...])


class Links:
    def __init__(self, dp, send, recv, local):
        self.sec = lax.axis_index("section")
        self.dp = lax.axis_index("dp")
        self.send, self.recv, self.local_sem = send, recv, local
        self.used = 0
        self.used_local = 0
        self.core = self.dp % 2
        self.chips = min(8, dp // 2)
        self.groups = dp // (2 * self.chips)
        self.chip = (self.dp // 2) % self.chips
        self.pending = []

    def flip(self, index, bit):
        return index + bit - 2 * bit * ((index // bit) % 2)

    def xor(self, index, mask):
        bit = 1
        while bit <= mask:
            if mask & bit:
                index = self.flip(index, bit)
            bit *= 2
        return index

    def section_peer(self):
        return (1 - self.sec, self.dp)

    def core_peer(self):
        return (self.sec, self.flip(self.dp, 1))

    def chip_peer(self, k):
        return (self.sec, self.xor(self.dp, 2 * k))

    def group_peer(self, k):
        return (self.sec, self.xor(self.dp, 2 * self.chips * k))

    def peers(self):
        out = [self.section_peer(), self.core_peer()]
        out += [self.chip_peer(k) for k in range(1, self.chips)]
        out += [self.group_peer(k) for k in range(1, self.groups)]
        return out

    def remote(self, src, dst, peer):
        i = self.used
        self.used += 1
        return pltpu.make_async_remote_copy(
            src, dst, self.send.at[i], self.recv.at[i], device_id=peer, device_id_type=MESH
        )

    def local(self, src, dst):
        i = self.used_local
        self.used_local += 1
        return pltpu.make_async_copy(src, dst, self.local_sem.at[i])


def reduction(K, l, grad, small, R, name, sum_two, give_two):
    get = lambda part: getattr(R, name + "_" + part).at[l]
    r1, s2, ry, r2, acc, r3 = [get(p) for p in ("r1", "s2", "ry", "r2", "acc", "r3")]
    res, out = getattr(R, name + "_res"), getattr(R, "res_" + name)
    c, chip, chips, groups = K.core, K.chip, K.chips, K.groups
    half = grad.shape[0] // 2
    piece = half // chips
    near = half // 2
    line = chips // 2

    def place_of(index):
        return (index % 2) * near + (index // 2) * piece

    start = c * half
    mine, other = pl.ds(start, half), pl.ds((1 - c) * half, half)
    my_near, other_near = (chip % 2) * near, (1 - chip % 2) * near
    part = pl.ds(place_of(chip), piece)
    owner = K.sec == l
    has_small = small is not None
    core_out = [K.remote(grad.at[other], r1, K.core_peer())]
    everyone = range(1, chips)
    ahead = range(2, chips, 2)
    to_near = [K.remote(s2.at[pl.ds(other_near, near)], ry, K.chip_peer(1))] if sum_two else []
    targets = ahead if sum_two else everyone
    scatter = [
        K.remote(s2.at[pl.ds(place_of(K.xor(chip, k)), piece)], r2.at[k], K.chip_peer(k)) for k in targets
    ]
    across = [K.remote(acc, r3, K.section_peer())]
    spread = []
    if groups > 1:
        r4 = get("r4")
        spread = [K.remote(acc, r4.at[k], K.group_peer(k)) for k in range(1, groups)]
    gather = [
        K.remote(res.at[part], res.at[part], K.chip_peer(k)) for k in (ahead if give_two else everyone)
    ]
    rows = pl.ds(my_near, near)
    from_near = [K.remote(res.at[rows], res.at[rows], K.chip_peer(1))] if give_two else []
    core_back = [K.remote(res, out.at[mine], K.core_peer())]
    keep = [K.local(res, out.at[mine])]
    if has_small:
        q1, q2, ty, t2, qacc, q3, qres = [get(p) for p in ("q1", "q2", "ty", "t2", "qacc", "q3", "qres")]
        core_out.append(K.remote(small.at[1 - c], q1, K.core_peer()))
        if sum_two:
            to_near.append(K.remote(q2, ty, K.chip_peer(1)))
        little_src = qacc if sum_two else q2
        scatter += [K.remote(little_src, t2.at[k], K.chip_peer(k)) for k in targets]
        across.append(K.remote(q2, q3, K.section_peer()))
        core_back.append(K.remote(qres, R.small_out.at[c], K.core_peer()))
        keep.append(K.local(qres, R.small_out.at[c]))
        if groups > 1:
            q4 = get("q4")
            spread += [K.remote(qacc, q4.at[k], K.group_peer(k)) for k in range(1, groups)]

    def each(copies, *what):
        for w in what:
            for x in copies:
                getattr(x, w)()

    def begin():
        each(core_out, "start")

    def to_neighbour():
        each(core_out, "wait")
        total = grad[mine, :] + r1[...]
        grad[mine, :] = total
        s2[...] = total.astype(bf16)
        if has_small:
            q2[...] = small[c] + q1[...]
        each(to_near if sum_two else scatter, "start")

    def to_line():
        if sum_two:
            each(to_near, "wait")
            own = pl.ds(start + my_near, near)
            total = grad[own, :] + ry[...].astype(f32)
            grad[own, :] = total
            s2[pl.ds(my_near, near), :] = total.astype(bf16)
            if has_small:
                qacc[...] = q2[...] + ty[...]
            each(scatter, "start")

    def sum_pieces():
        each(scatter, "wait")
        total = grad[pl.ds(start + place_of(chip), piece), :]
        for k in targets:
            total = total + r2[k].astype(f32)
        acc[...] = total
        if has_small:
            little = little_src[...]
            for k in targets:
                little = little + t2[k]
            q2[...] = little
        pl.when(jnp.logical_not(owner))(lambda: each(across, "start", "wait_send"))

    def give_line():
        @pl.when(owner)
        def _():
            each(across, "wait_recv")
            acc[...] += r3[...]
            if has_small:
                qacc[...] = q2[...] + q3[...]
            each(spread, "start", "wait")
            total = acc[...]
            for k in range(1, groups):
                total = total + r4[k]
            res[part, :] = total.astype(bf16)
            each(gather, "start")
            if has_small:
                little = qacc[...]
                for k in range(1, groups):
                    little = little + q4[k]
                qres[...] = little

    def give_neighbour():
        if give_two:

            @pl.when(owner)
            def _():
                each(gather, "wait")
                each(from_near, "start")

    def share():
        @pl.when(owner)
        def _():
            each(from_near if give_two else gather, "wait")
            each(core_back, "start")
            each(keep, "start")

    def finish():
        @pl.when(owner)
        def _():
            each(core_back, "wait")
            each(keep, "wait")

    return begin, to_neighbour, to_line, sum_pieces, give_line, give_neighbour, share, finish


TWO = ((False, False), (False, True), (False, False), (False, True))


def scratch(n, chips, groups):
    def V(*s):
        return pltpu.VMEM(s[:-1], s[-1])

    out = dict(
        wqkv=V(2, 256, 768, bf16), wout=V(2, 256, 256, bf16), wup=V(2, 256, 512, bf16), wdown=V(2, 512, 256, bf16),
        gains=V(2, 2, 256, f32), biases=V(2, 6, 1, 256, f32), upb=V(2, 1, 512, f32),
        x=V(3, n, 256, bf16), qn=V(2, n, 256, bf16), kn=V(2, n, 256, bf16), vn=V(2, n, 256, bf16),
        octx=V(2, n, 256, f32), DS=V(HEADS * TILE, n, bf16),
        n1=V(2, n, 256, f32), n2=V(2, n, 256, f32), stat=V(2, n, 128, f32),
        gp=V(2, n, 512, f32), act=V(2, n, 512, bf16),
        qcode=V(n, 128, bf16), qh=V(HEADS, n, 128, bf16), kc=V(512, n, bf16), vT=V(320, n, bf16),
        doh=V(HEADS, n, 128, bf16), doT=V(256, n, bf16), qT=V(256, n, bf16), delta=V(n, 128, f32), dctx=V(n, 256, bf16),
        dkT=V(256, n, f32), dvT=V(256, n, f32), dqkv=V(n, 768, bf16),
        d1=V(n, 256, f32),
        woutT=V(256, 256, bf16), wupT=V(512, 256, bf16), wdownT=V(256, 512, bf16), wqkvT=V(768, 256, bf16),
        dinb=V(2, n, 256, bf16),
        small=V(2, 2, 16, 128, f32),
    )
    for name, width in (("a", 1280), ("b", 768)):
        piece = 128 // chips
        out["grad_" + name] = V(2, 256, width, f32)
        out[name + "_r1"] = V(2, 128, width, f32)
        out[name + "_s2"] = V(2, 128, width, bf16)
        out[name + "_r2"] = V(2, chips, piece, width, bf16)
        out[name + "_acc"] = V(2, piece, width, f32)
        out[name + "_r3"] = V(2, piece, width, f32)
        out[name + "_ry"] = V(2, 64, width, bf16)
        out[name + "_res"] = V(128, width, bf16)
        if groups > 1:
            out[name + "_r4"] = V(2, groups, piece, width, f32)
    for part, lead in (("q1", ()), ("q2", ()), ("ty", ()), ("t2", (chips,)), ("qacc", ()), ("q3", ()), ("qres", ()), ("q4", (groups,))):
        out["b_" + part] = V(2, *lead, 16, 128, f32)
    for i, (_, width) in enumerate(spans(n)):
        out["P%d" % i] = V(HEADS * TILE, width, bf16)
    copies = 32 + 4 * (8 + 3 * chips + 2 * groups)
    out["send"] = pltpu.SemaphoreType.DMA((copies,))
    out["recv"] = pltpu.SemaphoreType.DMA((copies,))
    out["local"] = pltpu.SemaphoreType.DMA((64,))
    return out


INS = ["len_s", "seg_v", "cells", "ograd", "i_wqkv", "i_wout", "i_wup", "i_wdown", "i_gains", "i_biases", "i_upb"]
OUTS = ["layer_out", "din_own", "rdin", "res_a", "res_b", "small_out"]
WEIGHTS = ["wqkv", "wout", "wup", "wdown", "gains", "biases", "upb"]


def body(R, n, dp):
    K = Links(dp, R.send, R.recv, R.local)
    sec, c = K.sec, K.core
    R.n = n
    R.P = [getattr(R, "P%d" % i) for i in range(n // TILE)]
    R.dup = R.DS.at[:, pl.ds(0, 512)]
    R.dlow = R.DS.at[:, pl.ds(512, 256)]
    R.datt = R.DS.at[:, pl.ds(768, 256)]
    R.length = R.len_s[sec]
    R.seg_row = R.seg_v[pl.ds(sec, 1), :]

    barrier = pltpu.get_barrier_semaphore()
    peers = K.peers()
    for peer in peers:
        pl.semaphore_signal(barrier, 1, device_id=peer, device_id_type=MESH)

    take_x = K.local(R.cells.at[sec], R.x.at[0])
    take_g = K.local(R.ograd.at[sec], R.dinb.at[0])
    given = {w: getattr(R, "i_" + w) if w == "biases" else getattr(R, "i_" + w).at[0] for w in WEIGHTS}
    own = [K.local(given[w], getattr(R, w).at[sec]) for w in WEIGHTS]
    take_x.start()
    for x in own:
        x.start()
    take_g.start()

    away, forward_on = {}, {}
    for w in WEIGHTS:
        src, slots = given[w], getattr(R, w)
        if w in ("gains", "biases", "upb"):
            away[w] = K.remote(src, slots.at[sec], K.section_peer())
        else:
            half = src.shape[0] // 2
            rows = pl.ds(c * half, half)
            away[w] = K.remote(src.at[rows], slots.at[sec, rows], K.section_peer())
            theirs = slots.at[1 - sec, rows]
            forward_on[w] = K.remote(theirs, theirs, K.core_peer())

    setup(R)
    pl.semaphore_wait(barrier, len(peers))
    first = ("biases", "wqkv")
    second = ("gains", "upb", "wout", "wup", "wdown")
    for w in first + second:
        away[w].start()
    take_x.wait()
    for x in own:
        x.wait()

    def take_first():
        for w in first:
            away[w].wait()
        forward_on["wqkv"].start()

    @pl.when(sec == 1)
    def _():
        take_first()
        forward_on["wqkv"].wait()

    n_tiles = n // TILE
    x_out = [
        (K.local(R.x.at[l + 1], R.layer_out.at[sec]), K.remote(R.x.at[l + 1], R.layer_out.at[sec], K.section_peer()))
        for l in range(2)
    ]

    def start_out(l, pair):
        pl.when(sec == l)(pair[0].start)
        pl.when(sec != l)(pair[1].start)

    stash = [getattr(R, "stash%d" % i) for i in range(n_tiles)]
    put_away = [K.local(R.P[i], stash[i]) for i in range(n_tiles)]
    bring_back = [K.local(stash[i], R.P[i]) for i in range(n_tiles)]

    def starts(copies):
        for x in copies:
            x.start()

    def waits(copies):
        for x in copies:
            x.wait()

    def forward(l, _):
        def at(layer, *steps):
            @pl.when(l == layer)
            def _():
                for step in steps:
                    step()

        project(R, l)
        at(1, lambda: waits(put_away))
        for i in range(n_tiles):
            attend_tile(R, l, i)
            if i == n_tiles - 2:
                at(
                    0,
                    lambda: starts(put_away[: n_tiles - 1]),
                    lambda: pl.when(sec == 0)(take_first),
                    lambda: waits([away[w] for w in second]),
                    lambda: starts([forward_on[w] for w in ("wout", "wup", "wdown")]),
                )
        at(0, lambda: starts(put_away[n_tiles - 1 :]), lambda: waits([forward_on[w] for w in ("wout", "wup", "wdown")]),
            lambda: pl.when(sec == 0)(forward_on["wqkv"].wait))
        feed(R, l)
        at(0, lambda: start_out(0, x_out[0]))
        at(1, lambda: start_out(1, x_out[1]))
        return 0

    lax.fori_loop(0, 2, forward, 0)

    R.small[...] = jnp.zeros_like(R.small)
    A = [reduction(K, l, R.grad_a.at[l], None, R, "a", TWO[0][l], TWO[1][l]) for l in range(2)]
    B = [reduction(K, l, R.grad_b.at[l], R.small.at[l], R, "b", TWO[2][l], TWO[3][l]) for l in range(2)]
    BEGIN, NEAR, LINE, SUM, GIVE, GIVE_NEAR, SHARE, FINISH = range(8)

    din_local = [K.local(R.d1, R.din_own) for l in range(2)]
    quarter = n // 4
    din_away = [
        K.remote(R.dinb.at[1], R.rdin, K.section_peer()),
        [K.remote(R.dinb.at[0, pl.ds(i * quarter, quarter)], R.rdin.at[pl.ds(i * quarter, quarter)], K.section_peer()) for i in range(4)],
    ]
    take_g.wait()

    def start_din(l, part=slice(None)):
        @pl.when(sec == l)
        def _():
            din_local[l].start()

        @pl.when(sec != l)
        def _():
            starts([din_away[0]] if l == 1 else din_away[1][:2])

    def backward(j, _):
        l = 1 - j

        def at(turn, *steps):
            @pl.when(j == turn)
            def _():
                for step in steps:
                    step()

        at(1, lambda: pl.when(sec == 1)(din_local[1].wait))
        feed_back(R, l, R.dinb[j].astype(f32))
        at(0, A[1][BEGIN])
        at(1, A[0][BEGIN], A[1][LINE], B[1][NEAR], lambda: waits(bring_back))
        for i in range(n_tiles):
            attend_back_tile(R, l, i)
            if i == 1:
                at(0, A[1][NEAR], lambda: starts(bring_back[:2]))
                at(1, A[0][NEAR])
            if i == 2:
                at(1, B[1][LINE])
        at(0, lambda: starts(bring_back[2:]))
        project_back(R, l)
        at(0, lambda: start_din(1))
        at(1, lambda: start_din(0))
        weight_back(R, l)
        at(0, B[1][BEGIN])
        at(1, B[0][BEGIN])
        return 0

    lax.fori_loop(0, 2, backward, 0)

    A[0][LINE]()
    B[0][NEAR]()
    A[0][SUM]()
    A[1][SUM]()
    B[1][SUM]()
    B[0][LINE]()
    A[0][GIVE]()
    B[0][SUM]()
    pl.when(sec == 1)(lambda: starts(din_away[1][2:]))
    A[1][GIVE]()
    B[1][GIVE]()
    B[0][GIVE]()
    A[0][GIVE_NEAR]()
    A[1][GIVE_NEAR]()
    B[1][GIVE_NEAR]()
    B[0][GIVE_NEAR]()
    A[0][SHARE]()
    A[1][SHARE]()
    B[1][SHARE]()
    B[0][SHARE]()
    A[1][FINISH]()
    B[1][FINISH]()
    A[0][FINISH]()
    B[0][FINISH]()

    for l in range(2):

        @pl.when(sec == l)
        def _():
            x_out[l][0].wait()
            x_out[1 - l][1].wait_send()
            x_out[l][1].wait_recv()
            if l == 0:
                din_local[0].wait()
                din_away[0].wait_send()
                for x in din_away[1]:
                    x.wait_recv()
            else:
                for x in din_away[1]:
                    x.wait_send()
                din_away[0].wait_recv()


def place(n, *refs):
    names = OUTS + ["layer", "grad", "gqkv", "gout", "gup", "gdown", "ggains", "gbias", "gupb", "d", "a", "b", "df", "af", "bf", "tf", "small", "lay", "sem"]
    R = types.SimpleNamespace(**dict(zip(names, refs)))
    sec = lax.axis_index("section")
    used = iter(range(16))
    copy = lambda src, dst: pltpu.make_async_copy(src, dst, R.sem.at[next(used)])
    loads = [copy(R.res_a, R.a), copy(R.res_b, R.b), copy(R.rdin, R.d), copy(R.small_out, R.small)]
    loads += [copy(R.din_own, R.df.at[sec]), copy(R.layer_out, R.lay)]
    for x in loads:
        x.start()

    def row(small, i):
        return jnp.concatenate([small[0, i : i + 1, :], small[1, i : i + 1, :]], axis=1)

    loads[3].wait()
    for i in range(2):
        R.ggains[0, i : i + 1, :] = row(R.small, i)
        R.gupb[0, :, 256 * i : 256 * i + 256] = row(R.small, 6 + i)
        R.gbias[i] = row(R.small, 8 + i)
    for i in range(2, 6):
        R.gbias[i] = row(R.small, i)
    loads[0].wait()
    R.af[...] = R.a[:, 0:768].astype(f32)
    out = [copy(R.af.at[:, pl.ds(0, 256)], R.gout.at[0]), copy(R.af.at[:, pl.ds(256, 512)], R.gup.at[0])]
    R.tf[...] = R.a[:, 768:1280].astype(f32).T
    out += [copy(R.tf, R.gdown.at[0])]
    for x in out:
        x.start()
    loads[1].wait()
    R.bf[...] = R.b[...].astype(f32)
    out += [copy(R.bf, R.gqkv.at[0])]
    out[-1].start()
    loads[2].wait()
    R.df[1 - sec] = R.d[...].astype(f32)
    loads[4].wait()
    out += [copy(R.df, R.grad.at[0])]
    out[-1].start()
    loads[5].wait()
    out += [copy(R.lay, R.layer.at[0])]
    out[-1].start()
    for x in out:
        x.wait()


def kernel_call(dp, n, lengths, segments, cells, ograd, *weights):
    chips = min(8, dp // 2)
    groups = dp // (2 * chips)
    sc = scratch(n, chips, groups)

    def kern(*refs):
        body(types.SimpleNamespace(**dict(zip(names, refs))), n, dp)

    stash = [(HEADS * TILE, width) for _, width in spans(n)]
    names = INS + OUTS + ["stash%d" % i for i in range(len(stash))] + list(sc)
    vmem, smem, anywhere = [pl.BlockSpec(memory_space=m) for m in (pltpu.VMEM, pltpu.SMEM, pl.ANY)]
    shapes = [((2, n, 256), bf16), ((n, 256), f32), ((n, 256), bf16), ((256, 1280), bf16), ((256, 768), bf16)]
    shapes += [((2, 16, 128), f32)] + [(s, bf16) for s in stash]
    parts = pl.pallas_call(
        kern,
        out_shape=[jax.ShapeDtypeStruct(*s) for s in shapes],
        in_specs=[smem, vmem] + [anywhere] * 9,
        out_specs=[anywhere] * (len(OUTS) + len(stash)),
        scratch_shapes=list(sc.values()),
        compiler_params=pltpu.CompilerParams(
            vmem_limit_bytes=62 * 2**20, collective_id=0, has_side_effects=True
        ),
    )(lengths, segments, cells, ograd, *weights)[: len(OUTS)]
    shapes = [((1, 2, n, 256), bf16), ((1, 2, n, 256), f32), ((1, 256, 768), f32), ((1, 256, 256), f32),
              ((1, 256, 512), f32), ((1, 512, 256), f32), ((1, 2, 256), f32), ((6, 1, 256), f32), ((1, 1, 512), f32)]
    return pl.pallas_call(
        lambda *refs: place(n, *refs),
        out_shape=[jax.ShapeDtypeStruct(*s) for s in shapes],
        in_specs=[anywhere] * len(OUTS),
        out_specs=[anywhere] * 6 + [vmem] * 3,
        scratch_shapes=[
            pltpu.VMEM((n, 256), bf16), pltpu.VMEM((256, 1280), bf16), pltpu.VMEM((256, 768), bf16),
            pltpu.VMEM((2, n, 256), f32), pltpu.VMEM((256, 768), f32), pltpu.VMEM((256, 768), f32), pltpu.VMEM((512, 256), f32),
            pltpu.VMEM((2, 16, 128), f32), pltpu.VMEM((2, n, 256), bf16),
            pltpu.SemaphoreType.DMA((16,)),
        ],
        compiler_params=pltpu.CompilerParams(vmem_limit_bytes=62 * 2**20),
    )(*parts)


def solution(mesh):
    dp = mesh.shape["dp"]

    def on_device(cells, ograd, segments, lengths, *weights):
        *matrices, biases, up = weights
        weights = (*matrices, biases.transpose(1, 0, 2), up[:, None, :])
        out = kernel_call(dp, cells.shape[1], lengths, segments, cells, ograd, *weights)
        return (*out[:7], out[7].transpose(1, 0, 2), out[8][:, 0, :])

    w3, w2 = P("section", None, None), P("section", None)
    rows = P("section", "dp", None, None)
    return jax.shard_map(
        on_device,
        mesh=mesh,
        in_specs=(P("dp", None, None), P("dp", None, None), P("dp", None), P("dp"), w3, w3, w3, w3, w3, w3, w2),
        out_specs=(rows, rows, w3, w3, w3, w3, w3, w3, w2),
        check_vma=False,
    )
```

```python
import types

import jax
import jax.numpy as jnp
from jax import lax
from jax.experimental import pallas as pl
from jax.experimental.pallas import tpu as pltpu
from jax.sharding import PartitionSpec as P

MESH = pl.DeviceIdType.MESH
bf16 = jnp.bfloat16
f32 = jnp.float32
HEADS = 4
TILE = 256
REACH = 511
SEGMENTS = 12
CODE = 2.0**50
GELU_A = 0.7978845608028654
GELU_B = 0.044715


def dot(a, b):
    return lax.dot_general(a, b, (((1,), (0,)), ((), ())), preferred_element_type=f32)


def dot_tn(a, b):
    return lax.dot_general(a, b, (((0,), (0,)), ((), ())), preferred_element_type=f32)


def lanes(rows, width=128):
    return lax.broadcasted_iota(jnp.int32, (rows, width), 1)


def column_sum(v):
    return jnp.sum(v, axis=0, keepdims=True)


def setup(R):
    n = R.n
    token = lax.broadcasted_iota(jnp.int32, (64, n), 1)
    code = lax.broadcasted_iota(jnp.int32, (64, n), 0)
    segment = jnp.where(token < R.length, R.seg_row, SEGMENTS)
    used = code <= SEGMENTS
    key_code = jnp.where(used & (code == segment), CODE, 0.0).astype(bf16)
    query_code = jnp.where(used & (code != segment), -CODE, 0.0).astype(bf16)
    R.qcode[...] = jnp.concatenate([jnp.zeros((64, n), bf16), query_code], axis=0).T
    for h in range(HEADS):
        R.kc[128 * h + 64 : 128 * h + 128, :] = key_code
    R.vT[256:320, :] = jnp.zeros((64, n), bf16)


def spans(n):
    out = []
    for i in range(n // TILE):
        lo = max(0, (i * TILE - REACH) // 128 * 128)
        hi = min(n, -(-(i * TILE + TILE + REACH) // 128) * 128)
        out.append((lo, hi - lo))
    return out


def head_tile(pair, h):
    return pair if h % 2 == 0 else pltpu.roll(pair, 64, 1)


def real_rows(R, start, rows):
    return (start + lax.broadcasted_iota(jnp.int32, (rows, 1), 0)) < R.length


def pick_heads(t):
    lane = lanes(TILE, 256) // 64
    o = t[0:TILE]
    for h in range(1, HEADS):
        o = jnp.where(lane == h, t[h * TILE : h * TILE + TILE], o)
    return o


def project(R, l):
    n = R.n
    shift = jnp.concatenate([R.biases[l, 0], jnp.zeros((1, 256), f32), R.biases[l, 1]], axis=1)
    packed = dot(R.x[l], R.wqkv[l]) + shift
    lane = lanes(n)
    q = packed[:, 0:256] * 0.125
    R.qn[l] = q.astype(bf16)
    for h in range(HEADS):
        t = head_tile(q[:, 128 * (h // 2) : 128 * (h // 2) + 128], h)
        R.qh[h] = jnp.where(lane < 64, t, 0.0).astype(bf16) + R.qcode[...]
    k = packed[:, 256:512].astype(bf16)
    R.kn[l] = k
    R.vn[l] = packed[:, 512:768].astype(bf16)
    kT = k.T
    for h in range(HEADS):
        R.kc[128 * h : 128 * h + 64, :] = kT[64 * h : 64 * h + 64]


def attend_tile(R, l, i):
    lo, width = spans(R.n)[i]
    rows, cols = pl.ds(i * TILE, TILE), pl.ds(lo, width)
    real = real_rows(R, i * TILE, TILE)
    for h in range(HEADS):
        s = dot(R.qh[h, rows, :], R.kc[128 * h : 128 * h + 128, cols])
        e = jnp.exp(s - jnp.max(s, axis=1, keepdims=True))
        r = jnp.where(real, 1.0 / jnp.sum(e, axis=1, keepdims=True), 0.0)
        R.P[i][h * TILE : h * TILE + TILE, :] = (e * r).astype(bf16)
    o = pick_heads(dot(R.P[i][...], R.vn[l, cols, :]))
    o = jnp.where(real, o, R.vn[l, rows, :].astype(f32))
    R.octx[l, rows, :] = o


def norm(v):
    c = v - jnp.mean(v, axis=-1, keepdims=True)
    s = lax.rsqrt(jnp.mean(c * c, axis=-1, keepdims=True) + 1e-5)
    return c * s, s


def feed(R, l):
    att = dot(R.octx[l].astype(bf16), R.wout[l]) + R.biases[l, 2]
    n1, s1 = norm(R.x[l].astype(f32) + att)
    hidden = n1 * R.gains[l, 0:1] + R.biases[l, 3]
    low = hidden.astype(bf16)
    u = dot(low, R.wup[l]) + R.upb[l]
    q = (GELU_A * GELU_B) * (u * u)
    w = 0.5 * jnp.tanh(u * (q + GELU_A)) + 0.5
    a = u * w
    act = a.astype(bf16)
    slope = w + a * ((1.0 - w) * (6.0 * q + 2.0 * GELU_A))
    n2, s2 = norm(hidden + (dot(act, R.wdown[l]) + R.biases[l, 4]))
    R.n1[l] = n1
    R.stat[l, :, 4:5] = s1
    R.gp[l] = slope
    R.act[l] = act
    R.n2[l] = n2
    R.stat[l, :, 5:6] = s2
    R.x[l + 1] = (n2 * R.gains[l, 1:2] + R.biases[l, 5]).astype(bf16)


def norm_back(g, n, s, gain):
    gg = g * gain
    return s * (gg - jnp.mean(gg, axis=-1, keepdims=True) - n * jnp.mean(gg * n, axis=-1, keepdims=True))


def put_small(ref, row, v):
    ref[0, row : row + 1, :] = v[:, 0:128]
    ref[1, row : row + 1, :] = v[:, 128:256]


def feed_back(R, l, g):
    n = R.n
    R.woutT[...] = R.wout[l].T
    R.wupT[...] = R.wup[l].T
    R.wdownT[...] = R.wdown[l].T
    R.wqkvT[...] = R.wqkv[l].T
    small = R.small.at[l]
    n2 = R.n2[l]
    d2 = norm_back(g, n2, R.stat[l, :, 5:6], R.gains[l, 1:2])
    put_small(small, 1, column_sum(g * n2))
    put_small(small, 5, column_sum(g))
    dl = d2.astype(bf16)
    R.dlow[...] = dl
    put_small(small, 4, column_sum(d2))
    du = dot(dl, R.wdownT[...]) * R.gp[l]
    up = column_sum(du)
    put_small(small, 6, up[:, 0:256])
    put_small(small, 7, up[:, 256:512])
    du = du.astype(bf16)
    R.dup[...] = du
    dh = d2 + dot(du, R.wupT[...])
    n1 = R.n1[l]
    low = (n1 * R.gains[l, 0:1] + R.biases[l, 3]).astype(bf16)
    d1 = norm_back(dh, n1, R.stat[l, :, 4:5], R.gains[l, 0:1])
    put_small(small, 0, column_sum(dh * n1))
    put_small(small, 3, column_sum(dh))
    put_small(small, 2, column_sum(d1))
    R.d1[...] = d1
    da = d1.astype(bf16)
    R.datt[...] = da
    dcb = dot(da, R.woutT[...]).astype(bf16)
    R.dctx[...] = dcb
    R.grad_a[l, :, 0:256] = dot_tn(R.octx[l].astype(bf16), R.datt[...])
    R.grad_a[l, :, 256:768] = dot_tn(low, R.dup[...])
    R.grad_a[l, :, 768:1280] = dot_tn(R.dlow[...], R.act[l])


def attend_prepare(R, l):
    n = R.n
    dcb = R.dctx[...]
    dc = dcb.astype(f32)
    e = dc * R.octx[l]
    lane = lanes(n)
    for h in range(HEADS):
        pair = slice(128 * (h // 2), 128 * (h // 2) + 128)
        R.delta[:, h : h + 1] = jnp.sum(
            jnp.where((lane // 64) == (h % 2), e[:, pair], 0.0), axis=1, keepdims=True
        )
        R.doh[h] = jnp.where(lane < 64, head_tile(dc[:, pair], h), 0.0).astype(bf16)
    R.doT[...] = dcb.T
    R.qT[...] = R.qn[l].T
    R.vT[0:256, :] = R.vn[l].T


def add_columns(ref, head, lo, begun, v):
    old = max(0, min(begun - lo, v.shape[1]))
    if old:
        ref[head, pl.ds(lo, old)] += v[:, 0:old]
    if old < v.shape[1]:
        ref[head, pl.ds(lo + old, v.shape[1] - old)] = v[:, old:]


def attend_back_tile(R, l, i):
    lo, width = spans(R.n)[i]
    begun = max([a + b for a, b in spans(R.n)[:i]], default=0)
    rows, cols = pl.ds(i * TILE, TILE), pl.ds(lo, width)
    for h in range(HEADS):
        head, part = slice(64 * h, 64 * h + 64), slice(h * TILE, h * TILE + TILE)
        p = R.P[i][part, :]
        dp = dot(R.doh[h, rows, :], R.vT[64 * h : 64 * h + 128, cols])
        R.DS[part, 0:width] = (p.astype(f32) * (dp - R.delta[rows, h : h + 1])).astype(bf16)
        add_columns(R.dvT, head, lo, begun, dot(R.doT[head, rows], p))
    for h in range(HEADS):
        head, part = slice(64 * h, 64 * h + 64), slice(h * TILE, h * TILE + TILE)
        add_columns(R.dkT, head, lo, begun, dot(R.qT[head, rows], R.DS[part, 0:width]))
    R.dqkv[rows, 0:256] = (pick_heads(dot(R.DS[:, 0:width], R.kn[l, cols, :])) * 0.125).astype(bf16)


def project_back(R, l):
    real = real_rows(R, 0, R.n)
    dv = R.dvT[...].T + jnp.where(real, 0.0, R.dctx[...].astype(f32))
    R.dqkv[:, 256:512] = R.dkT[...].T.astype(bf16)
    R.dqkv[:, 512:768] = dv.astype(bf16)
    put_small(R.small.at[l], 8, column_sum(R.dqkv[:, 0:256].astype(f32)))
    put_small(R.small.at[l], 9, column_sum(dv))
    d = R.d1[...] + dot(R.dqkv[...], R.wqkvT[...])
    R.d1[...] = d
    R.dinb[l] = d.astype(bf16)


def weight_back(R, l):
    R.grad_b[l] = dot_tn(R.x[l], R.dqkv[...])


class Links:
    def __init__(self, dp, send, recv, local):
        self.sec = lax.axis_index("section")
        self.dp = lax.axis_index("dp")
        self.send, self.recv, self.local_sem = send, recv, local
        self.used = 0
        self.used_local = 0
        self.core = self.dp % 2
        self.chips = min(8, dp // 2)
        self.groups = dp // (2 * self.chips)
        self.chip = (self.dp // 2) % self.chips
        self.pending = []

    def flip(self, index, bit):
        return index + bit - 2 * bit * ((index // bit) % 2)

    def xor(self, index, mask):
        bit = 1
        while bit <= mask:
            if mask & bit:
                index = self.flip(index, bit)
            bit *= 2
        return index

    def section_peer(self):
        return (1 - self.sec, self.dp)

    def core_peer(self):
        return (self.sec, self.flip(self.dp, 1))

    def chip_peer(self, k):
        return (self.sec, self.xor(self.dp, 2 * k))

    def group_peer(self, k):
        return (self.sec, self.xor(self.dp, 2 * self.chips * k))

    def peers(self):
        out = [self.section_peer(), self.core_peer()]
        out += [self.chip_peer(k) for k in range(1, self.chips)]
        out += [self.group_peer(k) for k in range(1, self.groups)]
        return out

    def remote(self, src, dst, peer):
        i = self.used
        self.used += 1
        return pltpu.make_async_remote_copy(
            src, dst, self.send.at[i], self.recv.at[i], device_id=peer, device_id_type=MESH
        )

    def local(self, src, dst):
        i = self.used_local
        self.used_local += 1
        return pltpu.make_async_copy(src, dst, self.local_sem.at[i])


def reduction(K, l, grad, small, R, name, sum_two, give_two):
    get = lambda part: getattr(R, name + "_" + part).at[l]
    r1, s2, ry, r2, acc, r3 = [get(p) for p in ("r1", "s2", "ry", "r2", "acc", "r3")]
    res, out = getattr(R, name + "_res"), getattr(R, "res_" + name)
    c, chip, chips, groups = K.core, K.chip, K.chips, K.groups
    half = grad.shape[0] // 2
    piece = half // chips
    near = half // 2
    line = chips // 2

    def place_of(index):
        return (index % 2) * near + (index // 2) * piece

    start = c * half
    mine, other = pl.ds(start, half), pl.ds((1 - c) * half, half)
    my_near, other_near = (chip % 2) * near, (1 - chip % 2) * near
    part = pl.ds(place_of(chip), piece)
    owner = K.sec == l
    has_small = small is not None
    core_out = [K.remote(grad.at[other], r1, K.core_peer())]
    everyone = range(1, chips)
    ahead = range(2, chips, 2)
    to_near = [K.remote(s2.at[pl.ds(other_near, near)], ry, K.chip_peer(1))] if sum_two else []
    targets = ahead if sum_two else everyone
    scatter = [
        K.remote(s2.at[pl.ds(place_of(K.xor(chip, k)), piece)], r2.at[k], K.chip_peer(k)) for k in targets
    ]
    across = [K.remote(acc, r3, K.section_peer())]
    spread = []
    if groups > 1:
        r4 = get("r4")
        spread = [K.remote(acc, r4.at[k], K.group_peer(k)) for k in range(1, groups)]
    gather = [
        K.remote(res.at[part], res.at[part], K.chip_peer(k)) for k in (ahead if give_two else everyone)
    ]
    rows = pl.ds(my_near, near)
    from_near = [K.remote(res.at[rows], res.at[rows], K.chip_peer(1))] if give_two else []
    core_back = [K.remote(res, out.at[mine], K.core_peer())]
    keep = [K.local(res, out.at[mine])]
    if has_small:
        q1, q2, ty, t2, qacc, q3, qres = [get(p) for p in ("q1", "q2", "ty", "t2", "qacc", "q3", "qres")]
        core_out.append(K.remote(small.at[1 - c], q1, K.core_peer()))
        if sum_two:
            to_near.append(K.remote(q2, ty, K.chip_peer(1)))
        little_src = qacc if sum_two else q2
        scatter += [K.remote(little_src, t2.at[k], K.chip_peer(k)) for k in targets]
        across.append(K.remote(q2, q3, K.section_peer()))
        core_back.append(K.remote(qres, R.small_out.at[c], K.core_peer()))
        keep.append(K.local(qres, R.small_out.at[c]))
        if groups > 1:
            q4 = get("q4")
            spread += [K.remote(qacc, q4.at[k], K.group_peer(k)) for k in range(1, groups)]

    def each(copies, *what):
        for w in what:
            for x in copies:
                getattr(x, w)()

    def begin():
        each(core_out, "start")

    def to_neighbour():
        each(core_out, "wait")
        total = grad[mine, :] + r1[...]
        grad[mine, :] = total
        s2[...] = total.astype(bf16)
        if has_small:
            q2[...] = small[c] + q1[...]
        each(to_near if sum_two else scatter, "start")

    def to_line():
        if sum_two:
            each(to_near, "wait")
            own = pl.ds(start + my_near, near)
            total = grad[own, :] + ry[...].astype(f32)
            grad[own, :] = total
            s2[pl.ds(my_near, near), :] = total.astype(bf16)
            if has_small:
                qacc[...] = q2[...] + ty[...]
            each(scatter, "start")

    def sum_pieces():
        each(scatter, "wait")
        total = grad[pl.ds(start + place_of(chip), piece), :]
        for k in targets:
            total = total + r2[k].astype(f32)
        acc[...] = total
        if has_small:
            little = little_src[...]
            for k in targets:
                little = little + t2[k]
            q2[...] = little
        pl.when(jnp.logical_not(owner))(lambda: each(across, "start"))

    def give_line():
        @pl.when(owner)
        def _():
            each(across, "wait_recv")
            acc[...] += r3[...]
            if has_small:
                qacc[...] = q2[...] + q3[...]
            each(spread, "start", "wait")
            total = acc[...]
            for k in range(1, groups):
                total = total + r4[k]
            res[part, :] = total.astype(bf16)
            each(gather, "start")
            if has_small:
                little = qacc[...]
                for k in range(1, groups):
                    little = little + q4[k]
                qres[...] = little

    def give_neighbour():
        if give_two:

            @pl.when(owner)
            def _():
                each(gather, "wait")
                each(from_near, "start")

    def share():
        @pl.when(owner)
        def _():
            each(from_near if give_two else gather, "wait")
            each(core_back, "start")
            each(keep, "start")

    def finish():
        @pl.when(owner)
        def _():
            each(core_back, "wait")
            each(keep, "wait")

        pl.when(jnp.logical_not(owner))(lambda: each(across, "wait_send"))

    return begin, to_neighbour, to_line, sum_pieces, give_line, give_neighbour, share, finish


TWO = ((False, False), (False, True), (False, False), (False, True))


def scratch(n, chips, groups):
    def V(*s):
        return pltpu.VMEM(s[:-1], s[-1])

    out = dict(
        wqkv=V(2, 256, 768, bf16), wout=V(2, 256, 256, bf16), wup=V(2, 256, 512, bf16), wdown=V(2, 512, 256, bf16),
        gains=V(2, 2, 256, f32), biases=V(2, 6, 1, 256, f32), upb=V(2, 1, 512, f32),
        x=V(3, n, 256, bf16), qn=V(2, n, 256, bf16), kn=V(2, n, 256, bf16), vn=V(2, n, 256, bf16),
        octx=V(2, n, 256, f32), DS=V(HEADS * TILE, n, bf16),
        n1=V(2, n, 256, f32), n2=V(2, n, 256, f32), stat=V(2, n, 128, f32),
        gp=V(2, n, 512, f32), act=V(2, n, 512, bf16),
        qcode=V(n, 128, bf16), qh=V(HEADS, n, 128, bf16), kc=V(512, n, bf16), vT=V(320, n, bf16),
        doh=V(HEADS, n, 128, bf16), doT=V(256, n, bf16), qT=V(256, n, bf16), delta=V(n, 128, f32), dctx=V(n, 256, bf16),
        dkT=V(256, n, f32), dvT=V(256, n, f32), dqkv=V(n, 768, bf16),
        d1=V(n, 256, f32),
        woutT=V(256, 256, bf16), wupT=V(512, 256, bf16), wdownT=V(256, 512, bf16), wqkvT=V(768, 256, bf16),
        dinb=V(2, n, 256, bf16),
        small=V(2, 2, 16, 128, f32),
    )
    for name, width in (("a", 1280), ("b", 768)):
        piece = 128 // chips
        out["grad_" + name] = V(2, 256, width, f32)
        out[name + "_r1"] = V(2, 128, width, f32)
        out[name + "_s2"] = V(2, 128, width, bf16)
        out[name + "_r2"] = V(2, chips, piece, width, bf16)
        out[name + "_acc"] = V(2, piece, width, f32)
        out[name + "_r3"] = V(2, piece, width, f32)
        out[name + "_ry"] = V(2, 64, width, bf16)
        out[name + "_res"] = V(128, width, bf16)
        if groups > 1:
            out[name + "_r4"] = V(2, groups, piece, width, f32)
    for part, lead in (("q1", ()), ("q2", ()), ("ty", ()), ("t2", (chips,)), ("qacc", ()), ("q3", ()), ("qres", ()), ("q4", (groups,))):
        out["b_" + part] = V(2, *lead, 16, 128, f32)
    for i, (_, width) in enumerate(spans(n)):
        out["P%d" % i] = V(HEADS * TILE, width, bf16)
    copies = 32 + 4 * (8 + 3 * chips + 2 * groups)
    out["send"] = pltpu.SemaphoreType.DMA((copies,))
    out["recv"] = pltpu.SemaphoreType.DMA((copies,))
    out["local"] = pltpu.SemaphoreType.DMA((64,))
    return out


INS = ["len_s", "seg_v", "cells", "ograd", "i_wqkv", "i_wout", "i_wup", "i_wdown", "i_gains", "i_biases", "i_upb"]
OUTS = ["layer_out", "din_own", "rdin", "res_a", "res_b", "small_out"]
WEIGHTS = ["wqkv", "wout", "wup", "wdown", "gains", "biases", "upb"]


def body(R, n, dp):
    K = Links(dp, R.send, R.recv, R.local)
    sec, c = K.sec, K.core
    R.n = n
    R.P = [getattr(R, "P%d" % i) for i in range(n // TILE)]
    R.dup = R.DS.at[:, pl.ds(0, 512)]
    R.dlow = R.DS.at[:, pl.ds(512, 256)]
    R.datt = R.DS.at[:, pl.ds(768, 256)]
    R.length = R.len_s[sec]
    R.seg_row = R.seg_v[pl.ds(sec, 1), :]

    barrier = pltpu.get_barrier_semaphore()
    peers = K.peers()[::-1]
    for peer in peers:
        pl.semaphore_signal(barrier, 1, device_id=peer, device_id_type=MESH)

    take_x = K.local(R.cells.at[sec], R.x.at[0])
    take_g = K.local(R.ograd.at[sec], R.dinb.at[0])
    given = {w: getattr(R, "i_" + w) if w == "biases" else getattr(R, "i_" + w).at[0] for w in WEIGHTS}
    own = [K.local(given[w], getattr(R, w).at[sec]) for w in WEIGHTS]
    take_x.start()
    for x in own:
        x.start()
    take_g.start()

    away, forward_on = {}, {}
    for w in WEIGHTS:
        src, slots = given[w], getattr(R, w)
        if w in ("gains", "biases", "upb"):
            away[w] = K.remote(src, slots.at[sec], K.section_peer())
        else:
            half = src.shape[0] // 2
            rows = pl.ds(c * half, half)
            away[w] = K.remote(src.at[rows], slots.at[sec, rows], K.section_peer())
            theirs = slots.at[1 - sec, rows]
            forward_on[w] = K.remote(theirs, theirs, K.core_peer())

    setup(R)
    pl.semaphore_wait(barrier, len(peers))
    first = ("biases", "wqkv")
    second = ("gains", "upb", "wout", "wup", "wdown")
    for w in first + second:
        away[w].start()
    take_x.wait()
    for x in own:
        x.wait()

    def take_first():
        for w in first:
            away[w].wait()
        forward_on["wqkv"].start()

    @pl.when(sec == 1)
    def _():
        take_first()
        forward_on["wqkv"].wait()

    n_tiles = n // TILE
    x_out = [
        (K.local(R.x.at[l + 1], R.layer_out.at[sec]), K.remote(R.x.at[l + 1], R.layer_out.at[sec], K.section_peer()))
        for l in range(2)
    ]

    def start_out(l, pair):
        pl.when(sec == l)(pair[0].start)
        pl.when(sec != l)(pair[1].start)

    stash = [getattr(R, "stash%d" % i) for i in range(n_tiles)]
    put_away = [K.local(R.P[i], stash[i]) for i in range(n_tiles)]
    bring_back = [K.local(stash[i], R.P[i]) for i in range(n_tiles)]

    def starts(copies):
        for x in copies:
            x.start()

    def waits(copies):
        for x in copies:
            x.wait()

    def forward(l, _):
        def at(layer, *steps):
            @pl.when(l == layer)
            def _():
                for step in steps:
                    step()

        project(R, l)
        at(1, lambda: waits(put_away))
        for i in range(n_tiles):
            attend_tile(R, l, i)
            if i == n_tiles - 2:
                at(
                    0,
                    lambda: starts(put_away[: n_tiles - 1]),
                    lambda: pl.when(sec == 0)(take_first),
                    lambda: waits([away[w] for w in second]),
                    lambda: starts([forward_on[w] for w in ("wout", "wup", "wdown")]),
                )
        at(0, lambda: starts(put_away[n_tiles - 1 :]), lambda: waits([forward_on[w] for w in ("wout", "wup", "wdown")]),
            lambda: pl.when(sec == 0)(forward_on["wqkv"].wait))
        feed(R, l)
        at(0, lambda: start_out(0, x_out[0]))
        at(1, lambda: start_out(1, x_out[1]))
        return 0

    lax.fori_loop(0, 2, forward, 0)

    R.small[...] = jnp.zeros_like(R.small)
    A = [reduction(K, l, R.grad_a.at[l], None, R, "a", TWO[0][l], TWO[1][l]) for l in range(2)]
    B = [reduction(K, l, R.grad_b.at[l], R.small.at[l], R, "b", TWO[2][l], TWO[3][l]) for l in range(2)]
    BEGIN, NEAR, LINE, SUM, GIVE, GIVE_NEAR, SHARE, FINISH = range(8)

    din_local = [K.local(R.d1, R.din_own) for l in range(2)]
    quarter = n // 4
    din_away = [
        K.remote(R.dinb.at[1], R.rdin, K.section_peer()),
        [K.remote(R.dinb.at[0, pl.ds(i * quarter, quarter)], R.rdin.at[pl.ds(i * quarter, quarter)], K.section_peer()) for i in range(4)],
    ]
    take_g.wait()

    def start_din(l, part=slice(None)):
        @pl.when(sec == l)
        def _():
            din_local[l].start()

        @pl.when(sec != l)
        def _():
            starts([din_away[0]] if l == 1 else din_away[1][:2])

    def backward(j, _):
        l = 1 - j

        def at(turn, *steps):
            @pl.when(j == turn)
            def _():
                for step in steps:
                    step()

        at(1, lambda: pl.when(sec == 1)(din_local[1].wait))
        feed_back(R, l, R.dinb[j].astype(f32))
        at(0, A[1][BEGIN])
        at(1, A[0][BEGIN], A[1][LINE], B[1][NEAR], lambda: waits(bring_back))
        attend_prepare(R, l)
        for i in range(n_tiles):
            attend_back_tile(R, l, i)
            if i == 1:
                at(0, A[1][NEAR], lambda: starts(bring_back[:2]))
                at(1, A[0][NEAR])
            if i == 2:
                at(1, B[1][LINE])
        at(0, lambda: starts(bring_back[2:]))
        project_back(R, l)
        at(0, lambda: start_din(1))
        at(1, lambda: start_din(0))
        weight_back(R, l)
        at(0, B[1][BEGIN])
        at(1, B[0][BEGIN])
        return 0

    lax.fori_loop(0, 2, backward, 0)

    A[0][LINE]()
    B[0][NEAR]()
    A[0][SUM]()
    A[1][SUM]()
    B[1][SUM]()
    B[0][LINE]()
    A[0][GIVE]()
    B[0][SUM]()
    pl.when(sec == 1)(lambda: starts(din_away[1][2:]))
    A[1][GIVE]()
    B[1][GIVE]()
    B[0][GIVE]()
    A[0][GIVE_NEAR]()
    A[1][GIVE_NEAR]()
    B[1][GIVE_NEAR]()
    B[0][GIVE_NEAR]()
    A[0][SHARE]()
    A[1][SHARE]()
    B[1][SHARE]()
    B[0][SHARE]()
    A[1][FINISH]()
    B[1][FINISH]()
    A[0][FINISH]()
    B[0][FINISH]()

    for l in range(2):

        @pl.when(sec == l)
        def _():
            x_out[l][0].wait()
            x_out[1 - l][1].wait_send()
            x_out[l][1].wait_recv()
            if l == 0:
                din_local[0].wait()
                din_away[0].wait_send()
                for x in din_away[1]:
                    x.wait_recv()
            else:
                for x in din_away[1]:
                    x.wait_send()
                din_away[0].wait_recv()


def place(n, *refs):
    names = OUTS + ["layer", "grad", "gqkv", "gout", "gup", "gdown", "ggains", "gbias", "gupb", "d", "a", "b", "df", "af", "bf", "tf", "small", "lay", "sem"]
    R = types.SimpleNamespace(**dict(zip(names, refs)))
    sec = lax.axis_index("section")
    used = iter(range(16))
    copy = lambda src, dst: pltpu.make_async_copy(src, dst, R.sem.at[next(used)])
    lay, own, far, low_a, low_b, low = [
        copy(R.layer_out, R.lay), copy(R.din_own, R.df.at[sec]), copy(R.rdin, R.d),
        copy(R.res_a, R.a), copy(R.res_b, R.b), copy(R.small_out, R.small),
    ]
    for x in (lay, own, far, low_a, low_b, low):
        x.start()
    out = [
        copy(R.lay, R.layer.at[0]), copy(R.df.at[sec], R.grad.at[0, sec]), copy(R.df.at[1 - sec], R.grad.at[0, 1 - sec]),
        copy(R.af.at[:, pl.ds(0, 256)], R.gout.at[0]), copy(R.af.at[:, pl.ds(256, 512)], R.gup.at[0]),
        copy(R.tf, R.gdown.at[0]), copy(R.bf, R.gqkv.at[0]),
    ]
    lay.wait()
    out[0].start()
    own.wait()
    out[1].start()
    far.wait()
    R.df[1 - sec] = R.d[...].astype(f32)
    out[2].start()
    low_a.wait()
    R.af[...] = R.a[:, 0:768].astype(f32)
    out[3].start()
    out[4].start()
    R.tf[...] = R.a[:, 768:1280].astype(f32).T
    out[5].start()
    low_b.wait()
    R.bf[...] = R.b[...].astype(f32)
    out[6].start()
    low.wait()

    def row(small, i):
        return jnp.concatenate([small[0, i : i + 1, :], small[1, i : i + 1, :]], axis=1)

    for i in range(2):
        R.ggains[0, i : i + 1, :] = row(R.small, i)
        R.gupb[0, :, 256 * i : 256 * i + 256] = row(R.small, 6 + i)
        R.gbias[i] = row(R.small, 8 + i)
    for i in range(2, 6):
        R.gbias[i] = row(R.small, i)
    for x in out:
        x.wait()


def kernel_call(dp, n, lengths, segments, cells, ograd, *weights):
    chips = min(8, dp // 2)
    groups = dp // (2 * chips)
    sc = scratch(n, chips, groups)

    def kern(*refs):
        body(types.SimpleNamespace(**dict(zip(names, refs))), n, dp)

    stash = [(HEADS * TILE, width) for _, width in spans(n)]
    names = INS + OUTS + ["stash%d" % i for i in range(len(stash))] + list(sc)
    vmem, smem, anywhere = [pl.BlockSpec(memory_space=m) for m in (pltpu.VMEM, pltpu.SMEM, pl.ANY)]
    shapes = [((2, n, 256), bf16), ((n, 256), f32), ((n, 256), bf16), ((256, 1280), bf16), ((256, 768), bf16)]
    shapes += [((2, 16, 128), f32)] + [(s, bf16) for s in stash]
    parts = pl.pallas_call(
        kern,
        out_shape=[jax.ShapeDtypeStruct(*s) for s in shapes],
        in_specs=[smem, vmem] + [anywhere] * 9,
        out_specs=[anywhere] * (len(OUTS) + len(stash)),
        scratch_shapes=list(sc.values()),
        compiler_params=pltpu.CompilerParams(
            vmem_limit_bytes=62 * 2**20, collective_id=0, has_side_effects=True
        ),
    )(lengths, segments, cells, ograd, *weights)[: len(OUTS)]
    shapes = [((1, 2, n, 256), bf16), ((1, 2, n, 256), f32), ((1, 256, 768), f32), ((1, 256, 256), f32),
              ((1, 256, 512), f32), ((1, 512, 256), f32), ((1, 2, 256), f32), ((6, 1, 256), f32), ((1, 1, 512), f32)]
    return pl.pallas_call(
        lambda *refs: place(n, *refs),
        out_shape=[jax.ShapeDtypeStruct(*s) for s in shapes],
        in_specs=[anywhere] * len(OUTS),
        out_specs=[anywhere] * 6 + [vmem] * 3,
        scratch_shapes=[
            pltpu.VMEM((n, 256), bf16), pltpu.VMEM((256, 1280), bf16), pltpu.VMEM((256, 768), bf16),
            pltpu.VMEM((2, n, 256), f32), pltpu.VMEM((256, 768), f32), pltpu.VMEM((256, 768), f32), pltpu.VMEM((512, 256), f32),
            pltpu.VMEM((2, 16, 128), f32), pltpu.VMEM((2, n, 256), bf16),
            pltpu.SemaphoreType.DMA((16,)),
        ],
        compiler_params=pltpu.CompilerParams(vmem_limit_bytes=62 * 2**20),
    )(*parts)


def solution(mesh):
    dp = mesh.shape["dp"]

    def on_device(cells, ograd, segments, lengths, *weights):
        *matrices, biases, up = weights
        weights = (*matrices, biases.transpose(1, 0, 2), up[:, None, :])
        out = kernel_call(dp, cells.shape[1], lengths, segments, cells, ograd, *weights)
        return (*out[:7], out[7].transpose(1, 0, 2), out[8][:, 0, :])

    w3, w2 = P("section", None, None), P("section", None)
    rows = P("section", "dp", None, None)
    return jax.shard_map(
        on_device,
        mesh=mesh,
        in_specs=(P("dp", None, None), P("dp", None, None), P("dp", None), P("dp"), w3, w3, w3, w3, w3, w3, w2),
        out_specs=(rows, rows, w3, w3, w3, w3, w3, w3, w2),
        check_vma=False,
    )
```

```python
import types

import jax
import jax.numpy as jnp
from jax import lax
from jax.experimental import pallas as pl
from jax.experimental.pallas import tpu as pltpu
from jax.sharding import PartitionSpec as P

MESH = pl.DeviceIdType.MESH
bf16 = jnp.bfloat16
f32 = jnp.float32
HEADS = 4
TILE = 256
REACH = 511
SEGMENTS = 12
CODE = 2.0**50
GELU_A = 0.7978845608028654
GELU_B = 0.044715


def dot(a, b):
    return lax.dot_general(a, b, (((1,), (0,)), ((), ())), preferred_element_type=f32)


def dot_tn(a, b):
    return lax.dot_general(a, b, (((0,), (0,)), ((), ())), preferred_element_type=f32)


def lanes(rows, width=128):
    return lax.broadcasted_iota(jnp.int32, (rows, width), 1)


def column_sum(v):
    return jnp.sum(v, axis=0, keepdims=True)


def setup(R):
    n = R.n
    token = lax.broadcasted_iota(jnp.int32, (64, n), 1)
    code = lax.broadcasted_iota(jnp.int32, (64, n), 0)
    segment = jnp.where(token < R.length, R.seg_row, SEGMENTS)
    used = code <= SEGMENTS
    key_code = jnp.where(used & (code == segment), CODE, 0.0).astype(bf16)
    query_code = jnp.where(used & (code != segment), -CODE, 0.0).astype(bf16)
    R.qcode[...] = jnp.concatenate([jnp.zeros((64, n), bf16), query_code], axis=0).T
    for h in range(HEADS):
        R.kc[128 * h + 64 : 128 * h + 128, :] = key_code
    R.vT[256:320, :] = jnp.zeros((64, n), bf16)


def spans(n):
    out = []
    for i in range(n // TILE):
        lo = max(0, (i * TILE - REACH) // 128 * 128)
        hi = min(n, -(-(i * TILE + TILE + REACH) // 128) * 128)
        out.append((lo, hi - lo))
    return out


def head_tile(pair, h):
    return pair if h % 2 == 0 else pltpu.roll(pair, 64, 1)


def real_rows(R, start, rows):
    return (start + lax.broadcasted_iota(jnp.int32, (rows, 1), 0)) < R.length


def pick_heads(t):
    lane = lanes(TILE, 256) // 64
    o = t[0:TILE]
    for h in range(1, HEADS):
        o = jnp.where(lane == h, t[h * TILE : h * TILE + TILE], o)
    return o


def project(R, l):
    n = R.n
    shift = jnp.concatenate([R.biases[l, 0], jnp.zeros((1, 256), f32), R.biases[l, 1]], axis=1)
    packed = dot(R.x[l], R.wqkv[l]) + shift
    lane = lanes(n)
    q = packed[:, 0:256] * 0.125
    R.qn[l] = q.astype(bf16)
    for h in range(HEADS):
        t = head_tile(q[:, 128 * (h // 2) : 128 * (h // 2) + 128], h)
        R.qh[h] = jnp.where(lane < 64, t, 0.0).astype(bf16) + R.qcode[...]
    k = packed[:, 256:512].astype(bf16)
    R.kn[l] = k
    R.vn[l] = packed[:, 512:768].astype(bf16)
    kT = k.T
    for h in range(HEADS):
        R.kc[128 * h : 128 * h + 64, :] = kT[64 * h : 64 * h + 64]


def attend_tile(R, l, i):
    lo, width = spans(R.n)[i]
    rows, cols = pl.ds(i * TILE, TILE), pl.ds(lo, width)
    real = real_rows(R, i * TILE, TILE)
    for h in range(HEADS):
        s = dot(R.qh[h, rows, :], R.kc[128 * h : 128 * h + 128, cols])
        e = jnp.exp(s - jnp.max(s, axis=1, keepdims=True))
        r = jnp.where(real, 1.0 / jnp.sum(e, axis=1, keepdims=True), 0.0)
        R.P[i][h * TILE : h * TILE + TILE, :] = (e * r).astype(bf16)
    o = pick_heads(dot(R.P[i][...], R.vn[l, cols, :]))
    o = jnp.where(real, o, R.vn[l, rows, :].astype(f32))
    R.octx[l, rows, :] = o


def norm(v):
    c = v - jnp.mean(v, axis=-1, keepdims=True)
    s = lax.rsqrt(jnp.mean(c * c, axis=-1, keepdims=True) + 1e-5)
    return c * s, s


def feed(R, l):
    att = dot(R.octx[l].astype(bf16), R.wout[l]) + R.biases[l, 2]
    n1, s1 = norm(R.x[l].astype(f32) + att)
    hidden = n1 * R.gains[l, 0:1] + R.biases[l, 3]
    low = hidden.astype(bf16)
    u = dot(low, R.wup[l]) + R.upb[l]
    q = (GELU_A * GELU_B) * (u * u)
    w = 0.5 * jnp.tanh(u * (q + GELU_A)) + 0.5
    a = u * w
    act = a.astype(bf16)
    slope = w + a * ((1.0 - w) * (6.0 * q + 2.0 * GELU_A))
    n2, s2 = norm(hidden + (dot(act, R.wdown[l]) + R.biases[l, 4]))
    R.n1[l] = n1
    R.stat[l, :, 4:5] = s1
    R.gp[l] = slope
    R.act[l] = act
    R.n2[l] = n2
    R.stat[l, :, 5:6] = s2
    R.x[l + 1] = (n2 * R.gains[l, 1:2] + R.biases[l, 5]).astype(bf16)


def norm_back(g, n, s, gain):
    gg = g * gain
    return s * (gg - jnp.mean(gg, axis=-1, keepdims=True) - n * jnp.mean(gg * n, axis=-1, keepdims=True))


def put_small(ref, row, v):
    ref[0, row : row + 1, :] = v[:, 0:128]
    ref[1, row : row + 1, :] = v[:, 128:256]


def feed_back(R, l, g):
    n = R.n
    R.woutT[...] = R.wout[l].T
    R.wupT[...] = R.wup[l].T
    R.wdownT[...] = R.wdown[l].T
    R.wqkvT[...] = R.wqkv[l].T
    small = R.small.at[l]
    n2 = R.n2[l]
    d2 = norm_back(g, n2, R.stat[l, :, 5:6], R.gains[l, 1:2])
    put_small(small, 1, column_sum(g * n2))
    put_small(small, 5, column_sum(g))
    dl = d2.astype(bf16)
    R.dlow[...] = dl
    put_small(small, 4, column_sum(d2))
    du = dot(dl, R.wdownT[...]) * R.gp[l]
    up = column_sum(du)
    put_small(small, 6, up[:, 0:256])
    put_small(small, 7, up[:, 256:512])
    du = du.astype(bf16)
    R.dup[...] = du
    dh = d2 + dot(du, R.wupT[...])
    n1 = R.n1[l]
    low = (n1 * R.gains[l, 0:1] + R.biases[l, 3]).astype(bf16)
    d1 = norm_back(dh, n1, R.stat[l, :, 4:5], R.gains[l, 0:1])
    put_small(small, 0, column_sum(dh * n1))
    put_small(small, 3, column_sum(dh))
    put_small(small, 2, column_sum(d1))
    R.d1[...] = d1
    da = d1.astype(bf16)
    R.datt[...] = da
    dcb = dot(da, R.woutT[...]).astype(bf16)
    R.dctx[...] = dcb
    R.grad_a[l, :, 0:256] = dot_tn(R.octx[l].astype(bf16), R.datt[...])
    R.grad_a[l, :, 256:768] = dot_tn(low, R.dup[...])
    R.grad_a[l, :, 768:1280] = dot_tn(R.dlow[...], R.act[l])


def attend_prepare(R, l):
    n = R.n
    dcb = R.dctx[...]
    dc = dcb.astype(f32)
    e = dc * R.octx[l]
    lane = lanes(n)
    for h in range(HEADS):
        pair = slice(128 * (h // 2), 128 * (h // 2) + 128)
        R.delta[:, h : h + 1] = jnp.sum(
            jnp.where((lane // 64) == (h % 2), e[:, pair], 0.0), axis=1, keepdims=True
        )
        R.doh[h] = jnp.where(lane < 64, head_tile(dc[:, pair], h), 0.0).astype(bf16)
    R.doT[...] = dcb.T
    R.qT[...] = R.qn[l].T
    R.vT[0:256, :] = R.vn[l].T


def add_columns(ref, head, lo, begun, v):
    old = max(0, min(begun - lo, v.shape[1]))
    if old:
        ref[head, pl.ds(lo, old)] += v[:, 0:old]
    if old < v.shape[1]:
        ref[head, pl.ds(lo + old, v.shape[1] - old)] = v[:, old:]


def attend_back_tile(R, l, i):
    lo, width = spans(R.n)[i]
    begun = max([a + b for a, b in spans(R.n)[:i]], default=0)
    rows, cols = pl.ds(i * TILE, TILE), pl.ds(lo, width)
    for h in range(HEADS):
        head, part = slice(64 * h, 64 * h + 64), slice(h * TILE, h * TILE + TILE)
        p = R.P[i][part, :]
        dp = dot(R.doh[h, rows, :], R.vT[64 * h : 64 * h + 128, cols])
        R.DS[part, 0:width] = (p.astype(f32) * (dp - R.delta[rows, h : h + 1])).astype(bf16)
        add_columns(R.dvT, head, lo, begun, dot(R.doT[head, rows], p))
    for h in range(HEADS):
        head, part = slice(64 * h, 64 * h + 64), slice(h * TILE, h * TILE + TILE)
        add_columns(R.dkT, head, lo, begun, dot(R.qT[head, rows], R.DS[part, 0:width]))
    R.dqkv[rows, 0:256] = (pick_heads(dot(R.DS[:, 0:width], R.kn[l, cols, :])) * 0.125).astype(bf16)


def project_back(R, l):
    real = real_rows(R, 0, R.n)
    dv = R.dvT[...].T + jnp.where(real, 0.0, R.dctx[...].astype(f32))
    R.dqkv[:, 256:512] = R.dkT[...].T.astype(bf16)
    R.dqkv[:, 512:768] = dv.astype(bf16)
    put_small(R.small.at[l], 8, column_sum(R.dqkv[:, 0:256].astype(f32)))
    put_small(R.small.at[l], 9, column_sum(dv))
    d = R.d1[...] + dot(R.dqkv[...], R.wqkvT[...])
    R.d1[...] = d
    R.dinb[l] = d.astype(bf16)


def weight_back(R, l):
    R.grad_b[l] = dot_tn(R.x[l], R.dqkv[...])


class Links:
    def __init__(self, dp, send, recv, local):
        self.sec = lax.axis_index("section")
        self.dp = lax.axis_index("dp")
        self.send, self.recv, self.local_sem = send, recv, local
        self.used = 0
        self.used_local = 0
        self.core = self.dp % 2
        self.chips = min(8, dp // 2)
        self.groups = dp // (2 * self.chips)
        self.chip = (self.dp // 2) % self.chips
        self.pending = []

    def flip(self, index, bit):
        return index + bit - 2 * bit * ((index // bit) % 2)

    def xor(self, index, mask):
        bit = 1
        while bit <= mask:
            if mask & bit:
                index = self.flip(index, bit)
            bit *= 2
        return index

    def section_peer(self):
        return (1 - self.sec, self.dp)

    def core_peer(self):
        return (self.sec, self.flip(self.dp, 1))

    def chip_peer(self, k):
        return (self.sec, self.xor(self.dp, 2 * k))

    def group_peer(self, k):
        return (self.sec, self.xor(self.dp, 2 * self.chips * k))

    def peers(self):
        out = [self.section_peer(), self.core_peer()]
        out += [self.chip_peer(k) for k in range(1, self.chips)]
        out += [self.group_peer(k) for k in range(1, self.groups)]
        return out

    def remote(self, src, dst, peer):
        i = self.used
        self.used += 1
        return pltpu.make_async_remote_copy(
            src, dst, self.send.at[i], self.recv.at[i], device_id=peer, device_id_type=MESH
        )

    def local(self, src, dst):
        i = self.used_local
        self.used_local += 1
        return pltpu.make_async_copy(src, dst, self.local_sem.at[i])


def reduction(K, l, grad, small, R, name, sum_two, give_two):
    get = lambda part: getattr(R, name + "_" + part).at[l]
    r1, s2, ry, r2, acc, r3 = [get(p) for p in ("r1", "s2", "ry", "r2", "acc", "r3")]
    res, out = getattr(R, name + "_res"), getattr(R, "res_" + name)
    c, chip, chips, groups = K.core, K.chip, K.chips, K.groups
    half = grad.shape[0] // 2
    piece = half // chips
    near = half // 2
    line = chips // 2

    def place_of(index):
        return (index % 2) * near + (index // 2) * piece

    start = c * half
    mine, other = pl.ds(start, half), pl.ds((1 - c) * half, half)
    my_near, other_near = (chip % 2) * near, (1 - chip % 2) * near
    part = pl.ds(place_of(chip), piece)
    owner = K.sec == l
    has_small = small is not None
    core_out = [K.remote(grad.at[other], r1, K.core_peer())]
    everyone = range(1, chips)
    ahead = range(2, chips, 2)
    to_near = [K.remote(s2.at[pl.ds(other_near, near)], ry, K.chip_peer(1))] if sum_two else []
    targets = ahead if sum_two else everyone
    scatter = [
        K.remote(s2.at[pl.ds(place_of(K.xor(chip, k)), piece)], r2.at[k], K.chip_peer(k)) for k in targets
    ]
    across = [K.remote(acc, r3, K.section_peer())]
    spread = []
    if groups > 1:
        r4 = get("r4")
        spread = [K.remote(acc, r4.at[k], K.group_peer(k)) for k in range(1, groups)]
    gather = [
        K.remote(res.at[part], res.at[part], K.chip_peer(k)) for k in (ahead if give_two else everyone)
    ]
    rows = pl.ds(my_near, near)
    from_near = [K.remote(res.at[rows], res.at[rows], K.chip_peer(1))] if give_two else []
    core_back = [K.remote(res, out.at[mine], K.core_peer())]
    keep = [K.local(res, out.at[mine])]
    if has_small:
        q1, q2, ty, t2, qacc, q3, qres = [get(p) for p in ("q1", "q2", "ty", "t2", "qacc", "q3", "qres")]
        core_out.append(K.remote(small.at[1 - c], q1, K.core_peer()))
        if sum_two:
            to_near.append(K.remote(q2, ty, K.chip_peer(1)))
        little_src = qacc if sum_two else q2
        scatter += [K.remote(little_src, t2.at[k], K.chip_peer(k)) for k in targets]
        across.append(K.remote(q2, q3, K.section_peer()))
        core_back.append(K.remote(qres, R.small_out.at[c], K.core_peer()))
        keep.append(K.local(qres, R.small_out.at[c]))
        if groups > 1:
            q4 = get("q4")
            spread += [K.remote(qacc, q4.at[k], K.group_peer(k)) for k in range(1, groups)]

    def each(copies, *what):
        for w in what:
            for x in copies:
                getattr(x, w)()

    def begin():
        each(core_out, "start")

    def to_neighbour():
        each(core_out, "wait")
        total = grad[mine, :] + r1[...]
        grad[mine, :] = total
        s2[...] = total.astype(bf16)
        if has_small:
            q2[...] = small[c] + q1[...]
        each(to_near if sum_two else scatter, "start")

    def to_line():
        if sum_two:
            each(to_near, "wait")
            own = pl.ds(start + my_near, near)
            total = grad[own, :] + ry[...].astype(f32)
            grad[own, :] = total
            s2[pl.ds(my_near, near), :] = total.astype(bf16)
            if has_small:
                qacc[...] = q2[...] + ty[...]
            each(scatter, "start")

    def sum_pieces():
        each(scatter, "wait")
        total = grad[pl.ds(start + place_of(chip), piece), :]
        for k in targets:
            total = total + r2[k].astype(f32)
        acc[...] = total
        if has_small:
            little = little_src[...]
            for k in targets:
                little = little + t2[k]
            q2[...] = little
        pl.when(jnp.logical_not(owner))(lambda: each(across, "start"))

    def give_line():
        @pl.when(owner)
        def _():
            each(across, "wait_recv")
            acc[...] += r3[...]
            if has_small:
                qacc[...] = q2[...] + q3[...]
            each(spread, "start", "wait")
            total = acc[...]
            for k in range(1, groups):
                total = total + r4[k]
            res[part, :] = total.astype(bf16)
            each(gather, "start")
            if has_small:
                little = qacc[...]
                for k in range(1, groups):
                    little = little + q4[k]
                qres[...] = little

    def give_neighbour():
        if give_two:

            @pl.when(owner)
            def _():
                each(gather, "wait")
                each(from_near, "start")

    def share():
        @pl.when(owner)
        def _():
            each(from_near if give_two else gather, "wait")
            each(core_back, "start")
            each(keep, "start")

    def finish():
        @pl.when(owner)
        def _():
            each(core_back, "wait")
            each(keep, "wait")

        pl.when(jnp.logical_not(owner))(lambda: each(across, "wait_send"))

    return begin, to_neighbour, to_line, sum_pieces, give_line, give_neighbour, share, finish


TWO = ((False, False), (True, True), (False, False), (False, True))


def scratch(n, chips, groups):
    def V(*s):
        return pltpu.VMEM(s[:-1], s[-1])

    out = dict(
        wqkv=V(2, 256, 768, bf16), wout=V(2, 256, 256, bf16), wup=V(2, 256, 512, bf16), wdown=V(2, 512, 256, bf16),
        gains=V(2, 2, 256, f32), biases=V(2, 6, 1, 256, f32), upb=V(2, 1, 512, f32),
        x=V(3, n, 256, bf16), qn=V(2, n, 256, bf16), kn=V(2, n, 256, bf16), vn=V(2, n, 256, bf16),
        octx=V(2, n, 256, f32), DS=V(HEADS * TILE, n, bf16),
        n1=V(2, n, 256, f32), n2=V(2, n, 256, f32), stat=V(2, n, 128, f32),
        gp=V(2, n, 512, f32), act=V(2, n, 512, bf16),
        qcode=V(n, 128, bf16), qh=V(HEADS, n, 128, bf16), kc=V(512, n, bf16), vT=V(320, n, bf16),
        doh=V(HEADS, n, 128, bf16), doT=V(256, n, bf16), qT=V(256, n, bf16), delta=V(n, 128, f32), dctx=V(n, 256, bf16),
        dkT=V(256, n, f32), dvT=V(256, n, f32), dqkv=V(n, 768, bf16),
        d1=V(n, 256, f32),
        woutT=V(256, 256, bf16), wupT=V(512, 256, bf16), wdownT=V(256, 512, bf16), wqkvT=V(768, 256, bf16),
        dinb=V(2, n, 256, bf16),
        small=V(2, 2, 16, 128, f32),
    )
    for name, width in (("a", 1280), ("b", 768)):
        piece = 128 // chips
        out["grad_" + name] = V(2, 256, width, f32)
        out[name + "_r1"] = V(2, 128, width, f32)
        out[name + "_s2"] = V(2, 128, width, bf16)
        out[name + "_r2"] = V(2, chips, piece, width, bf16)
        out[name + "_acc"] = V(2, piece, width, f32)
        out[name + "_r3"] = V(2, piece, width, f32)
        out[name + "_ry"] = V(2, 64, width, bf16)
        out[name + "_res"] = V(128, width, bf16)
        if groups > 1:
            out[name + "_r4"] = V(2, groups, piece, width, f32)
    for part, lead in (("q1", ()), ("q2", ()), ("ty", ()), ("t2", (chips,)), ("qacc", ()), ("q3", ()), ("qres", ()), ("q4", (groups,))):
        out["b_" + part] = V(2, *lead, 16, 128, f32)
    for i, (_, width) in enumerate(spans(n)):
        out["P%d" % i] = V(HEADS * TILE, width, bf16)
    copies = 32 + 4 * (8 + 3 * chips + 2 * groups)
    out["send"] = pltpu.SemaphoreType.DMA((copies,))
    out["recv"] = pltpu.SemaphoreType.DMA((copies,))
    out["local"] = pltpu.SemaphoreType.DMA((64,))
    return out


INS = ["len_s", "seg_v", "cells", "ograd", "i_wqkv", "i_wout", "i_wup", "i_wdown", "i_gains", "i_biases", "i_upb"]
OUTS = ["layer_out", "din_own", "rdin", "res_a", "res_b", "small_out"]
WEIGHTS = ["wqkv", "wout", "wup", "wdown", "gains", "biases", "upb"]


def body(R, n, dp):
    K = Links(dp, R.send, R.recv, R.local)
    sec, c = K.sec, K.core
    R.n = n
    R.P = [getattr(R, "P%d" % i) for i in range(n // TILE)]
    R.dup = R.DS.at[:, pl.ds(0, 512)]
    R.dlow = R.DS.at[:, pl.ds(512, 256)]
    R.datt = R.DS.at[:, pl.ds(768, 256)]
    R.length = R.len_s[sec]
    R.seg_row = R.seg_v[pl.ds(sec, 1), :]

    barrier = pltpu.get_barrier_semaphore()
    peers = K.peers()[::-1]
    for peer in peers:
        pl.semaphore_signal(barrier, 1, device_id=peer, device_id_type=MESH)

    take_x = K.local(R.cells.at[sec], R.x.at[0])
    take_g = K.local(R.ograd.at[sec], R.dinb.at[0])
    given = {w: getattr(R, "i_" + w) if w == "biases" else getattr(R, "i_" + w).at[0] for w in WEIGHTS}
    own = [K.local(given[w], getattr(R, w).at[sec]) for w in WEIGHTS]
    take_x.start()
    for x in own:
        x.start()
    take_g.start()

    away, forward_on = {}, {}
    for w in WEIGHTS:
        src, slots = given[w], getattr(R, w)
        if w in ("gains", "biases", "upb"):
            away[w] = K.remote(src, slots.at[sec], K.section_peer())
        else:
            half = src.shape[0] // 2
            rows = pl.ds(c * half, half)
            away[w] = K.remote(src.at[rows], slots.at[sec, rows], K.section_peer())
            theirs = slots.at[1 - sec, rows]
            forward_on[w] = K.remote(theirs, theirs, K.core_peer())

    setup(R)
    pl.semaphore_wait(barrier, len(peers))
    first = ("biases", "wqkv")
    second = ("gains", "upb", "wout", "wup", "wdown")
    for w in first + second:
        away[w].start()
    take_x.wait()
    for x in own:
        x.wait()

    def take_first():
        for w in first:
            away[w].wait()
        forward_on["wqkv"].start()

    @pl.when(sec == 1)
    def _():
        take_first()
        forward_on["wqkv"].wait()

    n_tiles = n // TILE
    x_out = [
        (K.local(R.x.at[l + 1], R.layer_out.at[sec]), K.remote(R.x.at[l + 1], R.layer_out.at[sec], K.section_peer()))
        for l in range(2)
    ]

    def start_out(l, pair):
        pl.when(sec == l)(pair[0].start)
        pl.when(sec != l)(pair[1].start)

    stash = [getattr(R, "stash%d" % i) for i in range(n_tiles)]
    put_away = [K.local(R.P[i], stash[i]) for i in range(n_tiles)]
    bring_back = [K.local(stash[i], R.P[i]) for i in range(n_tiles)]

    def starts(copies):
        for x in copies:
            x.start()

    def waits(copies):
        for x in copies:
            x.wait()

    def forward(l, _):
        def at(layer, *steps):
            @pl.when(l == layer)
            def _():
                for step in steps:
                    step()

        project(R, l)
        at(1, lambda: waits(put_away))
        for i in range(n_tiles):
            attend_tile(R, l, i)
            if i == n_tiles - 2:
                at(
                    0,
                    lambda: starts(put_away[: n_tiles - 1]),
                    lambda: pl.when(sec == 0)(take_first),
                    lambda: waits([away[w] for w in second]),
                    lambda: starts([forward_on[w] for w in ("wout", "wup", "wdown")]),
                )
        at(0, lambda: starts(put_away[n_tiles - 1 :]), lambda: waits([forward_on[w] for w in ("wout", "wup", "wdown")]),
            lambda: pl.when(sec == 0)(forward_on["wqkv"].wait))
        feed(R, l)
        at(0, lambda: start_out(0, x_out[0]))
        at(1, lambda: start_out(1, x_out[1]))
        return 0

    lax.fori_loop(0, 2, forward, 0)

    R.small[...] = jnp.zeros_like(R.small)
    A = [reduction(K, l, R.grad_a.at[l], None, R, "a", TWO[0][l], TWO[1][l]) for l in range(2)]
    B = [reduction(K, l, R.grad_b.at[l], R.small.at[l], R, "b", TWO[2][l], TWO[3][l]) for l in range(2)]
    BEGIN, NEAR, LINE, SUM, GIVE, GIVE_NEAR, SHARE, FINISH = range(8)

    din_local = [K.local(R.d1, R.din_own) for l in range(2)]
    quarter = n // 4
    din_away = [
        K.remote(R.dinb.at[1], R.rdin, K.section_peer()),
        [K.remote(R.dinb.at[0, pl.ds(i * quarter, quarter)], R.rdin.at[pl.ds(i * quarter, quarter)], K.section_peer()) for i in range(4)],
    ]
    take_g.wait()

    def start_din(l, part=slice(None)):
        @pl.when(sec == l)
        def _():
            din_local[l].start()

        @pl.when(sec != l)
        def _():
            starts([din_away[0]] if l == 1 else din_away[1][:2])

    def backward(j, _):
        l = 1 - j

        def at(turn, *steps):
            @pl.when(j == turn)
            def _():
                for step in steps:
                    step()

        at(1, lambda: pl.when(sec == 1)(din_local[1].wait))
        feed_back(R, l, R.dinb[j].astype(f32))
        at(0, A[1][BEGIN])
        at(1, A[0][BEGIN], A[1][LINE], B[1][NEAR], lambda: waits(bring_back))
        attend_prepare(R, l)
        for i in range(n_tiles):
            attend_back_tile(R, l, i)
            if i == 1:
                at(0, A[1][NEAR], lambda: starts(bring_back[:2]))
                at(1, A[0][NEAR])
            if i == 2:
                at(1, B[1][LINE])
        at(0, lambda: starts(bring_back[2:]))
        project_back(R, l)
        at(0, lambda: start_din(1))
        at(1, lambda: start_din(0))
        weight_back(R, l)
        at(0, B[1][BEGIN])
        at(1, B[0][BEGIN])
        return 0

    lax.fori_loop(0, 2, backward, 0)

    A[0][LINE]()
    B[0][NEAR]()
    A[0][SUM]()
    A[1][SUM]()
    B[1][SUM]()
    B[0][LINE]()
    A[0][GIVE]()
    B[0][SUM]()
    pl.when(sec == 1)(lambda: starts(din_away[1][2:]))
    A[1][GIVE]()
    B[1][GIVE]()
    B[0][GIVE]()
    A[0][GIVE_NEAR]()
    A[1][GIVE_NEAR]()
    B[1][GIVE_NEAR]()
    B[0][GIVE_NEAR]()
    A[0][SHARE]()
    A[1][SHARE]()
    B[1][SHARE]()
    B[0][SHARE]()
    A[1][FINISH]()
    B[1][FINISH]()
    A[0][FINISH]()
    B[0][FINISH]()

    for l in range(2):

        @pl.when(sec == l)
        def _():
            x_out[l][0].wait()
            x_out[1 - l][1].wait_send()
            x_out[l][1].wait_recv()
            if l == 0:
                din_local[0].wait()
                din_away[0].wait_send()
                for x in din_away[1]:
                    x.wait_recv()
            else:
                for x in din_away[1]:
                    x.wait_send()
                din_away[0].wait_recv()


def place(n, *refs):
    names = OUTS + ["layer", "grad", "gqkv", "gout", "gup", "gdown", "ggains", "gbias", "gupb", "d", "a", "b", "df", "af", "bf", "tf", "small", "lay", "sem"]
    R = types.SimpleNamespace(**dict(zip(names, refs)))
    sec = lax.axis_index("section")
    used = iter(range(16))
    copy = lambda src, dst: pltpu.make_async_copy(src, dst, R.sem.at[next(used)])
    lay, own, far, low_a, low_b, low = [
        copy(R.layer_out, R.lay), copy(R.din_own, R.df.at[sec]), copy(R.rdin, R.d),
        copy(R.res_a, R.a), copy(R.res_b, R.b), copy(R.small_out, R.small),
    ]
    for x in (lay, own, far, low_a, low_b, low):
        x.start()
    out = [
        copy(R.lay, R.layer.at[0]), copy(R.df.at[sec], R.grad.at[0, sec]), copy(R.df.at[1 - sec], R.grad.at[0, 1 - sec]),
        copy(R.af.at[:, pl.ds(0, 256)], R.gout.at[0]), copy(R.af.at[:, pl.ds(256, 512)], R.gup.at[0]),
        copy(R.tf, R.gdown.at[0]), copy(R.bf, R.gqkv.at[0]),
    ]
    lay.wait()
    out[0].start()
    own.wait()
    out[1].start()
    far.wait()
    R.df[1 - sec] = R.d[...].astype(f32)
    out[2].start()
    low_a.wait()
    R.af[...] = R.a[:, 0:768].astype(f32)
    out[3].start()
    out[4].start()
    R.tf[...] = R.a[:, 768:1280].astype(f32).T
    out[5].start()
    low_b.wait()
    R.bf[...] = R.b[...].astype(f32)
    out[6].start()
    low.wait()

    def row(small, i):
        return jnp.concatenate([small[0, i : i + 1, :], small[1, i : i + 1, :]], axis=1)

    for i in range(2):
        R.ggains[0, i : i + 1, :] = row(R.small, i)
        R.gupb[0, :, 256 * i : 256 * i + 256] = row(R.small, 6 + i)
        R.gbias[i] = row(R.small, 8 + i)
    for i in range(2, 6):
        R.gbias[i] = row(R.small, i)
    for x in out:
        x.wait()


def kernel_call(dp, n, lengths, segments, cells, ograd, *weights):
    chips = min(8, dp // 2)
    groups = dp // (2 * chips)
    sc = scratch(n, chips, groups)

    def kern(*refs):
        body(types.SimpleNamespace(**dict(zip(names, refs))), n, dp)

    stash = [(HEADS * TILE, width) for _, width in spans(n)]
    names = INS + OUTS + ["stash%d" % i for i in range(len(stash))] + list(sc)
    vmem, smem, anywhere = [pl.BlockSpec(memory_space=m) for m in (pltpu.VMEM, pltpu.SMEM, pl.ANY)]
    shapes = [((2, n, 256), bf16), ((n, 256), f32), ((n, 256), bf16), ((256, 1280), bf16), ((256, 768), bf16)]
    shapes += [((2, 16, 128), f32)] + [(s, bf16) for s in stash]
    parts = pl.pallas_call(
        kern,
        out_shape=[jax.ShapeDtypeStruct(*s) for s in shapes],
        in_specs=[smem, vmem] + [anywhere] * 9,
        out_specs=[anywhere] * (len(OUTS) + len(stash)),
        scratch_shapes=list(sc.values()),
        compiler_params=pltpu.CompilerParams(
            vmem_limit_bytes=62 * 2**20, collective_id=0, has_side_effects=True
        ),
    )(lengths, segments, cells, ograd, *weights)[: len(OUTS)]
    shapes = [((1, 2, n, 256), bf16), ((1, 2, n, 256), f32), ((1, 256, 768), f32), ((1, 256, 256), f32),
              ((1, 256, 512), f32), ((1, 512, 256), f32), ((1, 2, 256), f32), ((6, 1, 256), f32), ((1, 1, 512), f32)]
    return pl.pallas_call(
        lambda *refs: place(n, *refs),
        out_shape=[jax.ShapeDtypeStruct(*s) for s in shapes],
        in_specs=[anywhere] * len(OUTS),
        out_specs=[anywhere] * 6 + [vmem] * 3,
        scratch_shapes=[
            pltpu.VMEM((n, 256), bf16), pltpu.VMEM((256, 1280), bf16), pltpu.VMEM((256, 768), bf16),
            pltpu.VMEM((2, n, 256), f32), pltpu.VMEM((256, 768), f32), pltpu.VMEM((256, 768), f32), pltpu.VMEM((512, 256), f32),
            pltpu.VMEM((2, 16, 128), f32), pltpu.VMEM((2, n, 256), bf16),
            pltpu.SemaphoreType.DMA((16,)),
        ],
        compiler_params=pltpu.CompilerParams(vmem_limit_bytes=62 * 2**20),
    )(*parts)


def solution(mesh):
    dp = mesh.shape["dp"]

    def on_device(cells, ograd, segments, lengths, *weights):
        *matrices, biases, up = weights
        weights = (*matrices, biases.transpose(1, 0, 2), up[:, None, :])
        out = kernel_call(dp, cells.shape[1], lengths, segments, cells, ograd, *weights)
        return (*out[:7], out[7].transpose(1, 0, 2), out[8][:, 0, :])

    w3, w2 = P("section", None, None), P("section", None)
    rows = P("section", "dp", None, None)
    return jax.shard_map(
        on_device,
        mesh=mesh,
        in_specs=(P("dp", None, None), P("dp", None, None), P("dp", None), P("dp"), w3, w3, w3, w3, w3, w3, w2),
        out_specs=(rows, rows, w3, w3, w3, w3, w3, w3, w2),
        check_vma=False,
    )
```

```python
import types

import jax
import jax.numpy as jnp
from jax import lax
from jax.experimental import pallas as pl
from jax.experimental.pallas import tpu as pltpu
from jax.sharding import PartitionSpec as P

MESH = pl.DeviceIdType.MESH
bf16 = jnp.bfloat16
f32 = jnp.float32
HEADS = 4
TILE = 256
REACH = 511
SEGMENTS = 12
CODE = 2.0**50
GELU_A = 0.7978845608028654
GELU_B = 0.044715


def dot(a, b):
    return lax.dot_general(a, b, (((1,), (0,)), ((), ())), preferred_element_type=f32)


def dot_tn(a, b):
    return lax.dot_general(a, b, (((0,), (0,)), ((), ())), preferred_element_type=f32)


def lanes(rows, width=128):
    return lax.broadcasted_iota(jnp.int32, (rows, width), 1)


def column_sum(v):
    return jnp.sum(v, axis=0, keepdims=True)


def setup(R):
    n = R.n
    token = lax.broadcasted_iota(jnp.int32, (64, n), 1)
    code = lax.broadcasted_iota(jnp.int32, (64, n), 0)
    segment = jnp.where(token < R.length, R.seg_row, SEGMENTS)
    used = code <= SEGMENTS
    key_code = jnp.where(used & (code == segment), CODE, 0.0).astype(bf16)
    query_code = jnp.where(used & (code != segment), -CODE, 0.0).astype(bf16)
    R.qcode[...] = jnp.concatenate([jnp.zeros((64, n), bf16), query_code], axis=0).T
    for h in range(HEADS):
        R.kc[128 * h + 64 : 128 * h + 128, :] = key_code
    R.vT[256:320, :] = jnp.zeros((64, n), bf16)


def spans(n):
    out = []
    for i in range(n // TILE):
        lo = max(0, (i * TILE - REACH) // 128 * 128)
        hi = min(n, -(-(i * TILE + TILE + REACH) // 128) * 128)
        out.append((lo, hi - lo))
    return out


def head_tile(pair, h):
    return pair if h % 2 == 0 else pltpu.roll(pair, 64, 1)


def real_rows(R, start, rows):
    return (start + lax.broadcasted_iota(jnp.int32, (rows, 1), 0)) < R.length


def pick_heads(t):
    lane = lanes(TILE, 256) // 64
    o = t[0:TILE]
    for h in range(1, HEADS):
        o = jnp.where(lane == h, t[h * TILE : h * TILE + TILE], o)
    return o


def project(R, l):
    n = R.n
    shift = jnp.concatenate([R.biases[l, 0], jnp.zeros((1, 256), f32), R.biases[l, 1]], axis=1)
    packed = dot(R.x[l], R.wqkv[l]) + shift
    lane = lanes(n)
    q = packed[:, 0:256] * 0.125
    R.qn[l] = q.astype(bf16)
    for h in range(HEADS):
        t = head_tile(q[:, 128 * (h // 2) : 128 * (h // 2) + 128], h)
        R.qh[h] = jnp.where(lane < 64, t, 0.0).astype(bf16) + R.qcode[...]
    k = packed[:, 256:512].astype(bf16)
    R.kn[l] = k
    R.vn[l] = packed[:, 512:768].astype(bf16)
    kT = k.T
    for h in range(HEADS):
        R.kc[128 * h : 128 * h + 64, :] = kT[64 * h : 64 * h + 64]


def attend_tile(R, l, i):
    lo, width = spans(R.n)[i]
    rows, cols = pl.ds(i * TILE, TILE), pl.ds(lo, width)
    real = real_rows(R, i * TILE, TILE)
    for h in range(HEADS):
        s = dot(R.qh[h, rows, :], R.kc[128 * h : 128 * h + 128, cols])
        e = jnp.exp(s - jnp.max(s, axis=1, keepdims=True))
        r = jnp.where(real, 1.0 / jnp.sum(e, axis=1, keepdims=True), 0.0)
        R.P[i][h * TILE : h * TILE + TILE, :] = (e * r).astype(bf16)
    o = pick_heads(dot(R.P[i][...], R.vn[l, cols, :]))
    o = jnp.where(real, o, R.vn[l, rows, :].astype(f32))
    R.octx[l, rows, :] = o


def norm(v):
    c = v - jnp.mean(v, axis=-1, keepdims=True)
    s = lax.rsqrt(jnp.mean(c * c, axis=-1, keepdims=True) + 1e-5)
    return c * s, s


def feed(R, l):
    att = dot(R.octx[l].astype(bf16), R.wout[l]) + R.biases[l, 2]
    n1, s1 = norm(R.x[l].astype(f32) + att)
    hidden = n1 * R.gains[l, 0:1] + R.biases[l, 3]
    low = hidden.astype(bf16)
    u = dot(low, R.wup[l]) + R.upb[l]
    q = (GELU_A * GELU_B) * (u * u)
    w = 0.5 * jnp.tanh(u * (q + GELU_A)) + 0.5
    a = u * w
    act = a.astype(bf16)
    slope = w + a * ((1.0 - w) * (6.0 * q + 2.0 * GELU_A))
    n2, s2 = norm(hidden + (dot(act, R.wdown[l]) + R.biases[l, 4]))
    R.n1[l] = n1
    R.stat[l, :, 4:5] = s1
    R.gp[l] = slope
    R.act[l] = act
    R.n2[l] = n2
    R.stat[l, :, 5:6] = s2
    R.x[l + 1] = (n2 * R.gains[l, 1:2] + R.biases[l, 5]).astype(bf16)


def norm_back(g, n, s, gain):
    gg = g * gain
    return s * (gg - jnp.mean(gg, axis=-1, keepdims=True) - n * jnp.mean(gg * n, axis=-1, keepdims=True))


def put_small(ref, row, v):
    ref[0, row : row + 1, :] = v[:, 0:128]
    ref[1, row : row + 1, :] = v[:, 128:256]


def feed_back(R, l, g):
    n = R.n
    R.woutT[...] = R.wout[l].T
    R.wupT[...] = R.wup[l].T
    R.wdownT[...] = R.wdown[l].T
    R.wqkvT[...] = R.wqkv[l].T
    small = R.small.at[l]
    n2 = R.n2[l]
    d2 = norm_back(g, n2, R.stat[l, :, 5:6], R.gains[l, 1:2])
    put_small(small, 1, column_sum(g * n2))
    put_small(small, 5, column_sum(g))
    dl = d2.astype(bf16)
    R.dlow[...] = dl
    put_small(small, 4, column_sum(d2))
    du = dot(dl, R.wdownT[...]) * R.gp[l]
    up = column_sum(du)
    put_small(small, 6, up[:, 0:256])
    put_small(small, 7, up[:, 256:512])
    du = du.astype(bf16)
    R.dup[...] = du
    dh = d2 + dot(du, R.wupT[...])
    n1 = R.n1[l]
    low = (n1 * R.gains[l, 0:1] + R.biases[l, 3]).astype(bf16)
    d1 = norm_back(dh, n1, R.stat[l, :, 4:5], R.gains[l, 0:1])
    put_small(small, 0, column_sum(dh * n1))
    put_small(small, 3, column_sum(dh))
    put_small(small, 2, column_sum(d1))
    R.d1[...] = d1
    da = d1.astype(bf16)
    R.datt[...] = da
    dcb = dot(da, R.woutT[...]).astype(bf16)
    R.dctx[...] = dcb
    R.grad_a[l, :, 0:256] = dot_tn(R.octx[l].astype(bf16), R.datt[...])
    R.grad_a[l, :, 256:768] = dot_tn(low, R.dup[...])
    R.grad_a[l, :, 768:1280] = dot_tn(R.dlow[...], R.act[l])


def attend_prepare(R, l):
    n = R.n
    dcb = R.dctx[...]
    dc = dcb.astype(f32)
    e = dc * R.octx[l]
    lane = lanes(n)
    for h in range(HEADS):
        pair = slice(128 * (h // 2), 128 * (h // 2) + 128)
        R.delta[:, h : h + 1] = jnp.sum(
            jnp.where((lane // 64) == (h % 2), e[:, pair], 0.0), axis=1, keepdims=True
        )
        R.doh[h] = jnp.where(lane < 64, head_tile(dc[:, pair], h), 0.0).astype(bf16)
    R.doT[...] = dcb.T
    R.qT[...] = R.qn[l].T
    R.vT[0:256, :] = R.vn[l].T


def add_columns(ref, head, lo, begun, v):
    old = max(0, min(begun - lo, v.shape[1]))
    if old:
        ref[head, pl.ds(lo, old)] += v[:, 0:old]
    if old < v.shape[1]:
        ref[head, pl.ds(lo + old, v.shape[1] - old)] = v[:, old:]


def attend_back_tile(R, l, i):
    lo, width = spans(R.n)[i]
    begun = max([a + b for a, b in spans(R.n)[:i]], default=0)
    rows, cols = pl.ds(i * TILE, TILE), pl.ds(lo, width)
    for h in range(HEADS):
        head, part = slice(64 * h, 64 * h + 64), slice(h * TILE, h * TILE + TILE)
        p = R.P[i][part, :]
        dp = dot(R.doh[h, rows, :], R.vT[64 * h : 64 * h + 128, cols])
        R.DS[part, 0:width] = (p.astype(f32) * (dp - R.delta[rows, h : h + 1])).astype(bf16)
        add_columns(R.dvT, head, lo, begun, dot(R.doT[head, rows], p))
    for h in range(HEADS):
        head, part = slice(64 * h, 64 * h + 64), slice(h * TILE, h * TILE + TILE)
        add_columns(R.dkT, head, lo, begun, dot(R.qT[head, rows], R.DS[part, 0:width]))
    R.dqkv[rows, 0:256] = (pick_heads(dot(R.DS[:, 0:width], R.kn[l, cols, :])) * 0.125).astype(bf16)


def project_back(R, l):
    real = real_rows(R, 0, R.n)
    dv = R.dvT[...].T + jnp.where(real, 0.0, R.dctx[...].astype(f32))
    R.dqkv[:, 256:512] = R.dkT[...].T.astype(bf16)
    R.dqkv[:, 512:768] = dv.astype(bf16)
    put_small(R.small.at[l], 8, column_sum(R.dqkv[:, 0:256].astype(f32)))
    put_small(R.small.at[l], 9, column_sum(dv))
    d = R.d1[...] + dot(R.dqkv[...], R.wqkvT[...])
    R.d1[...] = d
    R.dinb[l] = d.astype(bf16)


def weight_back(R, l):
    R.grad_b[l] = dot_tn(R.x[l], R.dqkv[...])


class Links:
    def __init__(self, dp, send, recv, local):
        self.sec = lax.axis_index("section")
        self.dp = lax.axis_index("dp")
        self.send, self.recv, self.local_sem = send, recv, local
        self.used = 0
        self.used_local = 0
        self.core = self.dp % 2
        self.chips = min(8, dp // 2)
        self.groups = dp // (2 * self.chips)
        self.chip = (self.dp // 2) % self.chips
        self.pending = []

    def flip(self, index, bit):
        return index + bit - 2 * bit * ((index // bit) % 2)

    def xor(self, index, mask):
        bit = 1
        while bit <= mask:
            if mask & bit:
                index = self.flip(index, bit)
            bit *= 2
        return index

    def section_peer(self):
        return (1 - self.sec, self.dp)

    def core_peer(self):
        return (self.sec, self.flip(self.dp, 1))

    def chip_peer(self, k):
        return (self.sec, self.xor(self.dp, 2 * k))

    def group_peer(self, k):
        return (self.sec, self.xor(self.dp, 2 * self.chips * k))

    def peers(self):
        out = [self.section_peer(), self.core_peer()]
        out += [self.chip_peer(k) for k in range(1, self.chips)]
        out += [self.group_peer(k) for k in range(1, self.groups)]
        return out

    def remote(self, src, dst, peer):
        i = self.used
        self.used += 1
        return pltpu.make_async_remote_copy(
            src, dst, self.send.at[i], self.recv.at[i], device_id=peer, device_id_type=MESH
        )

    def local(self, src, dst):
        i = self.used_local
        self.used_local += 1
        return pltpu.make_async_copy(src, dst, self.local_sem.at[i])


def reduction(K, l, grad, small, R, name, sum_two, give_two):
    get = lambda part: getattr(R, name + "_" + part).at[l]
    r1, s2, ry, r2, acc, r3 = [get(p) for p in ("r1", "s2", "ry", "r2", "acc", "r3")]
    res, out = getattr(R, name + "_res"), getattr(R, "res_" + name)
    c, chip, chips, groups = K.core, K.chip, K.chips, K.groups
    half = grad.shape[0] // 2
    piece = half // chips
    near = half // 2
    line = chips // 2

    def place_of(index):
        return (index % 2) * near + (index // 2) * piece

    start = c * half
    mine, other = pl.ds(start, half), pl.ds((1 - c) * half, half)
    my_near, other_near = (chip % 2) * near, (1 - chip % 2) * near
    part = pl.ds(place_of(chip), piece)
    owner = K.sec == l
    has_small = small is not None
    core_out = [K.remote(grad.at[other], r1, K.core_peer())]
    everyone = range(1, chips)
    ahead = range(2, chips, 2)
    to_near = [K.remote(s2.at[pl.ds(other_near, near)], ry, K.chip_peer(1))] if sum_two else []
    targets = ahead if sum_two else everyone
    scatter = [
        K.remote(s2.at[pl.ds(place_of(K.xor(chip, k)), piece)], r2.at[k], K.chip_peer(k)) for k in targets
    ]
    across = [K.remote(acc, r3, K.section_peer())]
    spread = []
    if groups > 1:
        r4 = get("r4")
        spread = [K.remote(acc, r4.at[k], K.group_peer(k)) for k in range(1, groups)]
    gather = [
        K.remote(res.at[part], res.at[part], K.chip_peer(k)) for k in (ahead if give_two else everyone)
    ]
    rows = pl.ds(my_near, near)
    from_near = [K.remote(res.at[rows], res.at[rows], K.chip_peer(1))] if give_two else []
    core_back = [K.remote(res, out.at[mine], K.core_peer())]
    keep = [K.local(res, out.at[mine])]
    if has_small:
        q1, q2, ty, t2, qacc, q3, qres = [get(p) for p in ("q1", "q2", "ty", "t2", "qacc", "q3", "qres")]
        core_out.append(K.remote(small.at[1 - c], q1, K.core_peer()))
        if sum_two:
            to_near.append(K.remote(q2, ty, K.chip_peer(1)))
        little_src = qacc if sum_two else q2
        scatter += [K.remote(little_src, t2.at[k], K.chip_peer(k)) for k in targets]
        across.append(K.remote(q2, q3, K.section_peer()))
        core_back.append(K.remote(qres, R.small_out.at[c], K.core_peer()))
        keep.append(K.local(qres, R.small_out.at[c]))
        if groups > 1:
            q4 = get("q4")
            spread += [K.remote(qacc, q4.at[k], K.group_peer(k)) for k in range(1, groups)]

    def each(copies, *what):
        for w in what:
            for x in copies:
                getattr(x, w)()

    def begin():
        each(core_out, "start")

    def to_neighbour():
        each(core_out, "wait_recv")
        total = grad[mine, :] + r1[...]
        grad[mine, :] = total
        s2[...] = total.astype(bf16)
        if has_small:
            q2[...] = small[c] + q1[...]
        each(to_near if sum_two else scatter, "start")

    def to_line():
        if sum_two:
            each(to_near, "wait")
            own = pl.ds(start + my_near, near)
            total = grad[own, :] + ry[...].astype(f32)
            grad[own, :] = total
            s2[pl.ds(my_near, near), :] = total.astype(bf16)
            if has_small:
                qacc[...] = q2[...] + ty[...]
            each(scatter, "start")

    def sum_pieces():
        each(scatter[: len(targets)], "wait_recv")
        total = grad[pl.ds(start + place_of(chip), piece), :]
        for k in targets:
            total = total + r2[k].astype(f32)
        acc[...] = total
        pl.when(jnp.logical_not(owner))(across[0].start)
        if has_small:
            each(scatter[len(targets) :], "wait")
            little = little_src[...]
            for k in targets:
                little = little + t2[k]
            q2[...] = little
            pl.when(jnp.logical_not(owner))(across[1].start)

    def give_line():
        @pl.when(owner)
        def _():
            across[0].wait_recv()
            acc[...] += r3[...]
            if groups > 1:
                if has_small:
                    across[1].wait_recv()
                    qacc[...] = q2[...] + q3[...]
                each(spread, "start", "wait")
            total = acc[...]
            for k in range(1, groups):
                total = total + r4[k]
            res[part, :] = total.astype(bf16)
            each(gather, "start")
            if has_small and groups > 1:
                little = qacc[...]
                for k in range(1, groups):
                    little = little + q4[k]
                qres[...] = little
            elif has_small:
                across[1].wait_recv()
                qres[...] = q2[...] + q3[...]

    def give_neighbour():
        if give_two:

            @pl.when(owner)
            def _():
                each(gather, "wait_recv")
                each(from_near, "start")

    def share():
        @pl.when(owner)
        def _():
            each(from_near if give_two else gather, "wait_recv")
            each(core_back, "start")
            each(keep, "start")

    def finish():
        @pl.when(owner)
        def _():
            each(core_back, "wait")
            each(keep, "wait")
            each(gather + from_near, "wait_send")

        each(core_out + scatter[: len(targets)], "wait_send")

        pl.when(jnp.logical_not(owner))(lambda: each(across, "wait_send"))

    return begin, to_neighbour, to_line, sum_pieces, give_line, give_neighbour, share, finish


TWO = ((False, False), (True, True), (False, False), (False, True))


def scratch(n, chips, groups):
    def V(*s):
        return pltpu.VMEM(s[:-1], s[-1])

    out = dict(
        wqkv=V(2, 256, 768, bf16), wout=V(2, 256, 256, bf16), wup=V(2, 256, 512, bf16), wdown=V(2, 512, 256, bf16),
        gains=V(2, 2, 256, f32), biases=V(2, 6, 1, 256, f32), upb=V(2, 1, 512, f32),
        x=V(3, n, 256, bf16), qn=V(2, n, 256, bf16), kn=V(2, n, 256, bf16), vn=V(2, n, 256, bf16),
        octx=V(2, n, 256, f32), DS=V(HEADS * TILE, n, bf16),
        n1=V(2, n, 256, f32), n2=V(2, n, 256, f32), stat=V(2, n, 128, f32),
        gp=V(2, n, 512, f32), act=V(2, n, 512, bf16),
        qcode=V(n, 128, bf16), qh=V(HEADS, n, 128, bf16), kc=V(512, n, bf16), vT=V(320, n, bf16),
        doh=V(HEADS, n, 128, bf16), doT=V(256, n, bf16), qT=V(256, n, bf16), delta=V(n, 128, f32), dctx=V(n, 256, bf16),
        dkT=V(256, n, f32), dvT=V(256, n, f32), dqkv=V(n, 768, bf16),
        d1=V(n, 256, f32),
        woutT=V(256, 256, bf16), wupT=V(512, 256, bf16), wdownT=V(256, 512, bf16), wqkvT=V(768, 256, bf16),
        dinb=V(2, n, 256, bf16),
        small=V(2, 2, 16, 128, f32),
    )
    for name, width in (("a", 1280), ("b", 768)):
        piece = 128 // chips
        out["grad_" + name] = V(2, 256, width, f32)
        out[name + "_r1"] = V(2, 128, width, f32)
        out[name + "_s2"] = V(2, 128, width, bf16)
        out[name + "_r2"] = V(2, chips, piece, width, bf16)
        out[name + "_acc"] = V(2, piece, width, f32)
        out[name + "_r3"] = V(2, piece, width, f32)
        out[name + "_ry"] = V(2, 64, width, bf16)
        out[name + "_res"] = V(128, width, bf16)
        if groups > 1:
            out[name + "_r4"] = V(2, groups, piece, width, f32)
    for part, lead in (("q1", ()), ("q2", ()), ("ty", ()), ("t2", (chips,)), ("qacc", ()), ("q3", ()), ("qres", ()), ("q4", (groups,))):
        out["b_" + part] = V(2, *lead, 16, 128, f32)
    for i, (_, width) in enumerate(spans(n)):
        out["P%d" % i] = V(HEADS * TILE, width, bf16)
    copies = 32 + 4 * (8 + 3 * chips + 2 * groups)
    out["send"] = pltpu.SemaphoreType.DMA((copies,))
    out["recv"] = pltpu.SemaphoreType.DMA((copies,))
    out["local"] = pltpu.SemaphoreType.DMA((64,))
    return out


INS = ["len_s", "seg_v", "cells", "ograd", "i_wqkv", "i_wout", "i_wup", "i_wdown", "i_gains", "i_biases", "i_upb"]
OUTS = ["layer_out", "din_own", "rdin", "res_a", "res_b", "small_out"]
WEIGHTS = ["wqkv", "wout", "wup", "wdown", "gains", "biases", "upb"]


def body(R, n, dp):
    K = Links(dp, R.send, R.recv, R.local)
    sec, c = K.sec, K.core
    R.n = n
    R.P = [getattr(R, "P%d" % i) for i in range(n // TILE)]
    R.dup = R.DS.at[:, pl.ds(0, 512)]
    R.dlow = R.DS.at[:, pl.ds(512, 256)]
    R.datt = R.DS.at[:, pl.ds(768, 256)]
    R.length = R.len_s[sec]
    R.seg_row = R.seg_v[pl.ds(sec, 1), :]

    barrier = pltpu.get_barrier_semaphore()
    peers = K.peers()[::-1]
    for peer in peers:
        pl.semaphore_signal(barrier, 1, device_id=peer, device_id_type=MESH)

    take_x = K.local(R.cells.at[sec], R.x.at[0])
    take_g = K.local(R.ograd.at[sec], R.dinb.at[0])
    given = {w: getattr(R, "i_" + w) if w == "biases" else getattr(R, "i_" + w).at[0] for w in WEIGHTS}
    own = [K.local(given[w], getattr(R, w).at[sec]) for w in WEIGHTS]
    take_x.start()
    for x in own:
        x.start()
    take_g.start()

    away, forward_on = {}, {}
    for w in WEIGHTS:
        src, slots = given[w], getattr(R, w)
        if w in ("gains", "biases", "upb"):
            away[w] = K.remote(src, slots.at[sec], K.section_peer())
        else:
            half = src.shape[0] // 2
            rows = pl.ds(c * half, half)
            away[w] = K.remote(src.at[rows], slots.at[sec, rows], K.section_peer())
            theirs = slots.at[1 - sec, rows]
            forward_on[w] = K.remote(theirs, theirs, K.core_peer())

    setup(R)
    pl.semaphore_wait(barrier, len(peers))
    first = ("biases", "wqkv")
    second = ("gains", "upb", "wout", "wup", "wdown")
    for w in first + second:
        away[w].start()
    take_x.wait()
    for x in own:
        x.wait()

    def take_first():
        for w in first:
            away[w].wait()
        forward_on["wqkv"].start()

    @pl.when(sec == 1)
    def _():
        take_first()
        forward_on["wqkv"].wait()

    n_tiles = n // TILE
    x_out = [
        (K.local(R.x.at[l + 1], R.layer_out.at[sec]), K.remote(R.x.at[l + 1], R.layer_out.at[sec], K.section_peer()))
        for l in range(2)
    ]

    def start_out(l, pair):
        pl.when(sec == l)(pair[0].start)
        pl.when(sec != l)(pair[1].start)

    stash = [getattr(R, "stash%d" % i) for i in range(n_tiles)]
    put_away = [K.local(R.P[i], stash[i]) for i in range(n_tiles)]
    bring_back = [K.local(stash[i], R.P[i]) for i in range(n_tiles)]

    def starts(copies):
        for x in copies:
            x.start()

    def waits(copies):
        for x in copies:
            x.wait()

    def forward(l, _):
        def at(layer, *steps):
            @pl.when(l == layer)
            def _():
                for step in steps:
                    step()

        project(R, l)
        at(1, lambda: waits(put_away))
        for i in range(n_tiles):
            attend_tile(R, l, i)
            if i == n_tiles - 2:
                at(
                    0,
                    lambda: starts(put_away[: n_tiles - 1]),
                    lambda: pl.when(sec == 0)(take_first),
                    lambda: waits([away[w] for w in second]),
                    lambda: starts([forward_on[w] for w in ("wout", "wup", "wdown")]),
                )
        at(0, lambda: starts(put_away[n_tiles - 1 :]), lambda: waits([forward_on[w] for w in ("wout", "wup", "wdown")]),
            lambda: pl.when(sec == 0)(forward_on["wqkv"].wait))
        feed(R, l)
        at(0, lambda: start_out(0, x_out[0]))
        at(1, lambda: start_out(1, x_out[1]))
        return 0

    lax.fori_loop(0, 2, forward, 0)

    R.small[...] = jnp.zeros_like(R.small)
    A = [reduction(K, l, R.grad_a.at[l], None, R, "a", TWO[0][l], TWO[1][l]) for l in range(2)]
    B = [reduction(K, l, R.grad_b.at[l], R.small.at[l], R, "b", TWO[2][l], TWO[3][l]) for l in range(2)]
    BEGIN, NEAR, LINE, SUM, GIVE, GIVE_NEAR, SHARE, FINISH = range(8)

    din_local = [K.local(R.d1, R.din_own) for l in range(2)]
    quarter = n // 4
    din_away = [
        K.remote(R.dinb.at[1], R.rdin, K.section_peer()),
        [K.remote(R.dinb.at[0, pl.ds(i * quarter, quarter)], R.rdin.at[pl.ds(i * quarter, quarter)], K.section_peer()) for i in range(4)],
    ]
    take_g.wait()

    def start_din(l, part=slice(None)):
        @pl.when(sec == l)
        def _():
            din_local[l].start()

        @pl.when(sec != l)
        def _():
            starts([din_away[0]] if l == 1 else din_away[1][:2])

    def backward(j, _):
        l = 1 - j

        def at(turn, *steps):
            @pl.when(j == turn)
            def _():
                for step in steps:
                    step()

        at(1, lambda: pl.when(sec == 1)(din_local[1].wait))
        feed_back(R, l, R.dinb[j].astype(f32))
        at(0, A[1][BEGIN])
        at(1, A[0][BEGIN], A[1][LINE], B[1][NEAR], lambda: waits(bring_back))
        attend_prepare(R, l)
        for i in range(n_tiles):
            attend_back_tile(R, l, i)
            if i == 1:
                at(0, A[1][NEAR], lambda: starts(bring_back[:2]))
                at(1, A[0][NEAR])
            if i == 2:
                at(1, B[1][LINE])
        at(0, lambda: starts(bring_back[2:]))
        project_back(R, l)
        at(0, lambda: start_din(1))
        at(1, lambda: start_din(0))
        weight_back(R, l)
        at(0, B[1][BEGIN])
        at(1, B[0][BEGIN])
        return 0

    lax.fori_loop(0, 2, backward, 0)

    A[0][LINE]()
    B[0][NEAR]()
    A[0][SUM]()
    A[1][SUM]()
    B[1][SUM]()
    B[0][LINE]()
    A[0][GIVE]()
    B[0][SUM]()
    pl.when(sec == 1)(lambda: starts(din_away[1][2:]))
    A[1][GIVE]()
    B[1][GIVE]()
    B[0][GIVE]()
    A[0][GIVE_NEAR]()
    A[1][GIVE_NEAR]()
    B[1][GIVE_NEAR]()
    B[0][GIVE_NEAR]()
    A[0][SHARE]()
    A[1][SHARE]()
    B[1][SHARE]()
    B[0][SHARE]()
    A[1][FINISH]()
    B[1][FINISH]()
    A[0][FINISH]()
    B[0][FINISH]()

    for l in range(2):

        @pl.when(sec == l)
        def _():
            x_out[l][0].wait()
            x_out[1 - l][1].wait_send()
            x_out[l][1].wait_recv()
            if l == 0:
                din_local[0].wait()
                din_away[0].wait_send()
                for x in din_away[1]:
                    x.wait_recv()
            else:
                for x in din_away[1]:
                    x.wait_send()
                din_away[0].wait_recv()


def place(n, *refs):
    names = OUTS + ["layer", "grad", "gqkv", "gout", "gup", "gdown", "ggains", "gbias", "gupb", "d", "a", "b", "df", "af", "bf", "tf", "small", "lay", "sem"]
    R = types.SimpleNamespace(**dict(zip(names, refs)))
    sec = lax.axis_index("section")
    used = iter(range(16))
    copy = lambda src, dst: pltpu.make_async_copy(src, dst, R.sem.at[next(used)])
    lay, own, far, low_a, low_b, low = [
        copy(R.layer_out, R.lay), copy(R.din_own, R.df.at[sec]), copy(R.rdin, R.d),
        copy(R.res_a, R.a), copy(R.res_b, R.b), copy(R.small_out, R.small),
    ]
    for x in (lay, own, far, low_a, low_b, low):
        x.start()
    out = [
        copy(R.lay, R.layer.at[0]), copy(R.df.at[sec], R.grad.at[0, sec]), copy(R.df.at[1 - sec], R.grad.at[0, 1 - sec]),
        copy(R.af.at[:, pl.ds(0, 256)], R.gout.at[0]), copy(R.af.at[:, pl.ds(256, 512)], R.gup.at[0]),
        copy(R.tf, R.gdown.at[0]), copy(R.bf, R.gqkv.at[0]),
    ]
    lay.wait()
    out[0].start()
    own.wait()
    out[1].start()
    far.wait()
    R.df[1 - sec] = R.d[...].astype(f32)
    out[2].start()
    low_a.wait()
    R.af[...] = R.a[:, 0:768].astype(f32)
    out[3].start()
    out[4].start()
    R.tf[...] = R.a[:, 768:1280].astype(f32).T
    out[5].start()
    low_b.wait()
    R.bf[...] = R.b[...].astype(f32)
    out[6].start()
    low.wait()

    def row(small, i):
        return jnp.concatenate([small[0, i : i + 1, :], small[1, i : i + 1, :]], axis=1)

    for i in range(2):
        R.ggains[0, i : i + 1, :] = row(R.small, i)
        R.gupb[0, :, 256 * i : 256 * i + 256] = row(R.small, 6 + i)
        R.gbias[i] = row(R.small, 8 + i)
    for i in range(2, 6):
        R.gbias[i] = row(R.small, i)
    for x in out:
        x.wait()


def kernel_call(dp, n, lengths, segments, cells, ograd, *weights):
    chips = min(8, dp // 2)
    groups = dp // (2 * chips)
    sc = scratch(n, chips, groups)

    def kern(*refs):
        body(types.SimpleNamespace(**dict(zip(names, refs))), n, dp)

    stash = [(HEADS * TILE, width) for _, width in spans(n)]
    names = INS + OUTS + ["stash%d" % i for i in range(len(stash))] + list(sc)
    vmem, smem, anywhere = [pl.BlockSpec(memory_space=m) for m in (pltpu.VMEM, pltpu.SMEM, pl.ANY)]
    shapes = [((2, n, 256), bf16), ((n, 256), f32), ((n, 256), bf16), ((256, 1280), bf16), ((256, 768), bf16)]
    shapes += [((2, 16, 128), f32)] + [(s, bf16) for s in stash]
    parts = pl.pallas_call(
        kern,
        out_shape=[jax.ShapeDtypeStruct(*s) for s in shapes],
        in_specs=[smem, vmem] + [anywhere] * 9,
        out_specs=[anywhere] * (len(OUTS) + len(stash)),
        scratch_shapes=list(sc.values()),
        compiler_params=pltpu.CompilerParams(
            vmem_limit_bytes=62 * 2**20, collective_id=0, has_side_effects=True
        ),
    )(lengths, segments, cells, ograd, *weights)[: len(OUTS)]
    shapes = [((1, 2, n, 256), bf16), ((1, 2, n, 256), f32), ((1, 256, 768), f32), ((1, 256, 256), f32),
              ((1, 256, 512), f32), ((1, 512, 256), f32), ((1, 2, 256), f32), ((6, 1, 256), f32), ((1, 1, 512), f32)]
    return pl.pallas_call(
        lambda *refs: place(n, *refs),
        out_shape=[jax.ShapeDtypeStruct(*s) for s in shapes],
        in_specs=[anywhere] * len(OUTS),
        out_specs=[anywhere] * 6 + [vmem] * 3,
        scratch_shapes=[
            pltpu.VMEM((n, 256), bf16), pltpu.VMEM((256, 1280), bf16), pltpu.VMEM((256, 768), bf16),
            pltpu.VMEM((2, n, 256), f32), pltpu.VMEM((256, 768), f32), pltpu.VMEM((256, 768), f32), pltpu.VMEM((512, 256), f32),
            pltpu.VMEM((2, 16, 128), f32), pltpu.VMEM((2, n, 256), bf16),
            pltpu.SemaphoreType.DMA((16,)),
        ],
        compiler_params=pltpu.CompilerParams(vmem_limit_bytes=62 * 2**20),
    )(*parts)


def solution(mesh):
    dp = mesh.shape["dp"]

    def on_device(cells, ograd, segments, lengths, *weights):
        *matrices, biases, up = weights
        weights = (*matrices, biases.transpose(1, 0, 2), up[:, None, :])
        out = kernel_call(dp, cells.shape[1], lengths, segments, cells, ograd, *weights)
        return (*out[:7], out[7].transpose(1, 0, 2), out[8][:, 0, :])

    w3, w2 = P("section", None, None), P("section", None)
    rows = P("section", "dp", None, None)
    return jax.shard_map(
        on_device,
        mesh=mesh,
        in_specs=(P("dp", None, None), P("dp", None, None), P("dp", None), P("dp"), w3, w3, w3, w3, w3, w3, w2),
        out_specs=(rows, rows, w3, w3, w3, w3, w3, w3, w2),
        check_vma=False,
    )
```
